32 devices in a mesh: cluster: 16 (over z, y, x), mp: 2 (over core).
Axes of the slice: x: 2, y: 2, z: 4, core: 2. Of those that a mesh axis runs over, the one named last changes fastest.
Arguments:
- features: bfloat16 [8192, 2048], P('cluster', 'mp'), may hold values from -6 to 6
- neighbour_ids: int32 [8192, 16], P('cluster'), may hold values from 0 to 639
- edge_weight: float32 [8192, 16], P('cluster'), may hold values from 0.02 to 0.12
- self_weight: float32 [8192], P('cluster'), may hold values from 0.05 to 0.5
- send_rows: int32 [16, 16, 8], P('cluster'), may hold values from 0 to 511
- valid_mask: int32 [8192], P('cluster'), may hold values 0 or 1
- weights: bfloat16 [2, 2048, 2048], P(None, None, 'mp'), may hold values from -0.25 to 0.25
- biases: float32 [2, 2048], P(None, 'mp'), may hold values from -3 to 3
- norm_gain: float32 [2, 2048], P(None, 'mp'), may hold values from 0.5 to 1.5
- norm_shift: float32 [2, 2048], P(None, 'mp'), may hold values from -3 to 3
- output_grad: bfloat16 [8192, 2048], P('cluster', 'mp'), may hold values from -6 to 6
Outputs:
- output: bfloat16 [8192, 2048], P('cluster', 'mp')
- input_grad: bfloat16 [8192, 2048], P('cluster', 'mp')
- weight_grad: float32 [2, 2048, 2048], P(None, None, 'mp')
- bias_grad: float32 [2, 2048], P(None, 'mp')
- gain_grad: float32 [2, 2048], P(None, 'mp')
- shift_grad: float32 [2, 2048], P(None, 'mp')
The draws below stay inside these ranges and needn't reach their ends.
Inputs may be any that keep to these rules, and one draw needn't show every extreme that they name: `neighbour_ids`: entry j below 512 names row j of the same cluster's nodes; j = 512 + s * 8 + q names the row send_rows[s, c, q] of cluster s, where c is the node's own cluster. send_rows[s, d, q] is a row of cluster s's own nodes, sent to cluster d in place q.
All inputs are finite; a program needn't handle non-finite values. No bound on the sum of `valid_mask` on one device may be relied on, other than what follows from the above.
Results may differ from the reference program's by a relative error of at most 0.023.
Values may be sent and summed in bfloat16 or wider, within the bound.
A program may use at most 128 MiB of HBM per device.

```python
import math
import jax
import jax.numpy as jnp
from jax import lax

D = 2048
NODES_DEV = 512
CAP = 8
K = 16
LAYERS = 2
NODES = 8192
N_CLUSTER = 16


def place_ends(result, key, smallest, high):
    longest = result.shape.index(max(result.shape))
    spots = []
    for shift in (0, 1):
        where = [jax.random.randint(jax.random.fold_in(key, axis), (), 0, length) for axis, length in enumerate(result.shape)]
        where[longest] = (where[longest] + shift) % result.shape[longest]
        spots.append(tuple(where))
    return result.at[spots[0]].set(smallest).at[spots[1]].set(high)


def block_scale(key, shape, split, low, largest):
    level, own = 1.0, jax.random.fold_in(key, 6)
    for dim, shards_of in split:
        draws = jnp.exp(jax.random.uniform(jax.random.fold_in(own, dim), (shards_of,), jnp.float32, low / len(split), largest / len(split)))
        level = level * jnp.repeat(draws, shape[dim] // shards_of).reshape([-1 if axis == dim else 1 for axis in range(len(shape))])
    return level


def noise(own_key, shape, deviation, limit, pieces=(), held_as=jnp.bfloat16):
    drawn = jax.random.normal(own_key, shape, jnp.float32) * deviation
    if len(pieces) > 0:
        drawn = block_scale(own_key, shape, pieces, -0.22, 0.18) * drawn
    return jnp.clip(drawn, min=-limit, max=limit).astype(held_as)


def setup_inputs(seed: int = 0) -> dict:
    splits = jax.random.split(jax.random.key(seed), 12)
    features = noise(splits[0], (NODES, D), 1.0, 6.0, ((0, 16), (1, 2)))
    neighbour_ids = place_ends(jax.random.randint(splits[1], (NODES, K), 0, NODES_DEV + N_CLUSTER * CAP), jax.random.fold_in(splits[1], 1), 0, (NODES_DEV + N_CLUSTER * CAP) - 1).astype(jnp.int32)
    edge_weight = jnp.clip(jnp.exp(math.log(0.12) - 1.7917595 * jax.random.uniform(splits[2], (NODES, K), jnp.float32) ** block_scale(splits[2], (NODES, K), ((0, 16),), -0.2, 0.2)), 0.02, 0.12)
    self_weight = jnp.clip(jnp.exp(math.log(0.5) - 2.3025851 * jax.random.uniform(splits[3], (NODES,), jnp.float32) ** block_scale(splits[3], (NODES,), ((0, 16),), -0.2, 0.2)), 0.05, 0.5)
    send_rows = place_ends(jax.random.randint(splits[4], (N_CLUSTER, N_CLUSTER, CAP), 0, NODES_DEV), jax.random.fold_in(splits[4], 1), 0, NODES_DEV - 1).astype(jnp.int32)
    valid_mask = place_ends((jax.random.randint(splits[5], (NODES,), 0, 8) < 7).astype(jnp.int32), jax.random.fold_in(splits[5], 1), 0, 1)
    weights = noise(splits[6], (LAYERS, D, D), (D // 4) ** -0.5, 0.25, ((2, 2),))
    biases = noise(splits[7], (LAYERS, D), 0.5, 3.0, ((1, 2),), jnp.float32)
    norm_gain = jnp.clip(1.0 + 0.1 * jax.random.normal(splits[8], (LAYERS, D), jnp.float32), 0.5, 1.5)
    norm_shift = noise(splits[9], (LAYERS, D), 0.5, 3.0, ((1, 2),), jnp.float32)
    output_grad = noise(splits[10], (NODES, D), 1.0, 6.0, ((0, 16), (1, 2)))
    return {"features": features, "neighbour_ids": neighbour_ids, "edge_weight": edge_weight, "self_weight": self_weight, "send_rows": send_rows, "valid_mask": valid_mask, "weights": weights, "biases": biases, "norm_gain": norm_gain, "norm_shift": norm_shift, "output_grad": output_grad}


EPS = 1e-05
LAMBDA = 1.0
HIGHEST_PREC = lax.Precision.HIGHEST

@jax.custom_vjp
def low(v):
    return lax.optimization_barrier(v.astype(jnp.bfloat16)).astype(jnp.float32)

@jax.custom_vjp
def low_back(v):
    return v

def low_keep(v):
    return (low(v), None)

def low_pass(kept, grad):
    return (grad,)

def back_keep(v):
    return (v, None)

def back_low(kept, grad):
    return (low(grad),)
low.defvjp(low_keep, low_pass)
low_back.defvjp(back_keep, back_low)

def global_index(neighbour_ids, send_rows):
    local_ids = neighbour_ids.reshape(N_CLUSTER, NODES_DEV, K)
    owner_ids = jnp.broadcast_to(jnp.arange(N_CLUSTER, dtype=jnp.int32)[:, None, None], local_ids.shape)
    halo_slot = jnp.maximum(local_ids - NODES_DEV, 0)
    source_ids = (halo_slot // CAP).astype(jnp.int32)
    slot_pos = (halo_slot % CAP).astype(jnp.int32)
    remote_rows = send_rows[source_ids, owner_ids, slot_pos]
    joined = jnp.where(local_ids < NODES_DEV, owner_ids * NODES_DEV + local_ids, source_ids * NODES_DEV + remote_rows)
    return joined.astype(jnp.int32)

def aggregate(hidden, joined, edge_weight, self_weight):

    def one_cluster(blocks):
        index_block, weight_block = blocks
        return lax.optimization_barrier(jnp.sum(weight_block[:, :, None] * hidden[index_block], axis=1))
    spread = lax.map(jax.checkpoint(one_cluster), (joined.reshape(N_CLUSTER, NODES_DEV, K), edge_weight.reshape(N_CLUSTER, NODES_DEV, K)))
    return spread.reshape(hidden.shape) + (1.0 + LAMBDA) * self_weight[:, None] * hidden

def one_layer(hidden, weight, bias, gain, shift, joined, edge_weight, self_weight, node_mask, valid_count):
    mixed_rows = low(aggregate(hidden, joined, edge_weight, self_weight))
    pre_act = low_back(jnp.dot(mixed_rows, weight, precision=HIGHEST_PREC) + bias)
    activation = jax.nn.silu(pre_act)
    column_mean = lax.optimization_barrier(jnp.sum(activation * node_mask, axis=0)) / valid_count
    centered = activation - column_mean
    variance = lax.optimization_barrier(jnp.sum(centered * centered * node_mask, axis=0)) / valid_count
    return node_mask * (gain * centered * lax.rsqrt(variance + EPS) + shift)

def reference(features, neighbour_ids, edge_weight, self_weight, send_rows, valid_mask, weights, biases, norm_gain, norm_shift, output_grad):
    joined = global_index(neighbour_ids, send_rows)
    node_mask = valid_mask.astype(jnp.float32)[:, None]
    valid_count = jnp.maximum(jnp.sum(valid_mask.astype(jnp.float32)), 1.0)

    def forward(hidden, weight_all, bias_all, gain_all, shift_all):
        first = low(one_layer(hidden, weight_all[0], bias_all[0], gain_all[0], shift_all[0], joined, edge_weight, self_weight, node_mask, valid_count))
        return one_layer(first, weight_all[1], bias_all[1], gain_all[1], shift_all[1], joined, edge_weight, self_weight, node_mask, valid_count)
    output, pullback = jax.vjp(forward, features.astype(jnp.float32), weights.astype(jnp.float32), biases, norm_gain, norm_shift)
    input_grad, weight_grads, bias_grads, gain_grads, shift_grads = pullback(output_grad.astype(jnp.float32))
    return (output.astype(jnp.bfloat16), input_grad.astype(jnp.bfloat16), weight_grads, bias_grads, gain_grads, shift_grads)
```

```python
import functools

import jax
import jax.numpy as jnp
from jax import lax
from jax.experimental import pallas as pl
from jax.experimental.pallas import tpu as pltpu
from jax.sharding import PartitionSpec as P

EPS = 1e-05
MESH = pl.DeviceIdType.MESH
BF = jnp.bfloat16
F32 = jnp.float32


def mm(a, b):
    return jnp.dot(a, b, preferred_element_type=F32)


def mm_t(a, b):
    return lax.dot_general(a, b, (((1,), (1,)), ((), ())), preferred_element_type=F32)


def chain(
    n, cap, fan,
    f_ref, aux_ref, rows_ref, par_ref, og_hbm, w_hbm,
    out_hbm, ig_hbm, y_hbm, dz_hbm, small_ref,
    w_ref, og_ref, adj, adj_t, sel, sel_t, h1_ref, out_ref, yf, s_ref, d_ref, zacc,
    dz_ref, dy_own, dy_send, dy_recv, dyb, g_ref, hsend, hrecv, st_row, stat0, stat1, stat2, stat3,
    w_sem, og_sem, out_sem, mp_ssem, mp_rsem, h_ssem, h_rsem, x_ssem, x_rsem,
):
    nodes, cols = f_ref.shape
    ct = 256
    tiles = cols // ct
    half = cols // 2
    c = lax.axis_index("cluster")
    m = lax.axis_index("mp")
    peer = (c, 1 - m)
    halo = n * cap
    lookup = nodes + halo

    barrier = pltpu.get_barrier_semaphore()

    def greet(i, _):
        pl.semaphore_signal(
            barrier, inc=1, device_id=(lax.rem(c + i, n), m), device_id_type=MESH
        )
        return 0

    lax.fori_loop(1, n, greet, 0)
    pl.semaphore_signal(barrier, inc=1, device_id=peer, device_id_type=MESH)

    w_copies = [
        pltpu.make_async_copy(w_hbm.at[layer], w_ref.at[layer], w_sem.at[layer])
        for layer in range(2)
    ]
    w_copies[0].start()
    og_copy = pltpu.make_async_copy(og_hbm, og_ref, og_sem)
    og_copy.start()
    w_copies[1].start()

    sel_f = jnp.where(
        rows_ref[...] == lax.broadcasted_iota(jnp.int32, (halo, nodes), 1), 1.0, 0.0
    )
    sel[...] = sel_f.astype(BF)

    def col(j):
        return pl.ds(pl.multiple_of(j * ct, ct), ct)

    def pack_halo(left, right):
        both = jnp.concatenate(
            [left.reshape(n, cap, half), right.reshape(n, cap, half)], axis=1
        )
        hsend[...] = both.reshape(n * 2 * cap, half).astype(BF)

    def halo_part(d):
        return pl.ds(pl.multiple_of(d * 2 * cap, 2 * cap), 2 * cap)

    def halo_start():
        def send(i, _):
            d = lax.rem(c + i, n)
            pltpu.make_async_remote_copy(
                src_ref=hsend.at[halo_part(d)],
                dst_ref=hrecv.at[halo_part(c)],
                send_sem=h_ssem.at[d],
                recv_sem=h_rsem.at[c],
                device_id=(d, m),
                device_id_type=MESH,
            ).start()
            return 0

        lax.fori_loop(1, n, send, 0)
        hrecv[halo_part(c)] = hsend[halo_part(c)]

    def halo_finish():
        def finish(i, _):
            s = lax.rem(c + i, n)
            copy = pltpu.make_async_remote_copy(
                src_ref=hsend.at[halo_part(s)],
                dst_ref=hrecv.at[halo_part(s)],
                send_sem=h_ssem.at[s],
                recv_sem=h_rsem.at[s],
                device_id=(s, m),
                device_id_type=MESH,
            )
            copy.wait_recv()
            copy.wait_send()
            return 0

        lax.fori_loop(1, n, finish, 0)

    def halo_read():
        got = hrecv[...].astype(F32).reshape(n, 2 * cap, half)
        left = got[:, :cap, :].reshape(halo, half).astype(BF)
        right = got[:, cap:, :].reshape(halo, half).astype(BF)
        return left, right

    def stat_start(e, buf):
        def send(i, _):
            d = lax.rem(c + i, n)
            pltpu.make_async_remote_copy(
                src_ref=buf.at[c],
                dst_ref=buf.at[c],
                send_sem=x_ssem.at[e, d],
                recv_sem=x_rsem.at[e, c],
                device_id=(d, m),
                device_id_type=MESH,
            ).start()
            return 0

        lax.fori_loop(1, n, send, 0)

    def stat_finish(e, buf):
        def finish(i, _):
            s = lax.rem(c + i, n)
            copy = pltpu.make_async_remote_copy(
                src_ref=buf.at[c],
                dst_ref=buf.at[s],
                send_sem=x_ssem.at[e, s],
                recv_sem=x_rsem.at[e, s],
                device_id=(s, m),
                device_id_type=MESH,
            )
            copy.wait_recv()
            copy.wait_send()
            return 0

        lax.fori_loop(1, n, finish, 0)

    lanes = cols // 8

    def fold(buf, k, row):
        for g in range(8):
            buf[c, k, g : g + 1, :] = st_row[row : row + 1, g * lanes : (g + 1) * lanes]

    def unfold(tile, row):
        for g in range(8):
            st_row[row : row + 1, g * lanes : (g + 1) * lanes] = tile[g : g + 1, :]

    def total(buf, k):
        return lax.fori_loop(
            1, n, lambda s, t: t + buf[s, k], buf[0, k]
        )

    def mp_copy(k, src, dst):
        return pltpu.make_async_remote_copy(
            src_ref=src,
            dst_ref=dst,
            send_sem=mp_ssem.at[k],
            recv_sem=mp_rsem.at[k],
            device_id=peer,
            device_id_type=MESH,
        )

    mask = aux_ref[:, 2 * fan + 2 : 2 * fan + 3]
    own_count = jnp.sum(mask, axis=0, keepdims=True)
    own_inv = 1.0 / jnp.maximum(own_count, 1.0)

    def pick(src):
        pack_halo(mm(sel[...], src[:, :half]), mm(sel[...], src[:, half:]))

    pick(f_ref)
    pl.semaphore_wait(barrier, n)
    halo_start()

    rb = 16
    slots = lax.broadcasted_iota(jnp.int32, (rb, lookup), 1).astype(F32)

    def build(i, _):
        r = pl.ds(pl.multiple_of(i * rb, rb), rb)
        part = aux_ref[r, :]
        a = jnp.zeros((rb, lookup), F32)
        for k in range(fan + 1):
            a = a + jnp.where(
                part[:, k : k + 1] == slots, part[:, fan + 1 + k : fan + 2 + k], 0.0
            )
        adj[r, :] = a.astype(BF)
        return 0

    lax.fori_loop(0, nodes // rb, build, 0)

    def turn(i, _):
        r = pl.ds(pl.multiple_of(i * 128, 128), 128)
        adj_t[r, :] = adj[:, r].astype(F32).T.astype(BF)
        return 0

    def turn_sel(i, _):
        r = pl.ds(pl.multiple_of(i * 128, 128), 128)
        sel_t[:, r] = sel[r, :].astype(F32).T.astype(BF)
        return 0

    stats = []
    gain_rows, shift_rows = [], []
    for layer in range(2):
        src = f_ref if layer == 0 else h1_ref
        for h in range(2):
            cs = slice(h * half, (h + 1) * half)
            zacc[:, cs] = mm(adj[:, :nodes], src[:, cs])
        if layer == 0:
            lax.fori_loop(0, lookup // 128, turn, 0)
            lax.fori_loop(0, halo // 128, turn_sel, 0)
        halo_finish()
        parts = halo_read()
        y_copy = []
        for h in range(2):
            cs = slice(h * half, (h + 1) * half)
            yf[layer, m, :, cs] = (zacc[:, cs] + mm(adj[:, nodes:], parts[h])).astype(BF)
            copy = mp_copy(
                layer * 2 + h, yf.at[layer, m, :, cs], yf.at[layer, m, :, cs]
            )
            copy.start()
            y_copy.append(copy)
        w_copies[layer].wait()

        def first(j, _):
            zacc[:, col(j)] = mm(
                yf[layer, m],
                w_ref[layer, pl.ds(pl.multiple_of(m * cols, cols), cols), col(j)],
            )
            return 0

        lax.fori_loop(0, tiles, first, 0)
        for copy in y_copy:
            copy.wait_recv()
        if layer == 1:
            og_copy.wait()

        def second(j, _):
            z = zacc[:, col(j)] + mm(
                yf[layer, 1 - m],
                w_ref[layer, pl.ds(pl.multiple_of((1 - m) * cols, cols), cols), col(j)],
            )
            z = z + par_ref[layer : layer + 1, col(j)]
            sig = jax.nn.sigmoid(z)
            s = z * sig
            s_ref[layer, :, col(j)] = s
            d_ref[layer, :, col(j)] = sig * (1.0 + z * (1.0 - sig))
            tot = jnp.sum(s * mask, axis=0, keepdims=True)
            cen = s - tot * own_inv
            st_row[0:1, col(j)] = tot
            st_row[1:2, col(j)] = jnp.sum(cen * cen * mask, axis=0, keepdims=True)
            if layer == 0:
                st_row[2:3, col(j)] = jnp.broadcast_to(own_count, (1, ct))
            else:
                pg = og_ref[:, col(j)].astype(F32) * mask
                st_row[2:3, col(j)] = jnp.sum(pg, axis=0, keepdims=True)
                st_row[3:4, col(j)] = jnp.sum(pg * cen, axis=0, keepdims=True)
            return 0

        lax.fori_loop(0, tiles, second, 0)
        buf = stat0 if layer == 0 else stat1
        for k in range(3 if layer == 0 else 4):
            fold(buf, k, k)
        stat_start(layer, buf)
        for copy in y_copy:
            copy.wait_send()
        y_out = pltpu.make_async_copy(yf.at[layer], y_hbm.at[layer], out_sem.at[2 + layer])
        y_out.start()
        stat_finish(layer, buf)
        count = jnp.maximum(total(stat0, 2), 1.0)
        mu = total(buf, 0) / count

        def spread(s, t):
            nc = stat0[s, 2]
            off = buf[s, 0] / jnp.maximum(nc, 1.0) - mu
            return t + buf[s, 1] + nc * off * off

        var = lax.fori_loop(0, n, spread, jnp.zeros_like(mu)) / count
        inv = lax.rsqrt(var + EPS)
        unfold(mu, 4)
        unfold(inv, 5)
        stats.append((mu, inv, count, y_out))
        mu_row, inv_row = st_row[4:5, :], st_row[5:6, :]
        gain_row = par_ref[2 + layer : 3 + layer, :]
        shift_row = par_ref[4 + layer : 5 + layer, :]
        dst = h1_ref if layer == 0 else out_ref
        if layer == 0:
            unfold(mu, 8)
            unfold(inv, 9)
        for j in range(tiles):
            cs = slice(j * ct, (j + 1) * ct)
            x = (s_ref[layer, :, cs] - mu_row[:, cs]) * inv_row[:, cs]
            dst[:, cs] = (mask * (gain_row[:, cs] * x + shift_row[:, cs])).astype(BF)
        if layer == 0:
            pick(h1_ref)
            halo_start()
    out_copy = pltpu.make_async_copy(out_ref, out_hbm, out_sem.at[0])
    out_copy.start()

    mu, inv, count, _ = stats[1]

    def gains(s, t):
        off = stat1[s, 0] / jnp.maximum(stat0[s, 2], 1.0) - mu
        return t + stat1[s, 3] + off * stat1[s, 2]

    gg = inv * lax.fori_loop(0, n, gains, jnp.zeros_like(mu))
    sg = total(stat1, 2)
    unfold(sg, 6)
    unfold(gg, 7)
    small_ref[2:3, :] = st_row[7:8, :]
    small_ref[4:5, :] = st_row[6:7, :]
    inv_count = 1.0 / jnp.concatenate([count] * 1, axis=0)
    unfold(inv_count, 10)
    dz_copies = []
    for layer in (1, 0):
        if layer == 1:
            mu_r, inv_r = 4, 5
        else:
            mu_r, inv_r = 8, 9
        grad_src = og_ref if layer == 1 else g_ref

        def pre(j, _):
            gain = par_ref[2 + layer : 3 + layer, col(j)]
            inv_row = st_row[inv_r : inv_r + 1, col(j)]
            ic = st_row[10:11, col(j)]
            x = (s_ref[layer, :, col(j)] - st_row[mu_r : mu_r + 1, col(j)]) * inv_row
            pg = grad_src[:, col(j)].astype(F32) * mask
            ds = (
                mask
                * (inv_row * gain)
                * (
                    pg
                    - st_row[6:7, col(j)] * ic
                    - x * (st_row[7:8, col(j)] * ic)
                )
            )
            dz = (ds * d_ref[layer, :, col(j)]).astype(BF)
            dz_ref[layer, :, col(j)] = dz
            st_row[11:12, col(j)] = jnp.sum(dz.astype(F32), axis=0, keepdims=True)
            return 0

        lax.fori_loop(0, tiles, pre, 0)
        dz_out = pltpu.make_async_copy(dz_ref.at[layer], dz_hbm.at[layer], out_sem.at[4 + layer])
        dz_out.start()
        dz_copies.append(dz_out)

        if layer == 1:
            fold(stat2, 2, 11)
        else:
            fold(stat3, 0, 11)
            stat_start(3, stat3)

        def other(j, _):
            r = pl.ds(pl.multiple_of((1 - m) * cols + j * ct, ct), ct)
            dy_send[:, col(j)] = mm_t(dz_ref[layer], w_ref[layer, r, :]).astype(BF)
            return 0

        lax.fori_loop(0, tiles, other, 0)
        dy_copy = mp_copy(4 + layer, dy_send, dy_recv.at[layer])
        dy_copy.start()

        def mine(j, _):
            r = pl.ds(pl.multiple_of(m * cols + j * ct, ct), ct)
            dy_own[:, col(j)] = mm_t(dz_ref[layer], w_ref[layer, r, :])
            return 0

        lax.fori_loop(0, tiles, mine, 0)
        dy_copy.wait_recv()
        for j in range(tiles):
            cs = slice(j * ct, (j + 1) * ct)
            dyb[:, cs] = (dy_own[:, cs] + dy_recv[layer, :, cs].astype(F32)).astype(BF)
        pack_halo(mm(adj_t[nodes:, :], dyb[:, :half]), mm(adj_t[nodes:, :], dyb[:, half:]))
        halo_start()
        for h in range(2):
            cs = slice(h * half, (h + 1) * half)
            g_ref[:, cs] = mm(adj_t[:nodes, :], dyb[:, cs])
        dy_copy.wait_send()
        halo_finish()
        parts = halo_read()
        for h in range(2):
            cs = slice(h * half, (h + 1) * half)
            got = g_ref[:, cs] + mm(sel_t[...], parts[h])
            if layer == 1:
                g_ref[:, cs] = got
                pg = got * mask
                x = (s_ref[0, :, cs] - st_row[8:9, cs]) * st_row[9:10, cs]
                st_row[0:1, cs] = jnp.sum(pg, axis=0, keepdims=True)
                st_row[1:2, cs] = jnp.sum(pg * x, axis=0, keepdims=True)
            else:
                h1_ref[:, cs] = got.astype(BF)
        if layer == 1:
            fold(stat2, 0, 0)
            fold(stat2, 1, 1)
            stat_start(2, stat2)
            stat_finish(2, stat2)
            unfold(total(stat2, 0), 6)
            unfold(total(stat2, 1), 7)
            unfold(total(stat2, 2), 12)
            small_ref[1:2, :] = st_row[7:8, :]
            small_ref[3:4, :] = st_row[6:7, :]
            small_ref[5:6, :] = st_row[12:13, :]
    ig_copy = pltpu.make_async_copy(h1_ref, ig_hbm, out_sem.at[1])
    ig_copy.start()
    stat_finish(3, stat3)
    unfold(total(stat3, 0), 12)
    small_ref[0:1, :] = st_row[12:13, :]
    small_ref[6:8, :] = jnp.zeros((2, cols), F32)
    out_copy.wait()
    ig_copy.wait()
    for copy in dz_copies:
        copy.wait()
    for entry in stats:
        entry[3].wait()


def per_device(
    features, neighbour_ids, edge_weight, self_weight, send_rows, valid_mask,
    weights, biases, norm_gain, norm_shift, output_grad,
):
    nodes, cols = features.shape
    fan = neighbour_ids.shape[1]
    n, cap = send_rows.shape[1], send_rows.shape[2]
    halo = n * cap
    lookup = nodes + halo
    aux = jnp.concatenate(
        [
            neighbour_ids.astype(F32),
            lax.broadcasted_iota(jnp.int32, (nodes, 1), 0).astype(F32),
            edge_weight,
            2.0 * self_weight[:, None],
            valid_mask.astype(F32)[:, None],
        ],
        axis=1,
    )
    rows = send_rows.reshape(halo, 1)
    params = jnp.concatenate([biases, norm_gain, norm_shift], axis=0)
    vm = pl.BlockSpec(memory_space=pltpu.VMEM)
    anyspace = pl.BlockSpec(memory_space=pl.ANY)
    dma = pltpu.SemaphoreType.DMA
    out, ig, y, dz, small = pl.pallas_call(
        functools.partial(chain, n, cap, fan),
        out_shape=(
            jax.ShapeDtypeStruct((nodes, cols), BF),
            jax.ShapeDtypeStruct((nodes, cols), BF),
            jax.ShapeDtypeStruct((2, 2, nodes, cols), BF),
            jax.ShapeDtypeStruct((2, nodes, cols), BF),
            jax.ShapeDtypeStruct((8, cols), F32),
        ),
        in_specs=[vm, vm, vm, vm, anyspace, anyspace],
        out_specs=(anyspace, anyspace, anyspace, anyspace, vm),
        scratch_shapes=[
            pltpu.VMEM((2, 2 * cols, cols), BF),
            pltpu.VMEM((nodes, cols), BF),
            pltpu.VMEM((nodes, lookup), BF),
            pltpu.VMEM((lookup, nodes), BF),
            pltpu.VMEM((halo, nodes), BF),
            pltpu.VMEM((nodes, halo), BF),
            pltpu.VMEM((nodes, cols), BF),
            pltpu.VMEM((nodes, cols), BF),
            pltpu.VMEM((2, 2, nodes, cols), BF),
            pltpu.VMEM((2, nodes, cols), F32),
            pltpu.VMEM((2, nodes, cols), F32),
            pltpu.VMEM((nodes, cols), F32),
            pltpu.VMEM((2, nodes, cols), BF),
            pltpu.VMEM((nodes, cols), F32),
            pltpu.VMEM((nodes, cols), BF),
            pltpu.VMEM((2, nodes, cols), BF),
            pltpu.VMEM((nodes, cols), BF),
            pltpu.VMEM((nodes, cols), F32),
            pltpu.VMEM((2 * halo, cols // 2), BF),
            pltpu.VMEM((2 * halo, cols // 2), BF),
            pltpu.VMEM((16, cols), F32),
            pltpu.VMEM((n, 3, 8, cols // 8), F32),
            pltpu.VMEM((n, 4, 8, cols // 8), F32),
            pltpu.VMEM((n, 3, 8, cols // 8), F32),
            pltpu.VMEM((n, 1, 8, cols // 8), F32),
            dma((2,)), dma, dma((6,)), dma((6,)), dma((6,)),
            dma((n,)), dma((n,)), dma((4, n)), dma((4, n)),
        ],
        compiler_params=pltpu.CompilerParams(
            collective_id=0, has_side_effects=True, vmem_limit_bytes=60 * 2**20
        ),
    )(features, aux, rows, params, output_grad, weights)
    parts = jnp.einsum("lhni,lnj->lhij", y, dz, preferred_element_type=F32)
    parts = parts.reshape(2, 2 * cols, cols).astype(BF)
    weight_grad = lax.psum(parts, "cluster").astype(F32)
    return out, ig, weight_grad, jnp.stack([small[0], small[5]]), small[1:3], small[3:5]


def solution(mesh):
    return jax.shard_map(
        per_device,
        mesh=mesh,
        in_specs=(
            P("cluster", "mp"),
            P("cluster", None),
            P("cluster", None),
            P("cluster"),
            P("cluster", None, None),
            P("cluster"),
            P(None, None, "mp"),
            P(None, "mp"),
            P(None, "mp"),
            P(None, "mp"),
            P("cluster", "mp"),
        ),
        out_specs=(
            P("cluster", "mp"),
            P("cluster", "mp"),
            P(None, None, "mp"),
            P(None, "mp"),
            P(None, "mp"),
            P(None, "mp"),
        ),
        check_vma=False,
    )
```

```python
import functools

import jax
import jax.numpy as jnp
from jax import lax
from jax.experimental import pallas as pl
from jax.experimental.pallas import tpu as pltpu
from jax.sharding import PartitionSpec as P

EPS = 1e-05
MESH = pl.DeviceIdType.MESH
BF = jnp.bfloat16
F32 = jnp.float32


def mm(a, b):
    return jnp.dot(a, b, preferred_element_type=F32)


def mm_t(a, b):
    return lax.dot_general(a, b, (((1,), (1,)), ((), ())), preferred_element_type=F32)


def chain(
    n, cap, fan,
    f_ref, aux_ref, rows_ref, par_ref, og_hbm, w_hbm,
    out_hbm, ig_hbm, wg_hbm, small_ref,
    w_ref, og_ref, adj, adj_t, sel, sel_t, h1_ref, yf, s_ref, d_ref, zacc,
    dy_recv, hsend, hrecv, st_row, stat0, stat1, stat2, stat3,
    yt, yr, dzr, wpart, zr, fin,
    w_sem, og_sem, out_sem, mp_ssem, mp_rsem, h_ssem, h_rsem, x_ssem, x_rsem,
    y_sem, yp_sem, dz_sem, zr_sem, az_sem, ax_sem, ay_sem, rl_sem, fin_sem,
):
    nodes, cols = f_ref.shape
    ct = 256
    tiles = cols // ct
    half = cols // 2
    c = lax.axis_index("cluster")
    m = lax.axis_index("mp")
    peer = (c, 1 - m)
    halo = n * cap
    lookup = nodes + halo
    line = n // 4
    zi, p = c // 4, c % 4
    px, py = p % 2, p // 2
    near = (c + 1 - 2 * px, c + 2 - 4 * py, c + 3 - 2 * px - 4 * py)
    rc = cols // line
    dy_own, dyb, g_ref = zacc, og_ref, s_ref.at[1]
    out_ref, dy_send, dz_ref = yf.at[0, 0], yf.at[0, 1], yf.at[1]

    def quarter(layer, who):
        qx = 1 - px if who in (0, 2) else px
        qy = 1 - py if who in (1, 2) else py
        return (qx, qy) if layer == 1 else (qy, qx)

    barrier = pltpu.get_barrier_semaphore()

    def greet(i, _):
        pl.semaphore_signal(
            barrier, inc=1, device_id=(lax.rem(c + i, n), m), device_id_type=MESH
        )
        return 0

    lax.fori_loop(1, n, greet, 0)
    pl.semaphore_signal(barrier, inc=1, device_id=peer, device_id_type=MESH)

    w_copies = [
        pltpu.make_async_copy(w_hbm.at[layer], w_ref.at[layer], w_sem.at[layer])
        for layer in range(2)
    ]
    w_copies[0].start()
    og_copy = pltpu.make_async_copy(og_hbm, og_ref, og_sem)
    og_copy.start()
    w_copies[1].start()

    sel_f = jnp.where(
        rows_ref[...] == lax.broadcasted_iota(jnp.int32, (halo, nodes), 1), 1.0, 0.0
    )
    sel[...] = sel_f.astype(BF)

    def col(j):
        return pl.ds(pl.multiple_of(j * ct, ct), ct)

    def pack_halo(left, right):
        both = jnp.concatenate(
            [left.reshape(n, cap, half), right.reshape(n, cap, half)], axis=1
        )
        hsend[...] = both.reshape(n * 2 * cap, half).astype(BF)

    def halo_part(d):
        return pl.ds(pl.multiple_of(d * 2 * cap, 2 * cap), 2 * cap)

    def halo_start():
        def send(i, _):
            d = lax.rem(c + i, n)
            pltpu.make_async_remote_copy(
                src_ref=hsend.at[halo_part(d)],
                dst_ref=hrecv.at[halo_part(c)],
                send_sem=h_ssem.at[d],
                recv_sem=h_rsem.at[c],
                device_id=(d, m),
                device_id_type=MESH,
            ).start()
            return 0

        lax.fori_loop(1, n, send, 0)
        hrecv[halo_part(c)] = hsend[halo_part(c)]

    def halo_finish():
        def finish(i, _):
            s = lax.rem(c + i, n)
            copy = pltpu.make_async_remote_copy(
                src_ref=hsend.at[halo_part(s)],
                dst_ref=hrecv.at[halo_part(s)],
                send_sem=h_ssem.at[s],
                recv_sem=h_rsem.at[s],
                device_id=(s, m),
                device_id_type=MESH,
            )
            copy.wait_recv()
            copy.wait_send()
            return 0

        lax.fori_loop(1, n, finish, 0)

    def halo_read():
        got = hrecv[...].astype(F32).reshape(n, 2 * cap, half)
        left = got[:, :cap, :].reshape(halo, half).astype(BF)
        right = got[:, cap:, :].reshape(halo, half).astype(BF)
        return left, right

    def stat_start(e, buf):
        def send(i, _):
            d = lax.rem(c + i, n)
            pltpu.make_async_remote_copy(
                src_ref=buf.at[c],
                dst_ref=buf.at[c],
                send_sem=x_ssem.at[e, d],
                recv_sem=x_rsem.at[e, c],
                device_id=(d, m),
                device_id_type=MESH,
            ).start()
            return 0

        lax.fori_loop(1, n, send, 0)

    def stat_finish(e, buf):
        def finish(i, _):
            s = lax.rem(c + i, n)
            copy = pltpu.make_async_remote_copy(
                src_ref=buf.at[c],
                dst_ref=buf.at[s],
                send_sem=x_ssem.at[e, s],
                recv_sem=x_rsem.at[e, s],
                device_id=(s, m),
                device_id_type=MESH,
            )
            copy.wait_recv()
            copy.wait_send()
            return 0

        lax.fori_loop(1, n, finish, 0)

    lanes = cols // 8

    def fold(buf, k, row):
        for g in range(8):
            buf[c, k, g : g + 1, :] = st_row[row : row + 1, g * lanes : (g + 1) * lanes]

    def unfold(tile, row):
        for g in range(8):
            st_row[row : row + 1, g * lanes : (g + 1) * lanes] = tile[g : g + 1, :]

    def total(buf, k):
        return lax.fori_loop(
            1, n, lambda s, t: t + buf[s, k], buf[0, k]
        )

    def mp_copy(k, src, dst):
        return pltpu.make_async_remote_copy(
            src_ref=src,
            dst_ref=dst,
            send_sem=mp_ssem.at[k],
            recv_sem=mp_rsem.at[k],
            device_id=peer,
            device_id_type=MESH,
        )

    def remote(src, dst, sems, idx, to):
        return pltpu.make_async_remote_copy(
            src_ref=src,
            dst_ref=dst,
            send_sem=sems.at[(0, *idx)],
            recv_sem=sems.at[(1, *idx)],
            device_id=to,
            device_id_type=MESH,
        )

    def rows_of(start, size):
        return pl.ds(pl.multiple_of(start, size), size)

    def y_copy_to(layer, who):
        hr, _ = quarter(layer, who)
        return remote(
            yt.at[layer, rows_of(hr * cols + m * half, half), :],
            yr.at[layer, who, rows_of(m * half, half), :],
            y_sem, (layer, who), (near[who], m),
        )

    def y_start(layer):
        def flip(i, _):
            r = pl.ds(pl.multiple_of(i * 128, 128), 128)
            for h in range(2):
                d = pl.ds(pl.multiple_of(h * cols + i * 128, 128), 128)
                yt[layer, d, :] = yf[layer, h, :, r].astype(F32).T.astype(BF)
            return 0

        lax.fori_loop(0, cols // 128, flip, 0)
        for who in range(3):
            y_copy_to(layer, who).start()

    def y_pass_copy(layer, who, part):
        r = rows_of(part * half, half)
        return remote(
            yr.at[layer, who, r, :], yr.at[layer, who, r, :], yp_sem, (layer, who), peer
        )

    def y_pass(layer):
        for who in range(3):
            y_copy_to(layer, who).wait()
            y_pass_copy(layer, who, m).start()

    def y_finish(layer):
        for who in range(3):
            y_pass_copy(layer, who, m).wait_send()
            y_pass_copy(layer, who, 1 - m).wait_recv()

    def dz_copy_to(layer, who, sb):
        _, hc = quarter(layer, who)
        return remote(
            dz_ref.at[layer, :, rows_of(hc * half + sb * ct, ct)],
            dzr.at[layer, who, sb],
            dz_sem, (layer, who, sb), (near[who], m),
        )

    def dz_start(layer):
        for sb in range(2):
            for who in range(3):
                dz_copy_to(layer, who, sb).start()

    def line_copy(layer, sb, to, frm):
        return remote(
            wpart.at[layer, sb, rows_of(to * rc, rc), :],
            zr.at[layer, sb, frm],
            zr_sem, (layer, sb, frm), (to * 4 + p, m),
        )

    def product(layer, sb):
        hr, hc = quarter(layer, 3)
        for who in range(3):
            dz_copy_to(layer, who, sb).wait()
        mine_dz = dz_ref[layer, :, rows_of(hc * half + sb * ct, ct)]

        def one(i, _):
            r = pl.ds(pl.multiple_of(i * ct, ct), ct)
            acc = mm(yt[layer, pl.ds(pl.multiple_of(hr * cols + i * ct, ct), ct), :], mine_dz)
            for who in range(3):
                acc = acc + mm(yr[layer, who, r, :], dzr[layer, who, sb])
            wpart[layer, sb, r, :] = acc.astype(BF)
            return 0

        lax.fori_loop(0, cols // ct, one, 0)

        def send(i, _):
            to = (zi + i) % line
            pltpu.make_async_remote_copy(
                src_ref=wpart.at[layer, sb, rows_of(to * rc, rc), :],
                dst_ref=zr.at[layer, sb, zi],
                send_sem=zr_sem.at[0, layer, sb, to],
                recv_sem=zr_sem.at[1, layer, sb, zi],
                device_id=(to * 4 + p, m),
                device_id_type=MESH,
            ).start()
            return 0

        lax.fori_loop(1, line, send, 0)

    def spot(layer, who, sb, k):
        hr, hc = quarter(layer, who)
        return wg_hbm.at[
            layer, rows_of(hr * cols + k * rc, rc), rows_of(hc * half + sb * ct, ct)
        ]

    def across(layer, sb, k, who):
        sems = ax_sem if who == 0 else ay_sem
        return remote(
            spot(layer, 3, sb, k), spot(layer, 3, sb, k), sems, (layer, sb, k), (near[who], m)
        )

    def along(layer, sb, i, frm):
        to = (zi + i) % line
        return pltpu.make_async_remote_copy(
            src_ref=spot(layer, 3, sb, frm),
            dst_ref=spot(layer, 3, sb, frm),
            send_sem=az_sem.at[0, layer, sb, to],
            recv_sem=az_sem.at[1, layer, sb, frm],
            device_id=(to * 4 + p, m),
            device_id_type=MESH,
        )

    def relay(layer, sb, k, first):
        return remote(
            spot(layer, first, sb, k), spot(layer, first, sb, k), rl_sem, (layer, sb, k),
            (near[1 - first], m),
        )

    def combine(layer, sb):
        def take(i, _):
            frm = (zi + i) % line
            copy = pltpu.make_async_remote_copy(
                src_ref=wpart.at[layer, sb, rows_of(frm * rc, rc), :],
                dst_ref=zr.at[layer, sb, frm],
                send_sem=zr_sem.at[0, layer, sb, frm],
                recv_sem=zr_sem.at[1, layer, sb, frm],
                device_id=(frm * 4 + p, m),
                device_id_type=MESH,
            )
            copy.wait_recv()
            copy.wait_send()
            return 0

        lax.fori_loop(1, line, take, 0)
        zr[layer, sb, zi] = wpart[layer, sb, rows_of(zi * rc, rc), :]
        fin[layer, sb] = lax.fori_loop(
            1, line,
            lambda j, t: t + zr[layer, sb, j].astype(F32),
            zr[layer, sb, 0].astype(F32),
        ).astype(BF)
        keep = pltpu.make_async_copy(
            fin.at[layer, sb], spot(layer, 3, sb, zi), fin_sem.at[layer, sb]
        )
        keep.start()
        keep.wait()

        def send(i, _):
            along(layer, sb, i, zi).start()
            return 0

        for who in range(2):
            across(layer, sb, zi, who).start()
        lax.fori_loop(1, line, send, 0)

    def spread_blocks(layer, sb):
        def step(u, _):
            for odd in range(2):
                i = 2 * u + odd
                k = (zi + i) % line

                @pl.when(i > 0)
                def _():
                    along(layer, sb, i, k).wait_recv()
                    for who in range(2):
                        across(layer, sb, k, who).start()

                arrived(layer, sb, k, odd).wait_recv()
                relay(layer, sb, k, odd).start()
            return 0

        lax.fori_loop(0, line // 2, step, 0)

    def arrived(layer, sb, k, who):
        sems = ax_sem if who == 0 else ay_sem
        return remote(
            spot(layer, who, sb, k), spot(layer, who, sb, k), sems, (layer, sb, k), (near[who], m)
        )

    def finish_blocks(layer, sb):
        def step(u, _):
            for odd in range(2):
                i = 2 * u + odd
                k = (zi + i) % line
                arrived(layer, sb, k, 1 - odd).wait_recv()
                relay(layer, sb, k, odd).wait_send()
                remote(
                    spot(layer, 2, sb, k), spot(layer, 2, sb, k), rl_sem, (layer, sb, k),
                    (near[1 - odd], m),
                ).wait_recv()
                for who in range(2):
                    across(layer, sb, k, who).wait_send()

                @pl.when(i > 0)
                def _():
                    along(layer, sb, i, zi).wait_send()
            return 0

        lax.fori_loop(0, line // 2, step, 0)

    mask = aux_ref[:, 2 * fan + 2 : 2 * fan + 3]
    own_count = jnp.sum(mask, axis=0, keepdims=True)
    own_inv = 1.0 / jnp.maximum(own_count, 1.0)

    def pick(src):
        pack_halo(mm(sel[...], src[:, :half]), mm(sel[...], src[:, half:]))

    pick(f_ref)
    pl.semaphore_wait(barrier, n)
    halo_start()

    rb = 16
    slots = lax.broadcasted_iota(jnp.int32, (rb, lookup), 1).astype(F32)

    def build(i, _):
        r = pl.ds(pl.multiple_of(i * rb, rb), rb)
        part = aux_ref[r, :]
        a = jnp.zeros((rb, lookup), F32)
        for k in range(fan + 1):
            a = a + jnp.where(
                part[:, k : k + 1] == slots, part[:, fan + 1 + k : fan + 2 + k], 0.0
            )
        adj[r, :] = a.astype(BF)
        return 0

    lax.fori_loop(0, nodes // rb, build, 0)

    def turn(i, _):
        r = pl.ds(pl.multiple_of(i * 128, 128), 128)
        adj_t[r, :] = adj[:, r].astype(F32).T.astype(BF)
        return 0

    def turn_sel(i, _):
        r = pl.ds(pl.multiple_of(i * 128, 128), 128)
        sel_t[:, r] = sel[r, :].astype(F32).T.astype(BF)
        return 0

    stats = []
    gain_rows, shift_rows = [], []
    for layer in range(2):
        src = f_ref if layer == 0 else h1_ref
        for h in range(2):
            cs = slice(h * half, (h + 1) * half)
            zacc[:, cs] = mm(adj[:, :nodes], src[:, cs])
        if layer == 0:
            lax.fori_loop(0, lookup // 128, turn, 0)
            lax.fori_loop(0, halo // 128, turn_sel, 0)
        halo_finish()
        parts = halo_read()
        y_copy = []
        for h in range(2):
            cs = slice(h * half, (h + 1) * half)
            yf[layer, m, :, cs] = (zacc[:, cs] + mm(adj[:, nodes:], parts[h])).astype(BF)
            copy = mp_copy(
                layer * 2 + h, yf.at[layer, m, :, cs], yf.at[layer, m, :, cs]
            )
            copy.start()
            y_copy.append(copy)
        w_copies[layer].wait()

        def first(j, _):
            zacc[:, col(j)] = mm(
                yf[layer, m],
                w_ref[layer, pl.ds(pl.multiple_of(m * cols, cols), cols), col(j)],
            )
            return 0

        lax.fori_loop(0, tiles, first, 0)
        for copy in y_copy:
            copy.wait_recv()
        if layer == 1:
            og_copy.wait()

        def second(j, _):
            z = zacc[:, col(j)] + mm(
                yf[layer, 1 - m],
                w_ref[layer, pl.ds(pl.multiple_of((1 - m) * cols, cols), cols), col(j)],
            )
            z = z + par_ref[layer : layer + 1, col(j)]
            sig = jax.nn.sigmoid(z)
            s = z * sig
            s_ref[layer, :, col(j)] = s
            d_ref[layer, :, col(j)] = (sig * (1.0 + z * (1.0 - sig))).astype(BF)
            tot = jnp.sum(s * mask, axis=0, keepdims=True)
            cen = s - tot * own_inv
            st_row[0:1, col(j)] = tot
            st_row[1:2, col(j)] = jnp.sum(cen * cen * mask, axis=0, keepdims=True)
            if layer == 0:
                st_row[2:3, col(j)] = jnp.broadcast_to(own_count, (1, ct))
            else:
                pg = og_ref[:, col(j)].astype(F32) * mask
                st_row[2:3, col(j)] = jnp.sum(pg, axis=0, keepdims=True)
                st_row[3:4, col(j)] = jnp.sum(pg * cen, axis=0, keepdims=True)
            return 0

        lax.fori_loop(0, tiles, second, 0)
        buf = stat0 if layer == 0 else stat1
        for k in range(3 if layer == 0 else 4):
            fold(buf, k, k)
        stat_start(layer, buf)
        for copy in y_copy:
            copy.wait_send()
        y_start(layer)
        stat_finish(layer, buf)
        count = jnp.maximum(total(stat0, 2), 1.0)
        mu = total(buf, 0) / count

        def spread(s, t):
            nc = stat0[s, 2]
            off = buf[s, 0] / jnp.maximum(nc, 1.0) - mu
            return t + buf[s, 1] + nc * off * off

        var = lax.fori_loop(0, n, spread, jnp.zeros_like(mu)) / count
        inv = lax.rsqrt(var + EPS)
        unfold(mu, 4)
        unfold(inv, 5)
        stats.append((mu, inv, count))
        mu_row, inv_row = st_row[4:5, :], st_row[5:6, :]
        gain_row = par_ref[2 + layer : 3 + layer, :]
        shift_row = par_ref[4 + layer : 5 + layer, :]
        dst = h1_ref if layer == 0 else out_ref
        if layer == 0:
            unfold(mu, 8)
            unfold(inv, 9)
        for j in range(tiles):
            cs = slice(j * ct, (j + 1) * ct)
            x = (s_ref[layer, :, cs] - mu_row[:, cs]) * inv_row[:, cs]
            dst[:, cs] = (mask * (gain_row[:, cs] * x + shift_row[:, cs])).astype(BF)
        if layer == 0:
            pick(h1_ref)
            halo_start()
    out_copy = pltpu.make_async_copy(out_ref, out_hbm, out_sem.at[0])
    out_copy.start()

    mu, inv, count = stats[1]

    def gains(s, t):
        off = stat1[s, 0] / jnp.maximum(stat0[s, 2], 1.0) - mu
        return t + stat1[s, 3] + off * stat1[s, 2]

    gg = inv * lax.fori_loop(0, n, gains, jnp.zeros_like(mu))
    sg = total(stat1, 2)
    unfold(sg, 6)
    unfold(gg, 7)
    small_ref[2:3, :] = st_row[7:8, :]
    small_ref[4:5, :] = st_row[6:7, :]
    inv_count = 1.0 / count
    unfold(inv_count, 10)
    for layer in (1, 0):
        if layer == 1:
            mu_r, inv_r = 4, 5
        else:
            mu_r, inv_r = 8, 9
        grad_src = og_ref if layer == 1 else g_ref

        def pre(j, _):
            gain = par_ref[2 + layer : 3 + layer, col(j)]
            inv_row = st_row[inv_r : inv_r + 1, col(j)]
            ic = st_row[10:11, col(j)]
            x = (s_ref[layer, :, col(j)] - st_row[mu_r : mu_r + 1, col(j)]) * inv_row
            pg = grad_src[:, col(j)].astype(F32) * mask
            ds = (
                mask
                * (inv_row * gain)
                * (
                    pg
                    - st_row[6:7, col(j)] * ic
                    - x * (st_row[7:8, col(j)] * ic)
                )
            )
            dz = (ds * d_ref[layer, :, col(j)].astype(F32)).astype(BF)
            dz_ref[layer, :, col(j)] = dz
            st_row[11:12, col(j)] = jnp.sum(dz.astype(F32), axis=0, keepdims=True)
            return 0

        lax.fori_loop(0, tiles, pre, 0)
        dz_start(layer)

        if layer == 1:
            fold(stat2, 2, 11)
        else:
            fold(stat3, 0, 11)
            stat_start(3, stat3)

        def other(j, _):
            r = pl.ds(pl.multiple_of((1 - m) * cols + j * ct, ct), ct)
            dy_send[:, col(j)] = mm_t(dz_ref[layer], w_ref[layer, r, :]).astype(BF)
            return 0

        lax.fori_loop(0, tiles, other, 0)
        dy_copy = mp_copy(4 + layer, dy_send, dy_recv.at[layer])
        dy_copy.start()

        def mine(j, _):
            r = pl.ds(pl.multiple_of(m * cols + j * ct, ct), ct)
            dy_own[:, col(j)] = mm_t(dz_ref[layer], w_ref[layer, r, :])
            return 0

        lax.fori_loop(0, tiles, mine, 0)
        dy_copy.wait_recv()
        for j in range(tiles):
            cs = slice(j * ct, (j + 1) * ct)
            dyb[:, cs] = (dy_own[:, cs] + dy_recv[layer, :, cs].astype(F32)).astype(BF)
        pack_halo(mm(adj_t[nodes:, :], dyb[:, :half]), mm(adj_t[nodes:, :], dyb[:, half:]))
        halo_start()
        for h in range(2):
            cs = slice(h * half, (h + 1) * half)
            g_ref[:, cs] = mm(adj_t[:nodes, :], dyb[:, cs])
        dy_copy.wait_send()
        if layer == 0:
            y_finish(1)
            for sb in range(2):
                product(1, sb)
        halo_finish()
        parts = halo_read()
        for h in range(2):
            cs = slice(h * half, (h + 1) * half)
            got = g_ref[:, cs] + mm(sel_t[...], parts[h])
            if layer == 1:
                g_ref[:, cs] = got
                pg = got * mask
                x = (s_ref[0, :, cs] - st_row[8:9, cs]) * st_row[9:10, cs]
                st_row[0:1, cs] = jnp.sum(pg, axis=0, keepdims=True)
                st_row[1:2, cs] = jnp.sum(pg * x, axis=0, keepdims=True)
            else:
                h1_ref[:, cs] = got.astype(BF)
        if layer == 1:
            fold(stat2, 0, 0)
            fold(stat2, 1, 1)
            stat_start(2, stat2)
            y_pass(0)
            y_pass(1)
            stat_finish(2, stat2)
            unfold(total(stat2, 0), 6)
            unfold(total(stat2, 1), 7)
            unfold(total(stat2, 2), 12)
            small_ref[1:2, :] = st_row[7:8, :]
            small_ref[3:4, :] = st_row[6:7, :]
            small_ref[5:6, :] = st_row[12:13, :]
    ig_copy = pltpu.make_async_copy(h1_ref, ig_hbm, out_sem.at[1])
    ig_copy.start()
    for sb in range(2):
        combine(1, sb)
    y_finish(0)
    for sb in range(2):
        product(0, sb)
    for sb in range(2):
        spread_blocks(1, sb)
    for sb in range(2):
        combine(0, sb)
    for sb in range(2):
        spread_blocks(0, sb)
    stat_finish(3, stat3)
    unfold(total(stat3, 0), 12)
    small_ref[0:1, :] = st_row[12:13, :]
    small_ref[6:8, :] = jnp.zeros((2, cols), F32)
    out_copy.wait()
    ig_copy.wait()
    for layer in (1, 0):
        for sb in range(2):
            finish_blocks(layer, sb)


def per_device(
    features, neighbour_ids, edge_weight, self_weight, send_rows, valid_mask,
    weights, biases, norm_gain, norm_shift, output_grad,
):
    nodes, cols = features.shape
    fan = neighbour_ids.shape[1]
    n, cap = send_rows.shape[1], send_rows.shape[2]
    halo = n * cap
    lookup = nodes + halo
    line = n // 4
    aux = jnp.concatenate(
        [
            neighbour_ids.astype(F32),
            lax.broadcasted_iota(jnp.int32, (nodes, 1), 0).astype(F32),
            edge_weight,
            2.0 * self_weight[:, None],
            valid_mask.astype(F32)[:, None],
        ],
        axis=1,
    )
    rows = send_rows.reshape(halo, 1)
    params = jnp.concatenate([biases, norm_gain, norm_shift], axis=0)
    vm = pl.BlockSpec(memory_space=pltpu.VMEM)
    anyspace = pl.BlockSpec(memory_space=pl.ANY)
    dma = pltpu.SemaphoreType.DMA
    out, ig, wg, small = pl.pallas_call(
        functools.partial(chain, n, cap, fan),
        out_shape=(
            jax.ShapeDtypeStruct((nodes, cols), BF),
            jax.ShapeDtypeStruct((nodes, cols), BF),
            jax.ShapeDtypeStruct((2, 2 * cols, cols), BF),
            jax.ShapeDtypeStruct((8, cols), F32),
        ),
        in_specs=[vm, vm, vm, vm, anyspace, anyspace],
        out_specs=(anyspace, anyspace, anyspace, vm),
        scratch_shapes=[
            pltpu.VMEM((2, 2 * cols, cols), BF),
            pltpu.VMEM((nodes, cols), BF),
            pltpu.VMEM((nodes, lookup), BF),
            pltpu.VMEM((lookup, nodes), BF),
            pltpu.VMEM((halo, nodes), BF),
            pltpu.VMEM((nodes, halo), BF),
            pltpu.VMEM((nodes, cols), BF),
            pltpu.VMEM((2, 2, nodes, cols), BF),
            pltpu.VMEM((2, nodes, cols), F32),
            pltpu.VMEM((2, nodes, cols), BF),
            pltpu.VMEM((nodes, cols), F32),
            pltpu.VMEM((2, nodes, cols), BF),
            pltpu.VMEM((2 * halo, cols // 2), BF),
            pltpu.VMEM((2 * halo, cols // 2), BF),
            pltpu.VMEM((16, cols), F32),
            pltpu.VMEM((n, 3, 8, cols // 8), F32),
            pltpu.VMEM((n, 4, 8, cols // 8), F32),
            pltpu.VMEM((n, 3, 8, cols // 8), F32),
            pltpu.VMEM((n, 1, 8, cols // 8), F32),
            pltpu.VMEM((2, 2 * cols, nodes), BF),
            pltpu.VMEM((2, 3, cols, nodes), BF),
            pltpu.VMEM((2, 3, 2, nodes, cols // 4), BF),
            pltpu.VMEM((2, 2, cols, cols // 4), BF),
            pltpu.VMEM((2, 2, line, cols // line, cols // 4), BF),
            pltpu.VMEM((2, 2, cols // line, cols // 4), BF),
            dma((2,)), dma, dma((2,)), dma((6,)), dma((6,)),
            dma((n,)), dma((n,)), dma((4, n)), dma((4, n)),
            dma((2, 2, 3)), dma((2, 2, 3)), dma((2, 2, 3, 2)),
            *[dma((2, 2, 2, line)) for _ in range(5)], dma((2, 2)),
        ],
        compiler_params=pltpu.CompilerParams(
            collective_id=0, has_side_effects=True, vmem_limit_bytes=62 * 2**20
        ),
    )(features, aux, rows, params, output_grad, weights)
    return out, ig, wg.astype(F32), jnp.stack([small[0], small[5]]), small[1:3], small[3:5]


def solution(mesh):
    return jax.shard_map(
        per_device,
        mesh=mesh,
        in_specs=(
            P("cluster", "mp"),
            P("cluster", None),
            P("cluster", None),
            P("cluster"),
            P("cluster", None, None),
            P("cluster"),
            P(None, None, "mp"),
            P(None, "mp"),
            P(None, "mp"),
            P(None, "mp"),
            P("cluster", "mp"),
        ),
        out_specs=(
            P("cluster", "mp"),
            P("cluster", "mp"),
            P(None, None, "mp"),
            P(None, "mp"),
            P(None, "mp"),
            P(None, "mp"),
        ),
        check_vma=False,
    )
```

```python
import functools

import jax
import jax.numpy as jnp
from jax import lax
from jax.experimental import pallas as pl
from jax.experimental.pallas import tpu as pltpu
from jax.sharding import PartitionSpec as P

EPS = 1e-05
MESH = pl.DeviceIdType.MESH
BF = jnp.bfloat16
F32 = jnp.float32


def mm(a, b):
    return jnp.dot(a, b, preferred_element_type=F32)


def mm_t(a, b):
    return lax.dot_general(a, b, (((1,), (1,)), ((), ())), preferred_element_type=F32)


def chain(
    n, cap, fan,
    f_ref, aux_ref, rows_ref, par_ref, og_hbm, w_hbm,
    out_hbm, ig_hbm, wg_hbm, small_ref,
    w_ref, og_ref, adj, adj_t, sel, sel_t, h1_ref, yf, s_ref, d_ref, zacc,
    dy_recv, hsend, hrecv, st_row, stat0, stat1, stat2, stat3,
    yt, yr, dzr, wpart, zr, fin,
    w_sem, og_sem, out_sem, mp_ssem, mp_rsem, h_ssem, h_rsem, x_ssem, x_rsem,
    y_sem, yp_sem, dz_sem, zr_sem, az_sem, ag_sem, fin_sem,
):
    nodes, cols = f_ref.shape
    ct = 256
    tiles = cols // ct
    half = cols // 2
    c = lax.axis_index("cluster")
    m = lax.axis_index("mp")
    peer = (c, 1 - m)
    halo = n * cap
    lookup = nodes + halo
    line = n // 4
    zi, p = c // 4, c % 4
    px, py = p % 2, p // 2
    near = (c + 1 - 2 * px, c + 2 - 4 * py, c + 3 - 2 * px - 4 * py)
    rc = cols // line
    dy_own, dyb, g_ref = zacc, og_ref, s_ref.at[1]
    out_ref, dy_send, dz_ref = yf.at[0, 0], yf.at[0, 1], yf.at[1]

    def quarter(layer, who):
        qx = 1 - px if who in (0, 2) else px
        qy = 1 - py if who in (1, 2) else py
        return (qx, qy) if layer == 1 else (qy, qx)

    barrier = pltpu.get_barrier_semaphore()

    def greet(i, _):
        pl.semaphore_signal(
            barrier, inc=1, device_id=(lax.rem(c + i, n), m), device_id_type=MESH
        )
        return 0

    lax.fori_loop(1, n, greet, 0)
    pl.semaphore_signal(barrier, inc=1, device_id=peer, device_id_type=MESH)

    w_copies = [
        pltpu.make_async_copy(w_hbm.at[layer], w_ref.at[layer], w_sem.at[layer])
        for layer in range(2)
    ]
    w_copies[0].start()
    og_copy = pltpu.make_async_copy(og_hbm, og_ref, og_sem)
    og_copy.start()
    w_copies[1].start()

    sel_f = jnp.where(
        rows_ref[...] == lax.broadcasted_iota(jnp.int32, (halo, nodes), 1), 1.0, 0.0
    )
    sel[...] = sel_f.astype(BF)

    def col(j):
        return pl.ds(pl.multiple_of(j * ct, ct), ct)

    def pack_halo(left, right):
        both = jnp.concatenate(
            [left.reshape(n, cap, half), right.reshape(n, cap, half)], axis=1
        )
        hsend[...] = both.reshape(n * 2 * cap, half).astype(BF)

    def halo_part(d):
        return pl.ds(pl.multiple_of(d * 2 * cap, 2 * cap), 2 * cap)

    def halo_start():
        def send(i, _):
            d = lax.rem(c + i, n)
            pltpu.make_async_remote_copy(
                src_ref=hsend.at[halo_part(d)],
                dst_ref=hrecv.at[halo_part(c)],
                send_sem=h_ssem.at[d],
                recv_sem=h_rsem.at[c],
                device_id=(d, m),
                device_id_type=MESH,
            ).start()
            return 0

        lax.fori_loop(1, n, send, 0)
        hrecv[halo_part(c)] = hsend[halo_part(c)]

    def halo_finish():
        def finish(i, _):
            s = lax.rem(c + i, n)
            copy = pltpu.make_async_remote_copy(
                src_ref=hsend.at[halo_part(s)],
                dst_ref=hrecv.at[halo_part(s)],
                send_sem=h_ssem.at[s],
                recv_sem=h_rsem.at[s],
                device_id=(s, m),
                device_id_type=MESH,
            )
            copy.wait_recv()
            copy.wait_send()
            return 0

        lax.fori_loop(1, n, finish, 0)

    def halo_read():
        got = hrecv[...].astype(F32).reshape(n, 2 * cap, half)
        left = got[:, :cap, :].reshape(halo, half).astype(BF)
        right = got[:, cap:, :].reshape(halo, half).astype(BF)
        return left, right

    def stat_start(e, buf):
        def send(i, _):
            d = lax.rem(c + i, n)
            pltpu.make_async_remote_copy(
                src_ref=buf.at[c],
                dst_ref=buf.at[c],
                send_sem=x_ssem.at[e, d],
                recv_sem=x_rsem.at[e, c],
                device_id=(d, m),
                device_id_type=MESH,
            ).start()
            return 0

        lax.fori_loop(1, n, send, 0)

    def stat_finish(e, buf):
        def finish(i, _):
            s = lax.rem(c + i, n)
            copy = pltpu.make_async_remote_copy(
                src_ref=buf.at[c],
                dst_ref=buf.at[s],
                send_sem=x_ssem.at[e, s],
                recv_sem=x_rsem.at[e, s],
                device_id=(s, m),
                device_id_type=MESH,
            )
            copy.wait_recv()
            copy.wait_send()
            return 0

        lax.fori_loop(1, n, finish, 0)

    lanes = cols // 8

    def fold(buf, k, row):
        for g in range(8):
            buf[c, k, g : g + 1, :] = st_row[row : row + 1, g * lanes : (g + 1) * lanes]

    def unfold(tile, row):
        for g in range(8):
            st_row[row : row + 1, g * lanes : (g + 1) * lanes] = tile[g : g + 1, :]

    def total(buf, k):
        return lax.fori_loop(
            1, n, lambda s, t: t + buf[s, k], buf[0, k]
        )

    def mp_copy(k, src, dst):
        return pltpu.make_async_remote_copy(
            src_ref=src,
            dst_ref=dst,
            send_sem=mp_ssem.at[k],
            recv_sem=mp_rsem.at[k],
            device_id=peer,
            device_id_type=MESH,
        )

    def remote(src, dst, sems, idx, to):
        return pltpu.make_async_remote_copy(
            src_ref=src,
            dst_ref=dst,
            send_sem=sems.at[(0, *idx)],
            recv_sem=sems.at[(1, *idx)],
            device_id=to,
            device_id_type=MESH,
        )

    def rows_of(start, size):
        return pl.ds(pl.multiple_of(start, size), size)

    pieces = 4
    prow = half // pieces

    def y_flip(layer):
        def flip(i, _):
            r = pl.ds(pl.multiple_of(i * 128, 128), 128)
            for h in range(2):
                d = pl.ds(pl.multiple_of(h * cols + i * 128, 128), 128)
                yt[layer, d, :] = yf[layer, h, :, r].astype(F32).T.astype(BF)
            return 0

        lax.fori_loop(0, cols // 128, flip, 0)

    def y_piece(layer, who, k):
        hr, _ = quarter(layer, who)
        return remote(
            yt.at[layer, rows_of(hr * cols + m * half + k * prow, prow), :],
            yr.at[layer, who, rows_of(m * half + k * prow, prow), :],
            y_sem, (layer, who, k), (near[who], m),
        )

    def y_first(layer):
        return 1 - layer

    def z_first(layer):
        return layer

    def y_relay(layer, k):
        first = y_first(layer)
        r = rows_of(m * half + k * prow, prow)
        return remote(
            yr.at[layer, first, r, :], yr.at[layer, 2, r, :], y_sem, (layer, 2, k),
            (near[1 - first], m),
        )

    def y_send(layer, who, *ks):
        for k in ks:
            y_piece(layer, who, k).start()

    def y_forward(layer, *ks):
        for k in ks:
            y_piece(layer, y_first(layer), k).wait_recv()
            y_relay(layer, k).start()

    def y_pass_copy(layer, who, part):
        r = rows_of(part * half, half)
        return remote(
            yr.at[layer, who, r, :], yr.at[layer, who, r, :], yp_sem, (layer, who), peer
        )

    def y_pass(layer, who):
        if who != y_first(layer):
            for k in range(pieces):
                copy = y_relay(layer, k) if who == 2 else y_piece(layer, who, k)
                copy.wait_recv()
        y_pass_copy(layer, who, m).start()

    def y_finish(layer):
        for who in range(3):
            y_pass_copy(layer, who, 1 - m).wait_recv()

    def y_sent(layer):
        for k in range(pieces):
            y_piece(layer, 0, k).wait_send()
            y_piece(layer, 1, k).wait_send()
            y_relay(layer, k).wait_send()
        for who in range(3):
            y_pass_copy(layer, who, m).wait_send()

    def dz_piece(layer, who, sb):
        _, hc = quarter(layer, who)
        return remote(
            dz_ref.at[layer, :, rows_of(hc * half + sb * ct, ct)],
            dzr.at[layer, who, sb],
            dz_sem, (layer, who, sb), (near[who], m),
        )

    def dz_relay(layer, sb):
        first = z_first(layer)
        return remote(
            dzr.at[layer, first, sb], dzr.at[layer, 2, sb], dz_sem, (layer, 2, sb),
            (near[1 - first], m),
        )

    def dz_forward(layer, sb):
        dz_piece(layer, z_first(layer), sb).wait_recv()
        dz_relay(layer, sb).start()

    def dz_sent(layer):
        for sb in range(2):
            dz_piece(layer, 0, sb).wait_send()
            dz_piece(layer, 1, sb).wait_send()
            dz_relay(layer, sb).wait_send()

    def line_copy(layer, sb, far, mine):
        return pltpu.make_async_remote_copy(
            src_ref=wpart.at[layer, sb, rows_of(far * rc, rc), :],
            dst_ref=zr.at[layer, sb, mine],
            send_sem=zr_sem.at[0, layer, sb, far],
            recv_sem=zr_sem.at[1, layer, sb, mine],
            device_id=(far * 4 + p, m),
            device_id_type=MESH,
        )

    def product(layer, sb):
        hr, hc = quarter(layer, 3)
        dz_piece(layer, 1 - z_first(layer), sb).wait_recv()
        dz_relay(layer, sb).wait_recv()
        mine_dz = dz_ref[layer, :, rows_of(hc * half + sb * ct, ct)]

        def one(i, _):
            r = pl.ds(pl.multiple_of(i * ct, ct), ct)
            acc = mm(yt[layer, pl.ds(pl.multiple_of(hr * cols + i * ct, ct), ct), :], mine_dz)
            for who in range(3):
                acc = acc + mm(yr[layer, who, r, :], dzr[layer, who, sb])
            wpart[layer, sb, r, :] = acc.astype(BF)
            return 0

        lax.fori_loop(0, cols // ct, one, 0)

        def send(i, _):
            line_copy(layer, sb, (zi + i) % line, zi).start()
            return 0

        lax.fori_loop(1, line, send, 0)

    far = n // 8

    def flip_bit(e, d):
        return e + d - 2 * d * ((e // d) % 2)

    def spot(layer, sb, e):
        ex, ey = e % 2, (e // 2) % 2
        hr, hc = (ex, ey) if layer == 1 else (ey, ex)
        return wg_hbm.at[
            layer, rows_of(hr * cols + (e // 4) * rc, rc), rows_of(hc * half + sb * ct, ct)
        ]

    X, Y, Z = 1, 2, 4
    orders = {
        (1, 0, 0): (Y, Z, X), (1, 0, 1): (Z, X, Y), (1, 1, 0): (X, Y, Z), (1, 1, 1): (Z, Y, X),
        (0, 0, 0): (X, Z, Y), (0, 0, 1): (Z, Y, X), (0, 1, 0): (Y, X, Z), (0, 1, 1): (Z, X, Y),
    }

    def held(base, dims):
        got = [base]
        for d in dims:
            got = got + [flip_bit(e, d) for e in got]
        return got

    def far_copy(layer, sb, to, frm):
        return pltpu.make_async_remote_copy(
            src_ref=fin.at[layer, sb],
            dst_ref=spot(layer, sb, frm),
            send_sem=az_sem.at[0, layer, sb, to // 8],
            recv_sem=az_sem.at[1, layer, sb, frm // 8],
            device_id=(to, m),
            device_id_type=MESH,
        )

    def hops(layer, sb, i, step):
        dims = orders[(layer, sb, 0 if isinstance(i, int) else 1)]
        base = (c + 8 * i) % n
        to = flip_bit(c, dims[step])
        slot = 2**step - 1
        return [
            remote(
                fin.at[layer, sb] if isinstance(i, int) and j == 0 else spot(layer, sb, e),
                spot(layer, sb, e), ag_sem, (layer, sb, base // 8, slot + j), (to, m),
            )
            for j, e in enumerate(held(base, dims[:step]))
        ]

    def landings(layer, sb, i, step):
        dims = orders[(layer, sb, 0 if isinstance(i, int) else 1)]
        base = (c + 8 * i) % n
        frm = flip_bit(c, dims[step])
        slot = 2**step - 1
        return [
            remote(
                spot(layer, sb, flip_bit(e, dims[step])), spot(layer, sb, flip_bit(e, dims[step])),
                ag_sem, (layer, sb, base // 8, slot + j), (frm, m),
            )
            for j, e in enumerate(held(base, dims[:step]))
        ]

    def combine(layer, sb):
        def take(i, _):
            frm = (zi + i) % line
            copy = line_copy(layer, sb, frm, frm)
            copy.wait_recv()
            copy.wait_send()
            return 0

        lax.fori_loop(1, line, take, 0)
        zr[layer, sb, zi] = wpart[layer, sb, rows_of(zi * rc, rc), :]
        fin[layer, sb] = lax.fori_loop(
            1, line,
            lambda j, t: t + zr[layer, sb, j].astype(F32),
            zr[layer, sb, 0].astype(F32),
        ).astype(BF)
        keep(layer, sb).start()

        def send(i, _):
            far_copy(layer, sb, (c + 8 * i) % n, c).start()
            return 0

        lax.fori_loop(1, far, send, 0)
        gather_own(layer, sb, 0)

    def keep(layer, sb):
        return pltpu.make_async_copy(
            fin.at[layer, sb], spot(layer, sb, c), fin_sem.at[layer, sb]
        )

    def gather_own(layer, sb, step):
        if step > 0:
            for copy in landings(layer, sb, 0, step - 1):
                copy.wait_recv()
        for copy in hops(layer, sb, 0, step):
            copy.start()

    def gather_far(layer, sb, step):
        def one(i, _):
            if step == 0:
                frm = (c + 8 * i) % n
                far_copy(layer, sb, frm, frm).wait_recv()
            else:
                for copy in landings(layer, sb, i, step - 1):
                    copy.wait_recv()
            for copy in hops(layer, sb, i, step):
                copy.start()
            return 0

        lax.fori_loop(1, far, one, 0)

    def gather_finish(layer, sb):
        keep(layer, sb).wait()

        def ends(i):
            for copy in landings(layer, sb, i, 2):
                copy.wait_recv()
            for step in range(3):
                for copy in hops(layer, sb, i, step):
                    copy.wait_send()

        def one(i, _):
            far_copy(layer, sb, (c + 8 * i) % n, c).wait_send()
            ends(i)
            return 0

        ends(0)
        lax.fori_loop(1, far, one, 0)

    mask = aux_ref[:, 2 * fan + 2 : 2 * fan + 3]
    own_count = jnp.sum(mask, axis=0, keepdims=True)
    own_inv = 1.0 / jnp.maximum(own_count, 1.0)

    def pick(src):
        pack_halo(mm(sel[...], src[:, :half]), mm(sel[...], src[:, half:]))

    pick(f_ref)
    pl.semaphore_wait(barrier, n)
    halo_start()

    rb = 16
    slots = lax.broadcasted_iota(jnp.int32, (rb, lookup), 1).astype(F32)

    def build(i, _):
        r = pl.ds(pl.multiple_of(i * rb, rb), rb)
        part = aux_ref[r, :]
        a = jnp.zeros((rb, lookup), F32)
        for k in range(fan + 1):
            a = a + jnp.where(
                part[:, k : k + 1] == slots, part[:, fan + 1 + k : fan + 2 + k], 0.0
            )
        adj[r, :] = a.astype(BF)
        return 0

    lax.fori_loop(0, nodes // rb, build, 0)

    def turn(i, _):
        r = pl.ds(pl.multiple_of(i * 128, 128), 128)
        adj_t[r, :] = adj[:, r].astype(F32).T.astype(BF)
        return 0

    def turn_sel(i, _):
        r = pl.ds(pl.multiple_of(i * 128, 128), 128)
        sel_t[:, r] = sel[r, :].astype(F32).T.astype(BF)
        return 0

    stats = []
    gain_rows, shift_rows = [], []
    for layer in range(2):
        src = f_ref if layer == 0 else h1_ref
        for h in range(2):
            cs = slice(h * half, (h + 1) * half)
            zacc[:, cs] = mm(adj[:, :nodes], src[:, cs])
        if layer == 0:
            lax.fori_loop(0, lookup // 128, turn, 0)
            lax.fori_loop(0, halo // 128, turn_sel, 0)
        halo_finish()
        parts = halo_read()
        y_copy = []
        for h in range(2):
            cs = slice(h * half, (h + 1) * half)
            yf[layer, m, :, cs] = (zacc[:, cs] + mm(adj[:, nodes:], parts[h])).astype(BF)
            copy = mp_copy(
                layer * 2 + h, yf.at[layer, m, :, cs], yf.at[layer, m, :, cs]
            )
            copy.start()
            y_copy.append(copy)
        w_copies[layer].wait()

        def first(j, _):
            zacc[:, col(j)] = mm(
                yf[layer, m],
                w_ref[layer, pl.ds(pl.multiple_of(m * cols, cols), cols), col(j)],
            )
            return 0

        lax.fori_loop(0, tiles, first, 0)
        for copy in y_copy:
            copy.wait_recv()
        if layer == 1:
            og_copy.wait()

        def second(j, _):
            z = zacc[:, col(j)] + mm(
                yf[layer, 1 - m],
                w_ref[layer, pl.ds(pl.multiple_of((1 - m) * cols, cols), cols), col(j)],
            )
            z = z + par_ref[layer : layer + 1, col(j)]
            sig = jax.nn.sigmoid(z)
            s = z * sig
            s_ref[layer, :, col(j)] = s
            d_ref[layer, :, col(j)] = (sig * (1.0 + z * (1.0 - sig))).astype(BF)
            tot = jnp.sum(s * mask, axis=0, keepdims=True)
            cen = s - tot * own_inv
            st_row[0:1, col(j)] = tot
            st_row[1:2, col(j)] = jnp.sum(cen * cen * mask, axis=0, keepdims=True)
            if layer == 0:
                st_row[2:3, col(j)] = jnp.broadcast_to(own_count, (1, ct))
            else:
                pg = og_ref[:, col(j)].astype(F32) * mask
                st_row[2:3, col(j)] = jnp.sum(pg, axis=0, keepdims=True)
                st_row[3:4, col(j)] = jnp.sum(pg * cen, axis=0, keepdims=True)
            return 0

        lax.fori_loop(0, tiles, second, 0)
        buf = stat0 if layer == 0 else stat1
        for k in range(3 if layer == 0 else 4):
            fold(buf, k, k)
        stat_start(layer, buf)
        for copy in y_copy:
            copy.wait_send()
        y_flip(layer)
        if layer == 0:
            y_send(0, 0, 0, 1)
            y_send(0, 1, 0, 1)
        else:
            y_forward(0, 2, 3)
            y_send(1, 1, 0, 1)
        stat_finish(layer, buf)
        count = jnp.maximum(total(stat0, 2), 1.0)
        mu = total(buf, 0) / count

        def spread(s, t):
            nc = stat0[s, 2]
            off = buf[s, 0] / jnp.maximum(nc, 1.0) - mu
            return t + buf[s, 1] + nc * off * off

        var = lax.fori_loop(0, n, spread, jnp.zeros_like(mu)) / count
        inv = lax.rsqrt(var + EPS)
        unfold(mu, 4)
        unfold(inv, 5)
        stats.append((mu, inv, count))
        mu_row, inv_row = st_row[4:5, :], st_row[5:6, :]
        gain_row = par_ref[2 + layer : 3 + layer, :]
        shift_row = par_ref[4 + layer : 5 + layer, :]
        dst = h1_ref if layer == 0 else out_ref
        if layer == 0:
            unfold(mu, 8)
            unfold(inv, 9)
        for j in range(tiles):
            cs = slice(j * ct, (j + 1) * ct)
            x = (s_ref[layer, :, cs] - mu_row[:, cs]) * inv_row[:, cs]
            dst[:, cs] = (mask * (gain_row[:, cs] * x + shift_row[:, cs])).astype(BF)
        if layer == 0:
            pick(h1_ref)
            halo_start()
            y_send(0, 0, 2, 3)
            y_send(0, 1, 2, 3)
            y_forward(0, 0, 1)
    out_copy = pltpu.make_async_copy(out_ref, out_hbm, out_sem.at[0])
    out_copy.start()

    mu, inv, count = stats[1]

    def gains(s, t):
        off = stat1[s, 0] / jnp.maximum(stat0[s, 2], 1.0) - mu
        return t + stat1[s, 3] + off * stat1[s, 2]

    gg = inv * lax.fori_loop(0, n, gains, jnp.zeros_like(mu))
    sg = total(stat1, 2)
    unfold(sg, 6)
    unfold(gg, 7)
    small_ref[2:3, :] = st_row[7:8, :]
    small_ref[4:5, :] = st_row[6:7, :]
    inv_count = 1.0 / count
    unfold(inv_count, 10)
    for layer in (1, 0):
        if layer == 1:
            mu_r, inv_r = 4, 5
        else:
            mu_r, inv_r = 8, 9
        grad_src = og_ref if layer == 1 else g_ref

        def pre(j, _):
            gain = par_ref[2 + layer : 3 + layer, col(j)]
            inv_row = st_row[inv_r : inv_r + 1, col(j)]
            ic = st_row[10:11, col(j)]
            x = (s_ref[layer, :, col(j)] - st_row[mu_r : mu_r + 1, col(j)]) * inv_row
            pg = grad_src[:, col(j)].astype(F32) * mask
            ds = (
                mask
                * (inv_row * gain)
                * (
                    pg
                    - st_row[6:7, col(j)] * ic
                    - x * (st_row[7:8, col(j)] * ic)
                )
            )
            dz = (ds * d_ref[layer, :, col(j)].astype(F32)).astype(BF)
            dz_ref[layer, :, col(j)] = dz
            st_row[11:12, col(j)] = jnp.sum(dz.astype(F32), axis=0, keepdims=True)
            return 0

        lax.fori_loop(0, tiles, pre, 0)
        if layer == 1:
            dz_piece(1, 0, 0).start()
            y_send(1, 1, 2, 3)
        else:
            y_send(1, 0, 2, 3)
            y_forward(1, 0, 1)

        if layer == 1:
            fold(stat2, 2, 11)
        else:
            fold(stat3, 0, 11)
            stat_start(3, stat3)

        def other(j, _):
            r = pl.ds(pl.multiple_of((1 - m) * cols + j * ct, ct), ct)
            dy_send[:, col(j)] = mm_t(dz_ref[layer], w_ref[layer, r, :]).astype(BF)
            return 0

        lax.fori_loop(0, tiles, other, 0)
        dy_copy = mp_copy(4 + layer, dy_send, dy_recv.at[layer])
        dy_copy.start()

        def mine(j, _):
            r = pl.ds(pl.multiple_of(m * cols + j * ct, ct), ct)
            dy_own[:, col(j)] = mm_t(dz_ref[layer], w_ref[layer, r, :])
            return 0

        lax.fori_loop(0, tiles, mine, 0)
        dy_copy.wait_recv()
        for j in range(tiles):
            cs = slice(j * ct, (j + 1) * ct)
            dyb[:, cs] = (dy_own[:, cs] + dy_recv[layer, :, cs].astype(F32)).astype(BF)
        pack_halo(mm(adj_t[nodes:, :], dyb[:, :half]), mm(adj_t[nodes:, :], dyb[:, half:]))
        halo_start()
        if layer == 1:
            y_send(1, 0, 0, 1)
            dz_piece(1, 1, 0).start()
        else:
            dz_forward(1, 0)
            dz_forward(1, 1)
            for sb in range(2):
                dz_piece(0, 0, sb).start()
                dz_piece(0, 1, sb).start()
        for h in range(2):
            cs = slice(h * half, (h + 1) * half)
            g_ref[:, cs] = mm(adj_t[:nodes, :], dyb[:, cs])
        dy_copy.wait_send()
        if layer == 0:
            y_forward(1, 2, 3)
            y_pass(1, 0)
            y_pass(1, 1)
        halo_finish()
        parts = halo_read()
        for h in range(2):
            cs = slice(h * half, (h + 1) * half)
            got = g_ref[:, cs] + mm(sel_t[...], parts[h])
            if layer == 1:
                g_ref[:, cs] = got
                pg = got * mask
                x = (s_ref[0, :, cs] - st_row[8:9, cs]) * st_row[9:10, cs]
                st_row[0:1, cs] = jnp.sum(pg, axis=0, keepdims=True)
                st_row[1:2, cs] = jnp.sum(pg * x, axis=0, keepdims=True)
            else:
                h1_ref[:, cs] = got.astype(BF)
        if layer == 1:
            fold(stat2, 0, 0)
            fold(stat2, 1, 1)
            stat_start(2, stat2)
            dz_piece(1, 0, 1).start()
            dz_piece(1, 1, 1).start()
            for who in range(3):
                y_pass(0, who)
            stat_finish(2, stat2)
            unfold(total(stat2, 0), 6)
            unfold(total(stat2, 1), 7)
            unfold(total(stat2, 2), 12)
            small_ref[1:2, :] = st_row[7:8, :]
            small_ref[3:4, :] = st_row[6:7, :]
            small_ref[5:6, :] = st_row[12:13, :]
    ig_copy = pltpu.make_async_copy(h1_ref, ig_hbm, out_sem.at[1])
    ig_copy.start()
    y_pass(1, 2)
    y_finish(1)
    for sb in range(2):
        product(1, sb)
    for sb in range(2):
        dz_forward(0, sb)
    for sb in range(2):
        combine(1, sb)
    y_finish(0)
    for sb in range(2):
        product(0, sb)
    for sb in range(2):
        gather_far(1, sb, 0)
        gather_own(1, sb, 1)
    for sb in range(2):
        gather_own(1, sb, 2)
        gather_far(1, sb, 1)
    for sb in range(2):
        combine(0, sb)
    for sb in range(2):
        gather_far(1, sb, 2)
    for step in range(3):
        for sb in range(2):
            gather_far(0, sb, step)
            if step < 2:
                gather_own(0, sb, step + 1)
    stat_finish(3, stat3)
    unfold(total(stat3, 0), 12)
    small_ref[0:1, :] = st_row[12:13, :]
    small_ref[6:8, :] = jnp.zeros((2, cols), F32)
    out_copy.wait()
    ig_copy.wait()
    for layer in (1, 0):
        y_sent(layer)
        dz_sent(layer)
        for sb in range(2):
            gather_finish(layer, sb)


def per_device(
    features, neighbour_ids, edge_weight, self_weight, send_rows, valid_mask,
    weights, biases, norm_gain, norm_shift, output_grad,
):
    nodes, cols = features.shape
    fan = neighbour_ids.shape[1]
    n, cap = send_rows.shape[1], send_rows.shape[2]
    halo = n * cap
    lookup = nodes + halo
    line = n // 4
    aux = jnp.concatenate(
        [
            neighbour_ids.astype(F32),
            lax.broadcasted_iota(jnp.int32, (nodes, 1), 0).astype(F32),
            edge_weight,
            2.0 * self_weight[:, None],
            valid_mask.astype(F32)[:, None],
        ],
        axis=1,
    )
    rows = send_rows.reshape(halo, 1)
    params = jnp.concatenate([biases, norm_gain, norm_shift], axis=0)
    vm = pl.BlockSpec(memory_space=pltpu.VMEM)
    anyspace = pl.BlockSpec(memory_space=pl.ANY)
    dma = pltpu.SemaphoreType.DMA
    out, ig, wg, small = pl.pallas_call(
        functools.partial(chain, n, cap, fan),
        out_shape=(
            jax.ShapeDtypeStruct((nodes, cols), BF),
            jax.ShapeDtypeStruct((nodes, cols), BF),
            jax.ShapeDtypeStruct((2, 2 * cols, cols), BF),
            jax.ShapeDtypeStruct((8, cols), F32),
        ),
        in_specs=[vm, vm, vm, vm, anyspace, anyspace],
        out_specs=(anyspace, anyspace, anyspace, vm),
        scratch_shapes=[
            pltpu.VMEM((2, 2 * cols, cols), BF),
            pltpu.VMEM((nodes, cols), BF),
            pltpu.VMEM((nodes, lookup), BF),
            pltpu.VMEM((lookup, nodes), BF),
            pltpu.VMEM((halo, nodes), BF),
            pltpu.VMEM((nodes, halo), BF),
            pltpu.VMEM((nodes, cols), BF),
            pltpu.VMEM((2, 2, nodes, cols), BF),
            pltpu.VMEM((2, nodes, cols), F32),
            pltpu.VMEM((2, nodes, cols), BF),
            pltpu.VMEM((nodes, cols), F32),
            pltpu.VMEM((2, nodes, cols), BF),
            pltpu.VMEM((2 * halo, cols // 2), BF),
            pltpu.VMEM((2 * halo, cols // 2), BF),
            pltpu.VMEM((16, cols), F32),
            pltpu.VMEM((n, 3, 8, cols // 8), F32),
            pltpu.VMEM((n, 4, 8, cols // 8), F32),
            pltpu.VMEM((n, 3, 8, cols // 8), F32),
            pltpu.VMEM((n, 1, 8, cols // 8), F32),
            pltpu.VMEM((2, 2 * cols, nodes), BF),
            pltpu.VMEM((2, 3, cols, nodes), BF),
            pltpu.VMEM((2, 3, 2, nodes, cols // 4), BF),
            pltpu.VMEM((2, 2, cols, cols // 4), BF),
            pltpu.VMEM((2, 2, line, cols // line, cols // 4), BF),
            pltpu.VMEM((2, 2, cols // line, cols // 4), BF),
            dma((2,)), dma, dma((2,)), dma((6,)), dma((6,)),
            dma((n,)), dma((n,)), dma((4, n)), dma((4, n)),
            dma((2, 2, 3, 4)), dma((2, 2, 3)), dma((2, 2, 3, 2)),
            dma((2, 2, 2, line)), dma((2, 2, 2, n // 8)), dma((2, 2, 2, n // 8, 7)), dma((2, 2)),
        ],
        compiler_params=pltpu.CompilerParams(
            collective_id=0, has_side_effects=True, vmem_limit_bytes=62 * 2**20
        ),
    )(features, aux, rows, params, output_grad, weights)
    return out, ig, wg.astype(F32), jnp.stack([small[0], small[5]]), small[1:3], small[3:5]


def solution(mesh):
    return jax.shard_map(
        per_device,
        mesh=mesh,
        in_specs=(
            P("cluster", "mp"),
            P("cluster", None),
            P("cluster", None),
            P("cluster"),
            P("cluster", None, None),
            P("cluster"),
            P(None, None, "mp"),
            P(None, "mp"),
            P(None, "mp"),
            P(None, "mp"),
            P("cluster", "mp"),
        ),
        out_specs=(
            P("cluster", "mp"),
            P("cluster", "mp"),
            P(None, None, "mp"),
            P(None, "mp"),
            P(None, "mp"),
            P(None, "mp"),
        ),
        check_vma=False,
    )
```

```python
import functools

import jax
import jax.numpy as jnp
from jax import lax
from jax.experimental import pallas as pl
from jax.experimental.pallas import tpu as pltpu
from jax.sharding import PartitionSpec as P

EPS = 1e-05
MESH = pl.DeviceIdType.MESH
BF = jnp.bfloat16
F32 = jnp.float32

SCHEDULE = (
    ("A0",),
    ("A",), ("ys", 0, 1, 0),
    ("B0",),
    ("B",), ("ys", 0, 1, 2), ("ys", 0, 0, 2), ("ys", 0, 0, 0),
    ("B1",), ("ys", 0, 0, 1),
    ("B2",),
    ("C",), ("ys", 1, 1, 2), ("ys", 1, 0, 0), ("ys", 1, 1, 0), ("ys", 1, 1, 3), ("ys", 1, 0, 2), ("ys", 0, 0, 3),
    ("ys", 1, 0, 1),
    ("C2",), ("ds", 1, 1, 1),
    ("C3",), ("yf", 1, 1), ("ys", 1, 0, 3),
    ("D",), ("ys", 1, 1, 1), ("yf", 1, 2), ("yf", 1, 0), ("df", 1, 1), ("ds", 1, 0, 1), ("yf", 1, 3),
    ("E",), ("yp", 1, 1), ("yp", 1, 0), ("ds", 1, 1, 0), ("ds", 1, 0, 0), ("yp", 0, 0), ("yp", 1, 2), ("pr", 1, 1),
    ("E2",), ("pr", 1, 3), ("ys", 0, 1, 1), ("df", 1, 0), ("ys", 0, 1, 3), ("cb", 1, 1), ("ds", 0, 0, 0),
    ("pr", 1, 0), ("yf", 0, 1), ("ds", 0, 1, 0), ("ds", 0, 1, 1), ("gf", 1, 1, 0), ("yf", 0, 2), ("pr", 1, 2),
    ("yf", 0, 3),
    ("E3",), ("df", 0, 0), ("yf", 0, 0), ("ds", 0, 0, 1), ("go", 1, 1, 1), ("cb", 1, 0), ("cb", 1, 3), ("yp", 0, 2),
    ("cb", 1, 2),
    ("F",), ("gf", 1, 1, 1), ("go", 1, 0, 1),
    ("G",), ("yp", 0, 1), ("gf", 1, 2, 0), ("go", 1, 1, 2), ("gf", 1, 3, 0), ("go", 1, 3, 1), ("gf", 1, 0, 0),
    ("pr", 0, 2), ("go", 1, 2, 1), ("pr", 0, 0), ("gf", 1, 0, 1), ("df", 0, 1), ("go", 1, 0, 2), ("go", 1, 2, 2),
    ("gf", 1, 2, 1), ("cb", 0, 2), ("gf", 1, 1, 2), ("cb", 0, 0), ("go", 1, 3, 2), ("gf", 1, 0, 2), ("pr", 0, 1),
    ("gf", 1, 3, 1), ("go", 0, 2, 1), ("gf", 0, 0, 0), ("gf", 0, 2, 0), ("pr", 0, 3), ("gf", 0, 2, 1), ("cb", 0, 1),
    ("IG",), ("gf", 1, 2, 2), ("cb", 0, 3), ("gf", 0, 1, 0), ("go", 0, 1, 1), ("go", 0, 0, 1), ("gf", 1, 3, 2),
    ("go", 0, 3, 1), ("gf", 0, 0, 1), ("gf", 0, 3, 0), ("gf", 0, 1, 1), ("gf", 0, 3, 1), ("go", 0, 1, 2),
    ("go", 0, 0, 2), ("gf", 0, 2, 2), ("go", 0, 2, 2), ("gf", 0, 1, 2), ("gf", 0, 0, 2), ("gf", 0, 3, 2),
    ("go", 0, 3, 2),
)
ORDERS = (
    (
        ((2, 1, 4), (1, 2, 4)),
        ((4, 2, 1), (4, 1, 2)),
        ((4, 2, 1), (4, 1, 2)),
        ((4, 2, 1), (1, 2, 4)),
    ),
    (
        ((4, 1, 2), (2, 4, 1)),
        ((4, 2, 1), (4, 1, 2)),
        ((4, 2, 1), (4, 1, 2)),
        ((4, 2, 1), (1, 2, 4)),
    ),
)


def mm(a, b):
    return jnp.dot(a, b, preferred_element_type=F32)


def mm_t(a, b):
    return lax.dot_general(a, b, (((1,), (1,)), ((), ())), preferred_element_type=F32)


def chain(
    n, cap, fan,
    f_ref, ids_ref, ew_ref, sw_ref, valid_ref, rows_ref, bias_ref, gain_ref, shift_ref, og_hbm, w_hbm,
    out_hbm, ig_hbm, wg_hbm, bias_out, gain_out, shift_out,
    w_ref, og_ref, adj, adj_t, sel, sel_t, mask_ref, h1_ref, yf, s_ref, d_ref, zacc,
    dy_recv, hsend, hrecv, st_row, stat0, stat1, stat2, stat3,
    yt, yr, dzr, wpart, zr, fin,
    w_sem, og_sem, out_sem, mp_sem, h_sem, x_sem,
    y_sem, yp_sem, dz_sem, zr_sem, az_sem, ag_sem, fin_sem,
):
    nodes, cols = f_ref.shape
    ct = 256
    tiles = cols // ct
    half = cols // 2
    c = lax.axis_index("cluster")
    m = lax.axis_index("mp")
    peer = (c, 1 - m)
    halo = n * cap
    lookup = nodes + halo
    line, far = n // 4, n // 8
    zi, p = c // 4, c % 4
    px, py = p % 2, p // 2
    near = (c + 1 - 2 * px, c + 2 - 4 * py)
    rc = half // line
    dy_own, dyb, g_ref = zacc, og_ref, s_ref.at[1]
    out_ref, dy_send, dz_ref = yf.at[0, 0], yf.at[0, 1], yf.at[1]
    pieces = 4
    prow = half // pieces
    lanes = cols // 8
    kept = {}

    def rows_of(start, size):
        return pl.ds(pl.multiple_of(start, size), size)

    def col(j):
        return rows_of(j * ct, ct)

    def remote(src, dst, sems, idx, to):
        return pltpu.make_async_remote_copy(
            src_ref=src,
            dst_ref=dst,
            send_sem=sems.at[(0, *idx)],
            recv_sem=sems.at[(1, *idx)],
            device_id=to,
            device_id_type=MESH,
        )

    def mask(width):
        return jnp.concatenate([mask_ref[...]] * (width // 128), axis=1)

    def halo_part(d):
        return rows_of(d * 2 * cap, 2 * cap)

    def pack_halo(left, right):
        both = jnp.concatenate(
            [left.reshape(n, cap, half), right.reshape(n, cap, half)], axis=1
        )
        hsend[...] = both.reshape(n * 2 * cap, half).astype(BF)

    def halo_copy(to, frm):
        return pltpu.make_async_remote_copy(
            src_ref=hsend.at[halo_part(to)],
            dst_ref=hrecv.at[halo_part(frm)],
            send_sem=h_sem.at[0, to],
            recv_sem=h_sem.at[1, frm],
            device_id=(to, m),
            device_id_type=MESH,
        )

    def halo_start():
        def send(i, _):
            halo_copy(lax.rem(c + i, n), c).start()
            return 0

        lax.fori_loop(1, n, send, 0)
        hrecv[halo_part(c)] = hsend[halo_part(c)]

    def halo_finish():
        def finish(i, _):
            s = lax.rem(c + i, n)
            copy = halo_copy(s, s)
            copy.wait_recv()
            copy.wait_send()
            return 0

        lax.fori_loop(1, n, finish, 0)
        got = hrecv[...].astype(F32).reshape(n, 2 * cap, half)
        left = got[:, :cap, :].reshape(halo, half).astype(BF)
        right = got[:, cap:, :].reshape(halo, half).astype(BF)
        return left, right

    def pick(src):
        pack_halo(mm(sel[...], src[:, :half]), mm(sel[...], src[:, half:]))

    def stat_copy(e, buf, to, frm):
        return pltpu.make_async_remote_copy(
            src_ref=buf.at[c],
            dst_ref=buf.at[frm],
            send_sem=x_sem.at[0, e % 2, to],
            recv_sem=x_sem.at[1, e % 2, frm],
            device_id=(to, m),
            device_id_type=MESH,
        )

    def stat_start(e, buf):
        def send(i, _):
            stat_copy(e, buf, lax.rem(c + i, n), c).start()
            return 0

        lax.fori_loop(1, n, send, 0)

    def stat_finish(e, buf):
        def finish(i, _):
            s = lax.rem(c + i, n)
            copy = stat_copy(e, buf, s, s)
            copy.wait_recv()
            copy.wait_send()
            return 0

        lax.fori_loop(1, n, finish, 0)

    def fold(buf, k, row):
        for g in range(8):
            buf[c, k, g : g + 1, :] = st_row[row : row + 1, g * lanes : (g + 1) * lanes]

    def unfold(tile, row):
        for g in range(8):
            st_row[row : row + 1, g * lanes : (g + 1) * lanes] = tile[g : g + 1, :]

    def total(buf, k):
        return lax.fori_loop(1, n, lambda s, t: t + buf[s, k], buf[0, k])

    def quarter(layer, who):
        qx = 1 - px if who in (0, 2) else px
        qy = 1 - py if who in (1, 2) else py
        return (qx, qy) if layer == 1 else (qy, qx)

    def y_flip(layer):
        def flip(i, _):
            r = rows_of(i * 128, 128)
            for h in range(2):
                yt[layer, rows_of(h * cols + i * 128, 128), :] = (
                    yf[layer, h, :, r].astype(F32).T.astype(BF)
                )
            return 0

        lax.fori_loop(0, cols // 128, flip, 0)

    def y_piece(layer, who, k):
        hr, _ = quarter(layer, who)
        return remote(
            yt.at[layer, rows_of(hr * cols + m * half + k * prow, prow), :],
            yr.at[layer, who, rows_of(m * half + k * prow, prow), :],
            y_sem, (layer, who, k), (near[who], m),
        )

    def y_first(layer):
        return 1 - layer

    def z_first(layer):
        return layer

    def y_relay(layer, k):
        first = y_first(layer)
        r = rows_of(m * half + k * prow, prow)
        return remote(
            yr.at[layer, first, r, :], yr.at[layer, 2, r, :], y_sem, (layer, 2, k),
            (near[1 - first], m),
        )

    def y_forward(layer, k):
        y_piece(layer, y_first(layer), k).wait_recv()
        y_relay(layer, k).start()

    def y_pass_copy(layer, who, part):
        r = rows_of(part * half, half)
        return remote(
            yr.at[layer, who, r, :], yr.at[layer, who, r, :], yp_sem, (layer, who), peer
        )

    def y_pass(layer, who):
        if who != y_first(layer):
            for k in range(pieces):
                copy = y_relay(layer, k) if who == 2 else y_piece(layer, who, k)
                copy.wait_recv()
        y_pass_copy(layer, who, m).start()

    def y_sent(layer):
        for k in range(pieces):
            y_piece(layer, 0, k).wait_send()
            y_piece(layer, 1, k).wait_send()
            y_relay(layer, k).wait_send()
        for who in range(3):
            y_pass_copy(layer, who, m).wait_send()

    def dz_piece(layer, who, h):
        _, hc = quarter(layer, who)
        return remote(
            dz_ref.at[layer, :, rows_of(hc * half + h * ct, ct)],
            dzr.at[layer, who, h],
            dz_sem, (layer, who, h), (near[who], m),
        )

    def dz_relay(layer, h):
        first = z_first(layer)
        return remote(
            dzr.at[layer, first, h], dzr.at[layer, 2, h], dz_sem, (layer, 2, h),
            (near[1 - first], m),
        )

    def dz_forward(layer, h):
        dz_piece(layer, z_first(layer), h).wait_recv()
        dz_relay(layer, h).start()

    def dz_sent(layer):
        for h in range(2):
            dz_piece(layer, 0, h).wait_send()
            dz_piece(layer, 1, h).wait_send()
            dz_relay(layer, h).wait_send()

    def part(b):
        return m if b < 2 else 1 - m

    def line_copy(layer, b, to, frm):
        return pltpu.make_async_remote_copy(
            src_ref=wpart.at[layer, b, rows_of(to * rc, rc), :],
            dst_ref=zr.at[layer, b, frm],
            send_sem=zr_sem.at[0, layer, b, to],
            recv_sem=zr_sem.at[1, layer, b, frm],
            device_id=(to * 4 + p, m),
            device_id_type=MESH,
        )

    def once(key):
        fresh = key not in kept
        kept[key] = True
        return fresh

    def product(layer, b):
        hr, hc = quarter(layer, 3)
        h = b % 2
        if b >= 2 and once(("y", layer)):
            for who in range(3):
                y_pass_copy(layer, who, 1 - m).wait_recv()
        if once(("dz", layer, h)):
            dz_piece(layer, 1 - z_first(layer), h).wait_recv()
            dz_relay(layer, h).wait_recv()
        own_dz = dz_ref[layer, :, rows_of(hc * half + h * ct, ct)]

        def one(i, _):
            start = part(b) * half + i * ct
            acc = mm(yt[layer, rows_of(hr * cols + start, ct), :], own_dz)
            for who in range(3):
                acc = acc + mm(yr[layer, who, rows_of(start, ct), :], dzr[layer, who, h])
            wpart[layer, b, rows_of(i * ct, ct), :] = acc.astype(BF)
            return 0

        lax.fori_loop(0, half // ct, one, 0)

        def send(i, _):
            line_copy(layer, b, (zi + i) % line, zi).start()
            return 0

        lax.fori_loop(1, line, send, 0)

    def flip_bit(e, d):
        return e + d - 2 * d * ((e // d) % 2)

    def spot(layer, b, e):
        ex, ey = e % 2, (e // 2) % 2
        hr, hc = (ex, ey) if layer == 1 else (ey, ex)
        return wg_hbm.at[
            layer,
            rows_of(hr * cols + part(b) * half + (e // 4) * rc, rc),
            rows_of(hc * half + (b % 2) * ct, ct),
        ]

    def held(base, dims):
        got = [base]
        for d in dims:
            got = got + [flip_bit(e, d) for e in got]
        return got

    def far_copy(layer, b, to, frm):
        return pltpu.make_async_remote_copy(
            src_ref=fin.at[layer, b],
            dst_ref=spot(layer, b, frm),
            send_sem=az_sem.at[0, layer, b, to // 8],
            recv_sem=az_sem.at[1, layer, b, frm // 8],
            device_id=(to, m),
            device_id_type=MESH,
        )

    def hops(layer, b, i, step, arriving):
        own = isinstance(i, int)
        dims = ORDERS[layer][b][0 if own else 1]
        base = (c + 8 * i) % n
        other = flip_bit(c, dims[step])
        slot = 2**step - 1
        copies = []
        for j, e in enumerate(held(base, dims[:step])):
            if arriving:
                e = flip_bit(e, dims[step])
            src = fin.at[layer, b] if own and j == 0 and not arriving else spot(layer, b, e)
            copies.append(
                remote(src, spot(layer, b, e), ag_sem, (layer, b, base // 8, slot + j), (other, m))
            )
        return copies

    def keep(layer, b):
        return pltpu.make_async_copy(
            fin.at[layer, b], spot(layer, b, c), fin_sem.at[layer, b]
        )

    def combine(layer, b):
        def take(i, _):
            frm = (zi + i) % line
            copy = line_copy(layer, b, frm, frm)
            copy.wait_recv()
            copy.wait_send()
            return 0

        lax.fori_loop(1, line, take, 0)
        zr[layer, b, zi] = wpart[layer, b, rows_of(zi * rc, rc), :]
        fin[layer, b] = lax.fori_loop(
            1, line,
            lambda j, t: t + zr[layer, b, j].astype(F32),
            zr[layer, b, 0].astype(F32),
        ).astype(BF)
        keep(layer, b).start()

        def send(i, _):
            far_copy(layer, b, (c + 8 * i) % n, c).start()
            return 0

        lax.fori_loop(1, far, send, 0)
        gather_own(layer, b, 0)

    def gather_own(layer, b, step):
        if step > 0:
            for copy in hops(layer, b, 0, step - 1, True):
                copy.wait_recv()
        for copy in hops(layer, b, 0, step, False):
            copy.start()

    def gather_far(layer, b, step):
        def one(i, _):
            if step == 0:
                frm = (c + 8 * i) % n
                far_copy(layer, b, frm, frm).wait_recv()
            else:
                for copy in hops(layer, b, i, step - 1, True):
                    copy.wait_recv()
            for copy in hops(layer, b, i, step, False):
                copy.start()
            return 0

        lax.fori_loop(1, far, one, 0)

    def gather_finish(layer, b):
        keep(layer, b).wait()

        def ends(i):
            for copy in hops(layer, b, i, 2, True):
                copy.wait_recv()
            for step in range(3):
                for copy in hops(layer, b, i, step, False):
                    copy.wait_send()

        def one(i, _):
            far_copy(layer, b, (c + 8 * i) % n, c).wait_send()
            ends(i)
            return 0

        ends(0)
        lax.fori_loop(1, far, one, 0)

    w_copies = [
        pltpu.make_async_copy(w_hbm.at[layer], w_ref.at[layer], w_sem.at[layer])
        for layer in range(2)
    ]
    og_copy = pltpu.make_async_copy(og_hbm, og_ref, og_sem)
    out_copy = pltpu.make_async_copy(out_ref, out_hbm, out_sem.at[0])
    ig_copy = pltpu.make_async_copy(h1_ref, ig_hbm, out_sem.at[1])

    def begin():
        barrier = pltpu.get_barrier_semaphore()

        def greet(i, _):
            pl.semaphore_signal(
                barrier, inc=1, device_id=(lax.rem(c + i, n), m), device_id_type=MESH
            )
            return 0

        lax.fori_loop(1, n, greet, 0)
        pl.semaphore_signal(barrier, inc=1, device_id=peer, device_id_type=MESH)
        w_copies[0].start()
        og_copy.start()
        w_copies[1].start()

        def choose(i, _):
            r = rows_of(i * 128, 128)
            one_hot = jnp.where(
                rows_ref[:, r] == lax.broadcasted_iota(jnp.int32, (nodes, 128), 0), 1.0, 0.0
            )
            sel_t[:, r] = one_hot.astype(BF)
            sel[r, :] = one_hot.T.astype(BF)
            return 0

        lax.fori_loop(0, halo // 128, choose, 0)
        pick(f_ref)
        pl.semaphore_wait(barrier, n)
        halo_start()
        mask_ref[...] = jnp.broadcast_to(valid_ref[...].astype(F32), (128, nodes)).T
        rb = 16
        place = lax.broadcasted_iota(jnp.int32, (rb, nodes), 0)
        node = lax.broadcasted_iota(jnp.int32, (rb, nodes), 1)

        def build(i, _):
            slots = place + i * rb
            a = jnp.where(node == slots, 2.0 * sw_ref[...], 0.0)
            for k in range(fan):
                a = a + jnp.where(ids_ref[k : k + 1, :] == slots, ew_ref[k : k + 1, :], 0.0)
            adj_t[rows_of(i * rb, rb), :] = a.astype(BF)
            return 0

        lax.fori_loop(0, lookup // rb, build, 0)

        def turn(i, _):
            r = rows_of(i * 128, 128)
            adj[:, r] = adj_t[r, :].astype(F32).T.astype(BF)
            return 0

        lax.fori_loop(0, lookup // 128, turn, 0)

    def agg_local(layer):
        src = f_ref if layer == 0 else h1_ref
        for h in range(2):
            cs = slice(h * half, (h + 1) * half)
            zacc[:, cs] = mm(adj[:, :nodes], src[:, cs])

    def mp_copy(k, src, dst):
        return remote(src, dst, mp_sem, (k,), peer)

    def y_exchange(layer, h):
        ref = yf.at[layer, m, :, slice(h * half, (h + 1) * half)]
        return mp_copy(layer * 2 + h, ref, ref)

    def agg_halo(layer):
        parts = halo_finish()
        for h in range(2):
            cs = slice(h * half, (h + 1) * half)
            yf[layer, m, :, cs] = (zacc[:, cs] + mm(adj[:, nodes:], parts[h])).astype(BF)
            y_exchange(layer, h).start()

    def z_own(layer):
        w_copies[layer].wait()

        def first(j, _):
            zacc[:, col(j)] = mm(yf[layer, m], w_ref[layer, rows_of(m * cols, cols), col(j)])
            return 0

        lax.fori_loop(0, tiles, first, 0)
        for h in range(2):
            y_exchange(layer, h).wait_recv()

    def z_other(layer):
        if layer == 1:
            og_copy.wait()
        own_count = jnp.sum(mask_ref[...], axis=0, keepdims=True)
        own_count = jnp.concatenate([own_count] * (ct // 128), axis=1)
        own_inv = 1.0 / jnp.maximum(own_count, 1.0)

        def second(j, _):
            z = zacc[:, col(j)] + mm(
                yf[layer, 1 - m], w_ref[layer, rows_of((1 - m) * cols, cols), col(j)]
            )
            z = z + bias_ref[layer : layer + 1, col(j)]
            sig = jax.nn.sigmoid(z)
            s = z * sig
            s_ref[layer, :, col(j)] = s
            d_ref[layer, :, col(j)] = (sig * (1.0 + z * (1.0 - sig))).astype(BF)
            valid = mask(ct)
            tot = jnp.sum(s * valid, axis=0, keepdims=True)
            cen = s - tot * own_inv
            st_row[0:1, col(j)] = tot
            st_row[1:2, col(j)] = jnp.sum(cen * cen * valid, axis=0, keepdims=True)
            if layer == 0:
                st_row[2:3, col(j)] = own_count
            else:
                pg = og_ref[:, col(j)].astype(F32) * valid
                st_row[2:3, col(j)] = jnp.sum(pg, axis=0, keepdims=True)
                st_row[3:4, col(j)] = jnp.sum(pg * cen, axis=0, keepdims=True)
            return 0

        lax.fori_loop(0, tiles, second, 0)
        buf = stat0 if layer == 0 else stat1
        for k in range(3 if layer == 0 else 4):
            fold(buf, k, k)

    def stats_out(layer):
        stat_start(layer, stat0 if layer == 0 else stat1)
        for h in range(2):
            y_exchange(layer, h).wait_send()
        y_flip(layer)

    def normalize(layer):
        buf = stat0 if layer == 0 else stat1
        stat_finish(layer, buf)
        count = jnp.maximum(total(stat0, 2), 1.0)
        mu = total(buf, 0) / count

        def spread(s, t):
            nc = stat0[s, 2]
            off = buf[s, 0] / jnp.maximum(nc, 1.0) - mu
            return t + buf[s, 1] + nc * off * off

        var = lax.fori_loop(0, n, spread, jnp.zeros_like(mu)) / count
        inv = lax.rsqrt(var + EPS)
        at = 8 if layer == 0 else 4
        unfold(mu, at)
        unfold(inv, at + 1)
        mu_row, inv_row = st_row[at : at + 1, :], st_row[at + 1 : at + 2, :]
        gain_row = gain_ref[layer : layer + 1, :]
        shift_row = shift_ref[layer : layer + 1, :]
        dst = h1_ref if layer == 0 else out_ref
        for j in range(tiles):
            cs = slice(j * ct, (j + 1) * ct)
            x = (s_ref[layer, :, cs] - mu_row[:, cs]) * inv_row[:, cs]
            dst[:, cs] = (mask(ct) * (gain_row[:, cs] * x + shift_row[:, cs])).astype(BF)
        if layer == 0:
            pick(h1_ref)
            return
        out_copy.start()

        def gains(s, t):
            off = stat1[s, 0] / jnp.maximum(stat0[s, 2], 1.0) - mu
            return t + stat1[s, 3] + off * stat1[s, 2]

        unfold(total(stat1, 2), 6)
        unfold(inv * lax.fori_loop(0, n, gains, jnp.zeros_like(mu)), 7)
        unfold(1.0 / count, 10)
        norm_sums(1)
        pre_grad(1)
        fold(stat2, 2, 11)

    def norm_sums(layer):
        gain_out[layer : layer + 1, :] = st_row[7:8, :]
        shift_out[layer : layer + 1, :] = st_row[6:7, :]

    def pre_grad(layer):
        at = 8 if layer == 0 else 4
        grad_src = og_ref if layer == 1 else g_ref

        def pre(j, _):
            gain = gain_ref[layer : layer + 1, col(j)]
            inv_row = st_row[at + 1 : at + 2, col(j)]
            ic = st_row[10:11, col(j)]
            x = (s_ref[layer, :, col(j)] - st_row[at : at + 1, col(j)]) * inv_row
            valid = mask(ct)
            pg = grad_src[:, col(j)].astype(F32) * valid
            ds = (
                valid
                * (inv_row * gain)
                * (pg - st_row[6:7, col(j)] * ic - x * (st_row[7:8, col(j)] * ic))
            )
            dz = (ds * d_ref[layer, :, col(j)].astype(F32)).astype(BF)
            dz_ref[layer, :, col(j)] = dz
            st_row[11:12, col(j)] = jnp.sum(dz.astype(F32), axis=0, keepdims=True)
            return 0

        lax.fori_loop(0, tiles, pre, 0)

    def dy_copy(layer):
        return mp_copy(4 + layer, dy_send, dy_recv.at[layer])

    def dy_other(layer):
        def other(j, _):
            r = rows_of((1 - m) * cols + j * ct, ct)
            dy_send[:, col(j)] = mm_t(dz_ref[layer], w_ref[layer, r, :]).astype(BF)
            return 0

        lax.fori_loop(0, tiles, other, 0)
        dy_copy(layer).start()

    def dy_mine(layer):
        def mine(j, _):
            r = rows_of(m * cols + j * ct, ct)
            dy_own[:, col(j)] = mm_t(dz_ref[layer], w_ref[layer, r, :])
            return 0

        lax.fori_loop(0, tiles, mine, 0)
        dy_copy(layer).wait_recv()
        for j in range(tiles):
            cs = slice(j * ct, (j + 1) * ct)
            dyb[:, cs] = (dy_own[:, cs] + dy_recv[layer, :, cs].astype(F32)).astype(BF)
        back = adj_t[nodes:, :]
        pack_halo(mm(back, dyb[:, :half]), mm(back, dyb[:, half:]))
        halo_start()

    def back_local(layer):
        for h in range(2):
            cs = slice(h * half, (h + 1) * half)
            g_ref[:, cs] = mm(adj_t[:nodes, :], dyb[:, cs])
        dy_copy(layer).wait_send()

    def back_halo(layer):
        parts = halo_finish()
        for h in range(2):
            cs = slice(h * half, (h + 1) * half)
            got = g_ref[:, cs] + mm(sel_t[...], parts[h])
            if layer == 1:
                g_ref[:, cs] = got
                pg = got * mask(half)
                x = (s_ref[0, :, cs] - st_row[8:9, cs]) * st_row[9:10, cs]
                st_row[0:1, cs] = jnp.sum(pg, axis=0, keepdims=True)
                st_row[1:2, cs] = jnp.sum(pg * x, axis=0, keepdims=True)
            else:
                h1_ref[:, cs] = got.astype(BF)
        if layer == 1:
            fold(stat2, 0, 0)
            fold(stat2, 1, 1)
            stat_start(2, stat2)
        else:
            ig_copy.start()

    def back_norm():
        stat_finish(2, stat2)
        unfold(total(stat2, 0), 6)
        unfold(total(stat2, 1), 7)
        unfold(total(stat2, 2), 12)
        norm_sums(0)
        bias_out[1:2, :] = st_row[12:13, :]
        pre_grad(0)
        fold(stat3, 0, 11)
        stat_start(3, stat3)

    table = {
        "A0": lambda: (begin(), agg_local(0), agg_halo(0), z_own(0), z_other(0)),
        "A": lambda: stats_out(0),
        "B0": lambda: normalize(0),
        "B": halo_start,
        "B1": lambda: (agg_local(1), agg_halo(1)),
        "B2": lambda: z_own(1),
        "C": lambda: (z_other(1), stats_out(1)),
        "C2": lambda: normalize(1),
        "C3": lambda: dy_other(1),
        "D": lambda: dy_mine(1),
        "E": lambda: (back_local(1), back_halo(1)),
        "E2": back_norm,
        "E3": lambda: dy_other(0),
        "F": lambda: dy_mine(0),
        "G": lambda: back_local(0),
        "IG": lambda: back_halo(0),
        "ys": lambda l, who, k: y_piece(l, who, k).start(),
        "yf": y_forward,
        "yp": y_pass,
        "ds": lambda l, who, h: dz_piece(l, who, h).start(),
        "df": dz_forward,
        "pr": product,
        "cb": combine,
        "go": gather_own,
        "gf": gather_far,
    }
    for name, *args in SCHEDULE:
        table[name](*args)

    stat_finish(3, stat3)
    unfold(total(stat3, 0), 12)
    bias_out[0:1, :] = st_row[12:13, :]
    out_copy.wait()
    ig_copy.wait()
    for layer in (1, 0):
        y_sent(layer)
        dz_sent(layer)
        for b in range(4):
            gather_finish(layer, b)


def hand_over(
    rows, slots,
    wg_hbm, out_in, ig_in, bias_in, gain_in, shift_in,
    wg_out, out_out, ig_out, bias_out, gain_out, shift_out,
    narrow, wide, in_sem, wide_sem, pass_sem,
):
    blocks = narrow.shape[0]
    per_layer = wg_hbm.shape[1] // rows

    def block(ref, i):
        return ref.at[i // per_layer, pl.ds((i % per_layer) * rows, rows), :]

    def read(i):
        return pltpu.make_async_copy(block(wg_hbm, i), narrow.at[i], in_sem.at[i])

    def write(i):
        return pltpu.make_async_copy(wide.at[i % slots], block(wg_out, i), wide_sem.at[i])

    for i in range(blocks):
        read(i).start()
    passes = [
        pltpu.make_async_copy(out_in, out_out, pass_sem.at[0]),
        pltpu.make_async_copy(ig_in, ig_out, pass_sem.at[1]),
    ]
    for i in range(blocks):
        read(i).wait()
        if i >= slots:
            write(i - slots).wait()
        wide[i % slots] = narrow[i].astype(F32)
        write(i).start()
        if i == 1:
            for copy in passes:
                copy.start()
    bias_out[...] = bias_in[...]
    gain_out[...] = gain_in[...]
    shift_out[...] = shift_in[...]
    for i in range(blocks - slots, blocks):
        write(i).wait()
    for copy in passes:
        copy.wait()


def per_device(
    features, neighbour_ids, edge_weight, self_weight, send_rows, valid_mask,
    weights, biases, norm_gain, norm_shift, output_grad,
):
    nodes, cols = features.shape
    fan = neighbour_ids.shape[1]
    n, cap = send_rows.shape[1], send_rows.shape[2]
    halo = n * cap
    lookup = nodes + halo
    line = n // 4
    half = cols // 2
    vm = pl.BlockSpec(memory_space=pltpu.VMEM)
    anyspace = pl.BlockSpec(memory_space=pl.ANY)
    dma = pltpu.SemaphoreType.DMA
    small = jax.ShapeDtypeStruct((2, cols), F32)
    wide_block = jax.ShapeDtypeStruct((nodes, cols), BF)
    out, ig, wg, bias, gain, shift = pl.pallas_call(
        functools.partial(chain, n, cap, fan),
        out_shape=(
            wide_block, wide_block, jax.ShapeDtypeStruct((2, 2 * cols, cols), BF),
            small, small, small,
        ),
        in_specs=[vm] * 9 + [anyspace] * 2,
        out_specs=(anyspace, anyspace, anyspace, vm, vm, vm),
        scratch_shapes=[
            pltpu.VMEM((2, 2 * cols, cols), BF),
            pltpu.VMEM((nodes, cols), BF),
            pltpu.VMEM((nodes, lookup), BF),
            pltpu.VMEM((lookup, nodes), BF),
            pltpu.VMEM((halo, nodes), BF),
            pltpu.VMEM((nodes, halo), BF),
            pltpu.VMEM((nodes, 128), F32),
            pltpu.VMEM((nodes, cols), BF),
            pltpu.VMEM((2, 2, nodes, cols), BF),
            pltpu.VMEM((2, nodes, cols), F32),
            pltpu.VMEM((2, nodes, cols), BF),
            pltpu.VMEM((nodes, cols), F32),
            pltpu.VMEM((2, nodes, cols), BF),
            pltpu.VMEM((2 * halo, half), BF),
            pltpu.VMEM((2 * halo, half), BF),
            pltpu.VMEM((16, cols), F32),
            pltpu.VMEM((n, 3, 8, cols // 8), F32),
            pltpu.VMEM((n, 4, 8, cols // 8), F32),
            pltpu.VMEM((n, 3, 8, cols // 8), F32),
            pltpu.VMEM((n, 1, 8, cols // 8), F32),
            pltpu.VMEM((2, 2 * cols, nodes), BF),
            pltpu.VMEM((2, 3, cols, nodes), BF),
            pltpu.VMEM((2, 3, 2, nodes, cols // 4), BF),
            pltpu.VMEM((2, 4, half, cols // 4), BF),
            pltpu.VMEM((2, 4, line, half // line, cols // 4), BF),
            pltpu.VMEM((2, 4, half // line, cols // 4), BF),
            dma((2,)), dma, dma((2,)), dma((2, 6)), dma((2, n)), dma((2, 2, n)),
            dma((2, 2, 3, 4)), dma((2, 2, 3)), dma((2, 2, 3, 2)),
            dma((2, 2, 4, line)), dma((2, 2, 4, n // 8)), dma((2, 2, 4, n // 8, 7)), dma((2, 4)),
        ],
        compiler_params=pltpu.CompilerParams(
            collective_id=0, has_side_effects=True, vmem_limit_bytes=62 * 2**20
        ),
    )(
        features, neighbour_ids.T, edge_weight.T, self_weight.reshape(1, nodes),
        valid_mask.reshape(1, nodes), send_rows.reshape(1, halo), biases, norm_gain, norm_shift,
        output_grad, weights,
    )
    rows, slots = 512, 4
    blocks = 2 * 2 * cols // rows
    wg, out, ig, bias, gain, shift = pl.pallas_call(
        functools.partial(hand_over, rows, slots),
        out_shape=(
            jax.ShapeDtypeStruct((2, 2 * cols, cols), F32), wide_block, wide_block,
            small, small, small,
        ),
        in_specs=[anyspace] * 3 + [vm] * 3,
        out_specs=(anyspace, anyspace, anyspace, vm, vm, vm),
        scratch_shapes=[
            pltpu.VMEM((blocks, rows, cols), BF),
            pltpu.VMEM((slots, rows, cols), F32),
            dma((blocks,)), dma((blocks,)), dma((2,)),
        ],
        compiler_params=pltpu.CompilerParams(vmem_limit_bytes=32 * 2**20),
    )(wg, out, ig, bias, gain, shift)
    return out, ig, wg, bias, gain, shift


def solution(mesh):
    return jax.shard_map(
        per_device,
        mesh=mesh,
        in_specs=(
            P("cluster", "mp"),
            P("cluster", None),
            P("cluster", None),
            P("cluster"),
            P("cluster", None, None),
            P("cluster"),
            P(None, None, "mp"),
            P(None, "mp"),
            P(None, "mp"),
            P(None, "mp"),
            P("cluster", "mp"),
        ),
        out_specs=(
            P("cluster", "mp"),
            P("cluster", "mp"),
            P(None, None, "mp"),
            P(None, "mp"),
            P(None, "mp"),
            P(None, "mp"),
        ),
        check_vma=False,
    )
```

```python
import functools

import jax
import jax.numpy as jnp
from jax import lax
from jax.experimental import pallas as pl
from jax.experimental.pallas import tpu as pltpu
from jax.sharding import PartitionSpec as P

EPS = 1e-05
MESH = pl.DeviceIdType.MESH
BF = jnp.bfloat16
F32 = jnp.float32

SCHEDULE = (
    ("A0",),
    ("A",), ("ys", 0, 0, 1), ("ys", 0, 0, 0), ("ys", 0, 1, 0), ("ys", 0, 1, 2),
    ("B0",),
    ("B",), ("ys", 0, 1, 1), ("ys", 0, 0, 3), ("yf", 0, 2), ("ys", 0, 1, 3),
    ("B1",), ("yf", 0, 1),
    ("B2",),
    ("C",), ("yf", 0, 0), ("yf", 0, 3), ("ys", 1, 0, 3), ("ys", 1, 1, 1), ("ys", 1, 0, 2), ("ys", 1, 1, 0),
    ("ys", 1, 1, 2),
    ("C2",), ("ds", 1, 1, 0),
    ("C3",), ("ys", 1, 0, 0),
    ("D",), ("ys", 1, 0, 1), ("yf", 1, 3), ("yf", 1, 0), ("df", 1, 0), ("yf", 1, 1),
    ("E",), ("ds", 1, 0, 0), ("yp", 0, 2), ("ys", 1, 1, 3), ("yf", 1, 2),
    ("E2",), ("ys", 0, 0, 2), ("ds", 1, 0, 1), ("ds", 1, 1, 1), ("yp", 1, 1), ("yp", 1, 0), ("ds", 0, 1, 0),
    ("yp", 1, 2), ("pr", 1, 0), ("yp", 0, 1), ("pr", 1, 2), ("df", 1, 1), ("ds", 0, 1, 1), ("cb", 1, 0),
    ("ds", 0, 0, 1), ("cb", 1, 2), ("pr", 1, 1), ("go", 1, 0, 1), ("gf", 1, 0, 0), ("ds", 0, 0, 0), ("df", 0, 1),
    ("gf", 1, 2, 0), ("pr", 1, 3), ("df", 0, 0), ("gf", 1, 0, 1), ("cb", 1, 1), ("go", 1, 0, 2), ("yp", 0, 0),
    ("go", 1, 2, 1), ("gf", 1, 2, 1), ("cb", 1, 3), ("go", 1, 1, 1), ("pr", 0, 3), ("gf", 1, 0, 2), ("pr", 0, 1),
    ("gf", 1, 2, 2), ("gf", 1, 1, 0), ("gf", 1, 3, 0),
    ("E3",),
    ("F",), ("cb", 0, 3),
    ("G",), ("go", 1, 3, 1), ("go", 1, 1, 2), ("gf", 1, 1, 1), ("cb", 0, 1), ("go", 1, 3, 2), ("gf", 1, 3, 1),
    ("go", 0, 3, 1), ("go", 0, 1, 1), ("pr", 0, 0), ("gf", 1, 3, 2), ("gf", 1, 1, 2), ("gf", 0, 3, 0),
    ("go", 1, 2, 2), ("go", 0, 1, 2), ("pr", 0, 2), ("cb", 0, 0), ("gf", 0, 1, 0), ("cb", 0, 2), ("gf", 0, 3, 1),
    ("go", 0, 2, 1), ("gf", 0, 0, 0), ("gf", 0, 2, 0), ("gf", 0, 1, 1), ("go", 0, 0, 1), ("go", 0, 3, 2),
    ("gf", 0, 2, 1), ("gf", 0, 0, 1), ("go", 0, 2, 2), ("go", 0, 0, 2), ("gf", 0, 1, 2),
    ("IG",), ("gf", 0, 0, 2), ("gf", 0, 2, 2), ("gf", 0, 3, 2),
)
ORDERS = (
    (
        ((4, 2, 1), (4, 2, 1)),
        ((1, 4, 2), (4, 1, 2)),
        ((1, 2, 4), (4, 1, 2)),
        ((2, 1, 4), (2, 1, 4)),
    ),
    (
        ((4, 2, 1), (4, 2, 1)),
        ((4, 1, 2), (2, 4, 1)),
        ((4, 2, 1), (4, 1, 2)),
        ((4, 1, 2), (4, 1, 2)),
    ),
)


def mm(a, b):
    return jnp.dot(a, b, preferred_element_type=F32)


def mm_t(a, b):
    return lax.dot_general(a, b, (((1,), (1,)), ((), ())), preferred_element_type=F32)


def chain(
    n, cap, fan,
    f_ref, ids_ref, ew_ref, sw_ref, valid_ref, rows_ref, bias_ref, gain_ref, shift_ref, og_hbm, w_hbm,
    out_hbm, ig_hbm, wg_hbm, bias_out, gain_out, shift_out,
    w_ref, og_ref, adj, adj_t, sel, sel_t, mask_ref, h1_ref, yf, s_ref, d_ref, zacc,
    dy_recv, hsend, hrecv, st_row, stat0, stat1, stat2, stat3,
    yt, yr, dzr, wpart, zr, fin,
    w_sem, og_sem, out_sem, mp_sem, h_sem, x_sem,
    y_sem, yp_sem, dz_sem, zr_sem, az_sem, ag_sem, fin_sem,
):
    nodes, cols = f_ref.shape
    ct = 256
    tiles = cols // ct
    half = cols // 2
    c = lax.axis_index("cluster")
    m = lax.axis_index("mp")
    peer = (c, 1 - m)
    halo = n * cap
    lookup = nodes + halo
    line, far = n // 4, n // 8
    zi, p = c // 4, c % 4
    px, py = p % 2, p // 2
    near = (c + 1 - 2 * px, c + 2 - 4 * py)
    rc = half // line
    dy_own, dyb, g_ref = zacc, og_ref, s_ref.at[1]
    out_ref, dy_send, dz_ref = yf.at[0, 0], yf.at[0, 1], yf.at[1]
    pieces = 4
    prow = half // pieces
    lanes = cols // 8
    kept = {}

    def rows_of(start, size):
        return pl.ds(pl.multiple_of(start, size), size)

    def col(j):
        return rows_of(j * ct, ct)

    def remote(src, dst, sems, idx, to):
        return pltpu.make_async_remote_copy(
            src_ref=src,
            dst_ref=dst,
            send_sem=sems.at[(0, *idx)],
            recv_sem=sems.at[(1, *idx)],
            device_id=to,
            device_id_type=MESH,
        )

    def mask(width):
        return jnp.concatenate([mask_ref[...]] * (width // 128), axis=1)

    def halo_part(d):
        return rows_of(d * 2 * cap, 2 * cap)

    def pack_halo(left, right):
        both = jnp.concatenate(
            [left.reshape(n, cap, half), right.reshape(n, cap, half)], axis=1
        )
        hsend[...] = both.reshape(n * 2 * cap, half).astype(BF)

    def halo_copy(to, frm):
        return pltpu.make_async_remote_copy(
            src_ref=hsend.at[halo_part(to)],
            dst_ref=hrecv.at[halo_part(frm)],
            send_sem=h_sem.at[0, to],
            recv_sem=h_sem.at[1, frm],
            device_id=(to, m),
            device_id_type=MESH,
        )

    def halo_start():
        def send(i, _):
            halo_copy(lax.rem(c + i, n), c).start()
            return 0

        lax.fori_loop(1, n, send, 0)
        hrecv[halo_part(c)] = hsend[halo_part(c)]

    def halo_finish():
        def finish(i, _):
            s = lax.rem(c + i, n)
            copy = halo_copy(s, s)
            copy.wait_recv()
            copy.wait_send()
            return 0

        lax.fori_loop(1, n, finish, 0)
        got = hrecv[...].astype(F32).reshape(n, 2 * cap, half)
        left = got[:, :cap, :].reshape(halo, half).astype(BF)
        right = got[:, cap:, :].reshape(halo, half).astype(BF)
        return left, right

    def pick(src):
        pack_halo(mm(sel[...], src[:, :half]), mm(sel[...], src[:, half:]))

    def stat_copy(e, buf, to, frm):
        return pltpu.make_async_remote_copy(
            src_ref=buf.at[c],
            dst_ref=buf.at[frm],
            send_sem=x_sem.at[0, e % 2, to],
            recv_sem=x_sem.at[1, e % 2, frm],
            device_id=(to, m),
            device_id_type=MESH,
        )

    def stat_start(e, buf):
        def send(i, _):
            stat_copy(e, buf, lax.rem(c + i, n), c).start()
            return 0

        lax.fori_loop(1, n, send, 0)

    def stat_finish(e, buf):
        def finish(i, _):
            s = lax.rem(c + i, n)
            copy = stat_copy(e, buf, s, s)
            copy.wait_recv()
            copy.wait_send()
            return 0

        lax.fori_loop(1, n, finish, 0)

    def fold(buf, k, row):
        for g in range(8):
            buf[c, k, g : g + 1, :] = st_row[row : row + 1, g * lanes : (g + 1) * lanes]

    def unfold(tile, row):
        for g in range(8):
            st_row[row : row + 1, g * lanes : (g + 1) * lanes] = tile[g : g + 1, :]

    def total(buf, k):
        return lax.fori_loop(1, n, lambda s, t: t + buf[s, k], buf[0, k])

    def quarter(layer, who):
        qx = 1 - px if who in (0, 2) else px
        qy = 1 - py if who in (1, 2) else py
        return (qx, qy) if layer == 1 else (qy, qx)

    def y_flip(layer):
        def flip(i, _):
            r = rows_of(i * 128, 128)
            for h in range(2):
                yt[layer, rows_of(h * cols + i * 128, 128), :] = (
                    yf[layer, h, :, r].astype(F32).T.astype(BF)
                )
            return 0

        lax.fori_loop(0, cols // 128, flip, 0)

    def y_piece(layer, who, k):
        hr, _ = quarter(layer, who)
        return remote(
            yt.at[layer, rows_of(hr * cols + m * half + k * prow, prow), :],
            yr.at[layer, who, rows_of(m * half + k * prow, prow), :],
            y_sem, (layer, who, k), (near[who], m),
        )

    def y_first(layer):
        return 1 - layer

    def z_first(layer):
        return layer

    def y_relay(layer, k):
        first = y_first(layer)
        r = rows_of(m * half + k * prow, prow)
        return remote(
            yr.at[layer, first, r, :], yr.at[layer, 2, r, :], y_sem, (layer, 2, k),
            (near[1 - first], m),
        )

    def y_forward(layer, k):
        y_piece(layer, y_first(layer), k).wait_recv()
        y_relay(layer, k).start()

    def y_pass_copy(layer, who, part):
        r = rows_of(part * half, half)
        return remote(
            yr.at[layer, who, r, :], yr.at[layer, who, r, :], yp_sem, (layer, who), peer
        )

    def y_pass(layer, who):
        if who != y_first(layer):
            for k in range(pieces):
                copy = y_relay(layer, k) if who == 2 else y_piece(layer, who, k)
                copy.wait_recv()
        y_pass_copy(layer, who, m).start()

    def y_sent(layer):
        for k in range(pieces):
            y_piece(layer, 0, k).wait_send()
            y_piece(layer, 1, k).wait_send()
            y_relay(layer, k).wait_send()
        for who in range(3):
            y_pass_copy(layer, who, m).wait_send()

    def dz_piece(layer, who, h):
        _, hc = quarter(layer, who)
        return remote(
            dz_ref.at[layer, :, rows_of(hc * half + h * ct, ct)],
            dzr.at[layer, who, h],
            dz_sem, (layer, who, h), (near[who], m),
        )

    def dz_relay(layer, h):
        first = z_first(layer)
        return remote(
            dzr.at[layer, first, h], dzr.at[layer, 2, h], dz_sem, (layer, 2, h),
            (near[1 - first], m),
        )

    def dz_forward(layer, h):
        dz_piece(layer, z_first(layer), h).wait_recv()
        dz_relay(layer, h).start()

    def dz_sent(layer):
        for h in range(2):
            dz_piece(layer, 0, h).wait_send()
            dz_piece(layer, 1, h).wait_send()
            dz_relay(layer, h).wait_send()

    def part(b):
        return m if b < 2 else 1 - m

    def line_copy(layer, b, to, frm):
        return pltpu.make_async_remote_copy(
            src_ref=wpart.at[layer, b, rows_of(to * rc, rc), :],
            dst_ref=zr.at[layer, b, frm],
            send_sem=zr_sem.at[0, layer, b, to],
            recv_sem=zr_sem.at[1, layer, b, frm],
            device_id=(to * 4 + p, m),
            device_id_type=MESH,
        )

    def once(key):
        fresh = key not in kept
        kept[key] = True
        return fresh

    def product(layer, b):
        hr, hc = quarter(layer, 3)
        h = b % 2
        if b >= 2 and once(("y", layer)):
            for who in range(3):
                y_pass_copy(layer, who, 1 - m).wait_recv()
        if once(("dz", layer, h)):
            dz_piece(layer, 1 - z_first(layer), h).wait_recv()
            dz_relay(layer, h).wait_recv()
        own_dz = dz_ref[layer, :, rows_of(hc * half + h * ct, ct)]

        def one(i, _):
            start = part(b) * half + i * ct
            acc = mm(yt[layer, rows_of(hr * cols + start, ct), :], own_dz)
            for who in range(3):
                acc = acc + mm(yr[layer, who, rows_of(start, ct), :], dzr[layer, who, h])
            wpart[layer, b, rows_of(i * ct, ct), :] = acc.astype(BF)
            return 0

        lax.fori_loop(0, half // ct, one, 0)

        def send(i, _):
            line_copy(layer, b, (zi + i) % line, zi).start()
            return 0

        lax.fori_loop(1, line, send, 0)

    def flip_bit(e, d):
        return e + d - 2 * d * ((e // d) % 2)

    def spot(layer, b, e):
        ex, ey = e % 2, (e // 2) % 2
        hr, hc = (ex, ey) if layer == 1 else (ey, ex)
        return wg_hbm.at[
            layer,
            rows_of(hr * cols + part(b) * half + (e // 4) * rc, rc),
            rows_of(hc * half + (b % 2) * ct, ct),
        ]

    def held(base, dims):
        got = [base]
        for d in dims:
            got = got + [flip_bit(e, d) for e in got]
        return got

    def far_copy(layer, b, to, frm):
        return pltpu.make_async_remote_copy(
            src_ref=fin.at[layer, b],
            dst_ref=spot(layer, b, frm),
            send_sem=az_sem.at[0, layer, b, to // 8],
            recv_sem=az_sem.at[1, layer, b, frm // 8],
            device_id=(to, m),
            device_id_type=MESH,
        )

    def hops(layer, b, i, step, arriving):
        own = isinstance(i, int)
        dims = ORDERS[layer][b][0 if own else 1]
        base = (c + 8 * i) % n
        other = flip_bit(c, dims[step])
        slot = 2**step - 1
        copies = []
        for j, e in enumerate(held(base, dims[:step])):
            if arriving:
                e = flip_bit(e, dims[step])
            src = fin.at[layer, b] if own and j == 0 and not arriving else spot(layer, b, e)
            copies.append(
                remote(src, spot(layer, b, e), ag_sem, (layer, b, base // 8, slot + j), (other, m))
            )
        return copies

    def keep(layer, b):
        return pltpu.make_async_copy(
            fin.at[layer, b], spot(layer, b, c), fin_sem.at[layer, b]
        )

    def combine(layer, b):
        def take(i, _):
            frm = (zi + i) % line
            copy = line_copy(layer, b, frm, frm)
            copy.wait_recv()
            copy.wait_send()
            return 0

        lax.fori_loop(1, line, take, 0)
        zr[layer, b, zi] = wpart[layer, b, rows_of(zi * rc, rc), :]
        fin[layer, b] = lax.fori_loop(
            1, line,
            lambda j, t: t + zr[layer, b, j].astype(F32),
            zr[layer, b, 0].astype(F32),
        ).astype(BF)
        keep(layer, b).start()

        def send(i, _):
            far_copy(layer, b, (c + 8 * i) % n, c).start()
            return 0

        lax.fori_loop(1, far, send, 0)
        gather_own(layer, b, 0)

    def gather_own(layer, b, step):
        if step > 0:
            for copy in hops(layer, b, 0, step - 1, True):
                copy.wait_recv()
        for copy in hops(layer, b, 0, step, False):
            copy.start()
        if step > 0:
            for copy in hops(layer, b, 0, step - 1, False):
                copy.wait_send()

    def gather_far(layer, b, step):
        def one(i, _):
            if step == 0:
                frm = (c + 8 * i) % n
                far_copy(layer, b, frm, frm).wait_recv()
            else:
                for copy in hops(layer, b, i, step - 1, True):
                    copy.wait_recv()
            for copy in hops(layer, b, i, step, False):
                copy.start()
            if step > 0:
                for copy in hops(layer, b, i, step - 1, False):
                    copy.wait_send()
            return 0

        lax.fori_loop(1, far, one, 0)

    def gather_finish(layer, b):
        keep(layer, b).wait()

        def ends(i):
            for copy in hops(layer, b, i, 2, True):
                copy.wait_recv()
            for copy in hops(layer, b, i, 2, False):
                copy.wait_send()

        def one(i, _):
            far_copy(layer, b, (c + 8 * i) % n, c).wait_send()
            ends(i)
            return 0

        ends(0)
        lax.fori_loop(1, far, one, 0)

    w_copies = [
        pltpu.make_async_copy(w_hbm.at[layer], w_ref.at[layer], w_sem.at[layer])
        for layer in range(2)
    ]
    og_copy = pltpu.make_async_copy(og_hbm, og_ref, og_sem)
    out_copy = pltpu.make_async_copy(out_ref, out_hbm, out_sem.at[0])
    ig_copy = pltpu.make_async_copy(h1_ref, ig_hbm, out_sem.at[1])

    def begin():
        barrier = pltpu.get_barrier_semaphore()

        def greet(i, _):
            pl.semaphore_signal(
                barrier, inc=1, device_id=(lax.rem(c + i, n), m), device_id_type=MESH
            )
            return 0

        lax.fori_loop(1, n, greet, 0)
        pl.semaphore_signal(barrier, inc=1, device_id=peer, device_id_type=MESH)
        w_copies[0].start()
        og_copy.start()
        w_copies[1].start()

        def choose(i, _):
            r = rows_of(i * 128, 128)
            one_hot = jnp.where(
                rows_ref[:, r] == lax.broadcasted_iota(jnp.int32, (nodes, 128), 0), 1.0, 0.0
            )
            sel_t[:, r] = one_hot.astype(BF)
            sel[r, :] = one_hot.T.astype(BF)
            return 0

        lax.fori_loop(0, halo // 128, choose, 0)
        pick(f_ref)
        pl.semaphore_wait(barrier, n)
        halo_start()
        mask_ref[...] = jnp.broadcast_to(valid_ref[...].astype(F32), (128, nodes)).T
        rb = 16
        place = lax.broadcasted_iota(jnp.int32, (rb, nodes), 0)
        node = lax.broadcasted_iota(jnp.int32, (rb, nodes), 1)

        def build(i, _):
            slots = place + i * rb
            a = jnp.where(node == slots, 2.0 * sw_ref[...], 0.0)
            for k in range(fan):
                a = a + jnp.where(ids_ref[k : k + 1, :] == slots, ew_ref[k : k + 1, :], 0.0)
            adj_t[rows_of(i * rb, rb), :] = a.astype(BF)
            return 0

        lax.fori_loop(0, lookup // rb, build, 0)

        def turn(i, _):
            r = rows_of(i * 128, 128)
            adj[:, r] = adj_t[r, :].astype(F32).T.astype(BF)
            return 0

        lax.fori_loop(0, lookup // 128, turn, 0)

    def agg_local(layer):
        src = f_ref if layer == 0 else h1_ref
        for h in range(2):
            cs = slice(h * half, (h + 1) * half)
            zacc[:, cs] = mm(adj[:, :nodes], src[:, cs])

    def mp_copy(k, src, dst):
        return remote(src, dst, mp_sem, (k,), peer)

    def y_exchange(layer, h):
        ref = yf.at[layer, m, :, slice(h * half, (h + 1) * half)]
        return mp_copy(layer * 2 + h, ref, ref)

    def agg_halo(layer):
        parts = halo_finish()
        for h in range(2):
            cs = slice(h * half, (h + 1) * half)
            yf[layer, m, :, cs] = (zacc[:, cs] + mm(adj[:, nodes:], parts[h])).astype(BF)
            y_exchange(layer, h).start()

    def z_own(layer):
        w_copies[layer].wait()

        def first(j, _):
            zacc[:, col(j)] = mm(yf[layer, m], w_ref[layer, rows_of(m * cols, cols), col(j)])
            return 0

        lax.fori_loop(0, tiles, first, 0)
        for h in range(2):
            y_exchange(layer, h).wait_recv()

    def z_other(layer):
        if layer == 1:
            og_copy.wait()
        own_count = jnp.sum(mask_ref[...], axis=0, keepdims=True)
        own_count = jnp.concatenate([own_count] * (ct // 128), axis=1)
        own_inv = 1.0 / jnp.maximum(own_count, 1.0)

        def second(j, _):
            z = zacc[:, col(j)] + mm(
                yf[layer, 1 - m], w_ref[layer, rows_of((1 - m) * cols, cols), col(j)]
            )
            z = z + bias_ref[layer : layer + 1, col(j)]
            sig = jax.nn.sigmoid(z)
            s = z * sig
            s_ref[layer, :, col(j)] = s
            d_ref[layer, :, col(j)] = (sig * (1.0 + z * (1.0 - sig))).astype(BF)
            valid = mask(ct)
            tot = jnp.sum(s * valid, axis=0, keepdims=True)
            cen = s - tot * own_inv
            st_row[0:1, col(j)] = tot
            st_row[1:2, col(j)] = jnp.sum(cen * cen * valid, axis=0, keepdims=True)
            if layer == 0:
                st_row[2:3, col(j)] = own_count
            else:
                pg = og_ref[:, col(j)].astype(F32) * valid
                st_row[2:3, col(j)] = jnp.sum(pg, axis=0, keepdims=True)
                st_row[3:4, col(j)] = jnp.sum(pg * cen, axis=0, keepdims=True)
            return 0

        lax.fori_loop(0, tiles, second, 0)
        buf = stat0 if layer == 0 else stat1
        for k in range(3 if layer == 0 else 4):
            fold(buf, k, k)

    def stats_out(layer):
        stat_start(layer, stat0 if layer == 0 else stat1)
        for h in range(2):
            y_exchange(layer, h).wait_send()
        y_flip(layer)

    def normalize(layer):
        buf = stat0 if layer == 0 else stat1
        stat_finish(layer, buf)
        count = jnp.maximum(total(stat0, 2), 1.0)
        mu = total(buf, 0) / count

        def spread(s, t):
            nc = stat0[s, 2]
            off = buf[s, 0] / jnp.maximum(nc, 1.0) - mu
            return t + buf[s, 1] + nc * off * off

        var = lax.fori_loop(0, n, spread, jnp.zeros_like(mu)) / count
        inv = lax.rsqrt(var + EPS)
        at = 8 if layer == 0 else 4
        unfold(mu, at)
        unfold(inv, at + 1)
        mu_row, inv_row = st_row[at : at + 1, :], st_row[at + 1 : at + 2, :]
        gain_row = gain_ref[layer : layer + 1, :]
        shift_row = shift_ref[layer : layer + 1, :]
        dst = h1_ref if layer == 0 else out_ref
        for j in range(tiles):
            cs = slice(j * ct, (j + 1) * ct)
            x = (s_ref[layer, :, cs] - mu_row[:, cs]) * inv_row[:, cs]
            dst[:, cs] = (mask(ct) * (gain_row[:, cs] * x + shift_row[:, cs])).astype(BF)
        if layer == 0:
            pick(h1_ref)
            return
        out_copy.start()

        def gains(s, t):
            off = stat1[s, 0] / jnp.maximum(stat0[s, 2], 1.0) - mu
            return t + stat1[s, 3] + off * stat1[s, 2]

        unfold(total(stat1, 2), 6)
        unfold(inv * lax.fori_loop(0, n, gains, jnp.zeros_like(mu)), 7)
        unfold(1.0 / count, 10)
        norm_sums(1)
        pre_grad(1)
        fold(stat2, 2, 11)

    def norm_sums(layer):
        gain_out[layer : layer + 1, :] = st_row[7:8, :]
        shift_out[layer : layer + 1, :] = st_row[6:7, :]

    def pre_grad(layer):
        at = 8 if layer == 0 else 4
        grad_src = og_ref if layer == 1 else g_ref

        def pre(j, _):
            gain = gain_ref[layer : layer + 1, col(j)]
            inv_row = st_row[at + 1 : at + 2, col(j)]
            ic = st_row[10:11, col(j)]
            x = (s_ref[layer, :, col(j)] - st_row[at : at + 1, col(j)]) * inv_row
            valid = mask(ct)
            pg = grad_src[:, col(j)].astype(F32) * valid
            ds = (
                valid
                * (inv_row * gain)
                * (pg - st_row[6:7, col(j)] * ic - x * (st_row[7:8, col(j)] * ic))
            )
            dz = (ds * d_ref[layer, :, col(j)].astype(F32)).astype(BF)
            dz_ref[layer, :, col(j)] = dz
            st_row[11:12, col(j)] = jnp.sum(dz.astype(F32), axis=0, keepdims=True)
            return 0

        lax.fori_loop(0, tiles, pre, 0)

    def dy_copy(layer):
        return mp_copy(4 + layer, dy_send, dy_recv.at[layer])

    def dy_other(layer):
        def other(j, _):
            r = rows_of((1 - m) * cols + j * ct, ct)
            dy_send[:, col(j)] = mm_t(dz_ref[layer], w_ref[layer, r, :]).astype(BF)
            return 0

        lax.fori_loop(0, tiles, other, 0)
        dy_copy(layer).start()

    def dy_mine(layer):
        def mine(j, _):
            r = rows_of(m * cols + j * ct, ct)
            dy_own[:, col(j)] = mm_t(dz_ref[layer], w_ref[layer, r, :])
            return 0

        lax.fori_loop(0, tiles, mine, 0)
        dy_copy(layer).wait_recv()
        for j in range(tiles):
            cs = slice(j * ct, (j + 1) * ct)
            dyb[:, cs] = (dy_own[:, cs] + dy_recv[layer, :, cs].astype(F32)).astype(BF)
        back = adj_t[nodes:, :]
        pack_halo(mm(back, dyb[:, :half]), mm(back, dyb[:, half:]))
        halo_start()

    def back_local(layer):
        for h in range(2):
            cs = slice(h * half, (h + 1) * half)
            g_ref[:, cs] = mm(adj_t[:nodes, :], dyb[:, cs])
        dy_copy(layer).wait_send()

    def back_halo(layer):
        parts = halo_finish()
        for h in range(2):
            cs = slice(h * half, (h + 1) * half)
            got = g_ref[:, cs] + mm(sel_t[...], parts[h])
            if layer == 1:
                g_ref[:, cs] = got
                pg = got * mask(half)
                x = (s_ref[0, :, cs] - st_row[8:9, cs]) * st_row[9:10, cs]
                st_row[0:1, cs] = jnp.sum(pg, axis=0, keepdims=True)
                st_row[1:2, cs] = jnp.sum(pg * x, axis=0, keepdims=True)
            else:
                h1_ref[:, cs] = got.astype(BF)
        if layer == 1:
            fold(stat2, 0, 0)
            fold(stat2, 1, 1)
            stat_start(2, stat2)
        else:
            ig_copy.start()

    def back_norm():
        stat_finish(2, stat2)
        unfold(total(stat2, 0), 6)
        unfold(total(stat2, 1), 7)
        unfold(total(stat2, 2), 12)
        norm_sums(0)
        bias_out[1:2, :] = st_row[12:13, :]
        pre_grad(0)
        fold(stat3, 0, 11)
        stat_start(3, stat3)

    table = {
        "A0": lambda: (begin(), agg_local(0), agg_halo(0), z_own(0), z_other(0)),
        "A": lambda: stats_out(0),
        "B0": lambda: normalize(0),
        "B": halo_start,
        "B1": lambda: (agg_local(1), agg_halo(1)),
        "B2": lambda: z_own(1),
        "C": lambda: (z_other(1), stats_out(1)),
        "C2": lambda: normalize(1),
        "C3": lambda: dy_other(1),
        "D": lambda: dy_mine(1),
        "E": lambda: (back_local(1), back_halo(1)),
        "E2": back_norm,
        "E3": lambda: dy_other(0),
        "F": lambda: dy_mine(0),
        "G": lambda: back_local(0),
        "IG": lambda: back_halo(0),
        "ys": lambda l, who, k: y_piece(l, who, k).start(),
        "yf": y_forward,
        "yp": y_pass,
        "ds": lambda l, who, h: dz_piece(l, who, h).start(),
        "df": dz_forward,
        "pr": product,
        "cb": combine,
        "go": gather_own,
        "gf": gather_far,
    }
    for name, *args in SCHEDULE:
        table[name](*args)

    stat_finish(3, stat3)
    unfold(total(stat3, 0), 12)
    bias_out[0:1, :] = st_row[12:13, :]
    out_copy.wait()
    ig_copy.wait()
    for layer in (1, 0):
        y_sent(layer)
        dz_sent(layer)
        for b in range(4):
            gather_finish(layer, b)


def hand_over(
    rows, slots,
    wg_hbm, out_in, ig_in, bias_in, gain_in, shift_in,
    wg_out, out_out, ig_out, bias_out, gain_out, shift_out,
    narrow, wide, through, in_sem, wide_sem, pass_sem,
):
    blocks = narrow.shape[0]
    per_layer = wg_hbm.shape[1] // rows

    def block(ref, i):
        return ref.at[i // per_layer, pl.ds((i % per_layer) * rows, rows), :]

    def read(i):
        return pltpu.make_async_copy(block(wg_hbm, i), narrow.at[i], in_sem.at[i])

    def write(i):
        return pltpu.make_async_copy(wide.at[i % slots], block(wg_out, i), wide_sem.at[i])

    takes = [
        pltpu.make_async_copy(ref, through.at[i], pass_sem.at[0, i])
        for i, ref in enumerate((out_in, ig_in))
    ]
    gives = [
        pltpu.make_async_copy(through.at[i], ref, pass_sem.at[1, i])
        for i, ref in enumerate((out_out, ig_out))
    ]
    for i in range(blocks):
        read(i).start()
        if i == 1:
            for copy in takes:
                copy.start()
    for i in range(blocks):
        read(i).wait()
        if i >= slots:
            write(i - slots).wait()
        wide[i % slots] = narrow[i].astype(F32)
        write(i).start()
        if i == 2:
            for take, give in zip(takes, gives):
                take.wait()
                give.start()
    bias_out[...] = bias_in[...]
    gain_out[...] = gain_in[...]
    shift_out[...] = shift_in[...]
    for i in range(blocks - slots, blocks):
        write(i).wait()
    for give in gives:
        give.wait()


def per_device(
    features, neighbour_ids, edge_weight, self_weight, send_rows, valid_mask,
    weights, biases, norm_gain, norm_shift, output_grad,
):
    nodes, cols = features.shape
    fan = neighbour_ids.shape[1]
    n, cap = send_rows.shape[1], send_rows.shape[2]
    halo = n * cap
    lookup = nodes + halo
    line = n // 4
    half = cols // 2
    vm = pl.BlockSpec(memory_space=pltpu.VMEM)
    anyspace = pl.BlockSpec(memory_space=pl.ANY)
    dma = pltpu.SemaphoreType.DMA
    small = jax.ShapeDtypeStruct((2, cols), F32)
    wide_block = jax.ShapeDtypeStruct((nodes, cols), BF)
    resident = n <= 16
    place = pltpu.VMEM if resident else jax.ShapeDtypeStruct
    out, ig, wg, bias, gain, shift = pl.pallas_call(
        functools.partial(chain, n, cap, fan),
        out_shape=(
            place((nodes, cols), BF), place((nodes, cols), BF), place((2, 2 * cols, cols), BF),
            *[place((2, cols), F32) for _ in range(3)],
        ),
        in_specs=[vm] * 9 + [anyspace] * 2,
        out_specs=(anyspace, anyspace, anyspace, vm, vm, vm),
        scratch_shapes=[
            pltpu.VMEM((2, 2 * cols, cols), BF),
            pltpu.VMEM((nodes, cols), BF),
            pltpu.VMEM((nodes, lookup), BF),
            pltpu.VMEM((lookup, nodes), BF),
            pltpu.VMEM((halo, nodes), BF),
            pltpu.VMEM((nodes, halo), BF),
            pltpu.VMEM((nodes, 128), F32),
            pltpu.VMEM((nodes, cols), BF),
            pltpu.VMEM((2, 2, nodes, cols), BF),
            pltpu.VMEM((2, nodes, cols), F32),
            pltpu.VMEM((2, nodes, cols), BF),
            pltpu.VMEM((nodes, cols), F32),
            pltpu.VMEM((2, nodes, cols), BF),
            pltpu.VMEM((2 * halo, half), BF),
            pltpu.VMEM((2 * halo, half), BF),
            pltpu.VMEM((16, cols), F32),
            pltpu.VMEM((n, 3, 8, cols // 8), F32),
            pltpu.VMEM((n, 4, 8, cols // 8), F32),
            pltpu.VMEM((n, 3, 8, cols // 8), F32),
            pltpu.VMEM((n, 1, 8, cols // 8), F32),
            pltpu.VMEM((2, 2 * cols, nodes), BF),
            pltpu.VMEM((2, 3, cols, nodes), BF),
            pltpu.VMEM((2, 3, 2, nodes, cols // 4), BF),
            pltpu.VMEM((2, 4, half, cols // 4), BF),
            pltpu.VMEM((2, 4, line, half // line, cols // 4), BF),
            pltpu.VMEM((2, 4, half // line, cols // 4), BF),
            dma((2,)), dma, dma((2,)), dma((2, 6)), dma((2, n)), dma((2, 2, n)),
            dma((2, 2, 3, 4)), dma((2, 2, 3)), dma((2, 2, 3, 2)),
            dma((2, 2, 4, line)), dma((2, 2, 4, n // 8)), dma((2, 2, 4, n // 8, 7)), dma((2, 4)),
        ],
        compiler_params=pltpu.CompilerParams(
            collective_id=0,
            has_side_effects=True,
            vmem_limit_bytes=(52 if resident else 62) * 2**20,
        ),
    )(
        features, neighbour_ids.T, edge_weight.T, self_weight.reshape(1, nodes),
        valid_mask.reshape(1, nodes), send_rows.reshape(1, halo), biases, norm_gain, norm_shift,
        output_grad, weights,
    )
    if resident:
        out, ig, wg, bias, gain, shift = (
            pltpu.with_memory_space_constraint(v, pltpu.VMEM)
            for v in (out, ig, wg, bias, gain, shift)
        )
    rows, slots = 512, 4
    blocks = 2 * 2 * cols // rows
    wg, out, ig, bias, gain, shift = pl.pallas_call(
        functools.partial(hand_over, rows, slots),
        out_shape=(
            jax.ShapeDtypeStruct((2, 2 * cols, cols), F32), wide_block, wide_block,
            small, small, small,
        ),
        in_specs=[anyspace] * 3 + [vm] * 3,
        out_specs=(anyspace, anyspace, anyspace, vm, vm, vm),
        scratch_shapes=[
            pltpu.VMEM((blocks, rows, cols), BF),
            pltpu.VMEM((slots, rows, cols), F32),
            pltpu.VMEM((2, nodes, cols), BF),
            dma((blocks,)), dma((blocks,)), dma((2, 2)),
        ],
        compiler_params=pltpu.CompilerParams(vmem_limit_bytes=(40 if resident else 62) * 2**20),
    )(wg, out, ig, bias, gain, shift)
    return out, ig, wg, bias, gain, shift


def solution(mesh):
    return jax.shard_map(
        per_device,
        mesh=mesh,
        in_specs=(
            P("cluster", "mp"),
            P("cluster", None),
            P("cluster", None),
            P("cluster"),
            P("cluster", None, None),
            P("cluster"),
            P(None, None, "mp"),
            P(None, "mp"),
            P(None, "mp"),
            P(None, "mp"),
            P("cluster", "mp"),
        ),
        out_specs=(
            P("cluster", "mp"),
            P("cluster", "mp"),
            P(None, None, "mp"),
            P(None, "mp"),
            P(None, "mp"),
            P(None, "mp"),
        ),
        check_vma=False,
    )
```

```python
import functools

import jax
import jax.numpy as jnp
from jax import lax
from jax.experimental import pallas as pl
from jax.experimental.pallas import tpu as pltpu
from jax.sharding import PartitionSpec as P

EPS = 1e-05
MESH = pl.DeviceIdType.MESH
BF = jnp.bfloat16
F32 = jnp.float32

SCHEDULE = (
    ("A0",),
    ("A",), ("ys", 0, 0, 1), ("ys", 0, 0, 0), ("ys", 0, 1, 0), ("ys", 0, 1, 2),
    ("B0",),
    ("B",), ("ys", 0, 1, 1), ("ys", 0, 0, 3), ("yf", 0, 2), ("ys", 0, 1, 3),
    ("B1",), ("yf", 0, 1),
    ("B2",),
    ("C",), ("yf", 0, 0), ("yf", 0, 3), ("ys", 1, 0, 3), ("ys", 1, 1, 1), ("ys", 1, 0, 2), ("ys", 1, 1, 0),
    ("ys", 1, 1, 2),
    ("C2",), ("ds", 1, 1, 0),
    ("C3",), ("ys", 1, 0, 0),
    ("D",), ("ys", 1, 0, 1), ("yf", 1, 3), ("yf", 1, 0), ("df", 1, 0), ("yf", 1, 1),
    ("E",), ("ds", 1, 0, 0), ("yp", 0, 2), ("ys", 1, 1, 3), ("yf", 1, 2),
    ("E2",), ("ys", 0, 0, 2), ("ds", 1, 0, 1), ("ds", 1, 1, 1), ("yp", 1, 1), ("yp", 1, 0), ("ds", 0, 1, 0),
    ("yp", 1, 2), ("pr", 1, 0), ("yp", 0, 1), ("pr", 1, 2), ("df", 1, 1), ("ds", 0, 1, 1), ("cb", 1, 0),
    ("ds", 0, 0, 1), ("cb", 1, 2), ("pr", 1, 1), ("go", 1, 0, 1), ("gf", 1, 0, 0), ("ds", 0, 0, 0), ("df", 0, 1),
    ("gf", 1, 2, 0), ("pr", 1, 3), ("df", 0, 0), ("gf", 1, 0, 1), ("cb", 1, 1), ("go", 1, 0, 2), ("yp", 0, 0),
    ("go", 1, 2, 1), ("gf", 1, 2, 1), ("cb", 1, 3), ("go", 1, 1, 1), ("pr", 0, 3), ("gf", 1, 0, 2), ("pr", 0, 1),
    ("gf", 1, 2, 2), ("gf", 1, 1, 0), ("gf", 1, 3, 0),
    ("E3",),
    ("F",), ("cb", 0, 3),
    ("G",), ("go", 1, 3, 1), ("go", 1, 1, 2), ("gf", 1, 1, 1), ("cb", 0, 1), ("go", 1, 3, 2), ("gf", 1, 3, 1),
    ("go", 0, 3, 1), ("go", 0, 1, 1), ("pr", 0, 0), ("gf", 1, 3, 2), ("gf", 1, 1, 2), ("gf", 0, 3, 0),
    ("go", 1, 2, 2), ("go", 0, 1, 2), ("pr", 0, 2), ("cb", 0, 0), ("gf", 0, 1, 0), ("cb", 0, 2), ("gf", 0, 3, 1),
    ("go", 0, 2, 1), ("gf", 0, 0, 0), ("gf", 0, 2, 0), ("gf", 0, 1, 1), ("go", 0, 0, 1), ("go", 0, 3, 2),
    ("gf", 0, 2, 1), ("gf", 0, 0, 1), ("go", 0, 2, 2), ("go", 0, 0, 2), ("gf", 0, 1, 2),
    ("IG",), ("gf", 0, 0, 2), ("gf", 0, 2, 2), ("gf", 0, 3, 2),
)
ORDERS = (
    (
        ((4, 2, 1), (4, 2, 1)),
        ((1, 4, 2), (4, 1, 2)),
        ((1, 2, 4), (4, 1, 2)),
        ((2, 1, 4), (2, 1, 4)),
    ),
    (
        ((4, 2, 1), (4, 2, 1)),
        ((4, 1, 2), (2, 4, 1)),
        ((4, 2, 1), (4, 1, 2)),
        ((4, 1, 2), (4, 1, 2)),
    ),
)


def mm(a, b):
    return jnp.dot(a, b, preferred_element_type=F32)


def mm_t(a, b):
    return lax.dot_general(a, b, (((1,), (1,)), ((), ())), preferred_element_type=F32)


def chain(
    n, cap, fan,
    f_hbm, rows_hbm, ids_hbm, ew_hbm, sw_hbm, valid_hbm, bias_hbm, gain_hbm, shift_hbm, og_hbm, w_hbm,
    out_hbm, ig_hbm, wg_hbm, bias_res, gain_res, shift_res,
    f_ref, rows_ref, ids_ref, ew_ref, sw_ref, valid_ref, bias_ref, gain_ref, shift_ref,
    bias_out, gain_out, shift_out, rows_row, in_sem,
    w_ref, og_ref, adj, adj_t, sel, sel_t, mask_ref, h1_ref, yf, s_ref, d_ref, zacc,
    dy_recv, hsend, hrecv, st_row, stat0, stat1, stat2, stat3,
    yt, yr, dzr, wpart, zr, fin,
    w_sem, og_sem, out_sem, mp_sem, h_sem, x_sem,
    y_sem, yp_sem, dz_sem, zr_sem, az_sem, ag_sem, fin_sem,
):
    nodes, cols = f_hbm.shape
    ct = 256
    tiles = cols // ct
    half = cols // 2
    c = lax.axis_index("cluster")
    m = lax.axis_index("mp")
    peer = (c, 1 - m)
    halo = n * cap
    lookup = nodes + halo
    line, far = n // 4, n // 8
    zi, p = c // 4, c % 4
    px, py = p % 2, p // 2
    near = (c + 1 - 2 * px, c + 2 - 4 * py)
    rc = half // line
    dy_own, dyb, g_ref = zacc, og_ref, s_ref.at[1]
    out_ref, dy_send, dz_ref = yf.at[0, 0], yf.at[0, 1], yf.at[1]
    pieces = 4
    prow = half // pieces
    lanes = cols // 8
    kept = {}

    def rows_of(start, size):
        return pl.ds(pl.multiple_of(start, size), size)

    def col(j):
        return rows_of(j * ct, ct)

    def remote(src, dst, sems, idx, to):
        return pltpu.make_async_remote_copy(
            src_ref=src,
            dst_ref=dst,
            send_sem=sems.at[(0, *idx)],
            recv_sem=sems.at[(1, *idx)],
            device_id=to,
            device_id_type=MESH,
        )

    def mask(width):
        return jnp.concatenate([mask_ref[...]] * (width // 128), axis=1)

    def halo_part(d):
        return rows_of(d * 2 * cap, 2 * cap)

    def pack_halo(left, right):
        both = jnp.concatenate(
            [left.reshape(n, cap, half), right.reshape(n, cap, half)], axis=1
        )
        hsend[...] = both.reshape(n * 2 * cap, half).astype(BF)

    def halo_copy(to, frm):
        return pltpu.make_async_remote_copy(
            src_ref=hsend.at[halo_part(to)],
            dst_ref=hrecv.at[halo_part(frm)],
            send_sem=h_sem.at[0, to],
            recv_sem=h_sem.at[1, frm],
            device_id=(to, m),
            device_id_type=MESH,
        )

    def halo_start():
        def send(i, _):
            halo_copy(lax.rem(c + i, n), c).start()
            return 0

        lax.fori_loop(1, n, send, 0)
        hrecv[halo_part(c)] = hsend[halo_part(c)]

    def halo_finish():
        def finish(i, _):
            s = lax.rem(c + i, n)
            copy = halo_copy(s, s)
            copy.wait_recv()
            copy.wait_send()
            return 0

        lax.fori_loop(1, n, finish, 0)
        got = hrecv[...].astype(F32).reshape(n, 2 * cap, half)
        left = got[:, :cap, :].reshape(halo, half).astype(BF)
        right = got[:, cap:, :].reshape(halo, half).astype(BF)
        return left, right

    def pick(src):
        pack_halo(mm(sel[...], src[:, :half]), mm(sel[...], src[:, half:]))

    def stat_copy(e, buf, to, frm):
        return pltpu.make_async_remote_copy(
            src_ref=buf.at[c],
            dst_ref=buf.at[frm],
            send_sem=x_sem.at[0, e % 2, to],
            recv_sem=x_sem.at[1, e % 2, frm],
            device_id=(to, m),
            device_id_type=MESH,
        )

    def stat_start(e, buf):
        def send(i, _):
            stat_copy(e, buf, lax.rem(c + i, n), c).start()
            return 0

        lax.fori_loop(1, n, send, 0)

    def stat_finish(e, buf):
        def finish(i, _):
            s = lax.rem(c + i, n)
            copy = stat_copy(e, buf, s, s)
            copy.wait_recv()
            copy.wait_send()
            return 0

        lax.fori_loop(1, n, finish, 0)

    def fold(buf, k, row):
        for g in range(8):
            buf[c, k, g : g + 1, :] = st_row[row : row + 1, g * lanes : (g + 1) * lanes]

    def unfold(tile, row):
        for g in range(8):
            st_row[row : row + 1, g * lanes : (g + 1) * lanes] = tile[g : g + 1, :]

    def total(buf, k):
        return lax.fori_loop(1, n, lambda s, t: t + buf[s, k], buf[0, k])

    def quarter(layer, who):
        qx = 1 - px if who in (0, 2) else px
        qy = 1 - py if who in (1, 2) else py
        return (qx, qy) if layer == 1 else (qy, qx)

    def y_flip(layer):
        def flip(i, _):
            r = rows_of(i * 128, 128)
            for h in range(2):
                yt[layer, rows_of(h * cols + i * 128, 128), :] = (
                    yf[layer, h, :, r].astype(F32).T.astype(BF)
                )
            return 0

        lax.fori_loop(0, cols // 128, flip, 0)

    def y_piece(layer, who, k):
        hr, _ = quarter(layer, who)
        return remote(
            yt.at[layer, rows_of(hr * cols + m * half + k * prow, prow), :],
            yr.at[layer, who, rows_of(m * half + k * prow, prow), :],
            y_sem, (layer, who, k), (near[who], m),
        )

    def y_first(layer):
        return 1 - layer

    def z_first(layer):
        return layer

    def y_relay(layer, k):
        first = y_first(layer)
        r = rows_of(m * half + k * prow, prow)
        return remote(
            yr.at[layer, first, r, :], yr.at[layer, 2, r, :], y_sem, (layer, 2, k),
            (near[1 - first], m),
        )

    def y_forward(layer, k):
        y_piece(layer, y_first(layer), k).wait_recv()
        y_relay(layer, k).start()

    def y_pass_copy(layer, who, part):
        r = rows_of(part * half, half)
        return remote(
            yr.at[layer, who, r, :], yr.at[layer, who, r, :], yp_sem, (layer, who), peer
        )

    def y_pass(layer, who):
        if who != y_first(layer):
            for k in range(pieces):
                copy = y_relay(layer, k) if who == 2 else y_piece(layer, who, k)
                copy.wait_recv()
        y_pass_copy(layer, who, m).start()

    def y_sent(layer):
        for k in range(pieces):
            y_piece(layer, 0, k).wait_send()
            y_piece(layer, 1, k).wait_send()
            y_relay(layer, k).wait_send()
        for who in range(3):
            y_pass_copy(layer, who, m).wait_send()

    def dz_piece(layer, who, h):
        _, hc = quarter(layer, who)
        return remote(
            dz_ref.at[layer, :, rows_of(hc * half + h * ct, ct)],
            dzr.at[layer, who, h],
            dz_sem, (layer, who, h), (near[who], m),
        )

    def dz_relay(layer, h):
        first = z_first(layer)
        return remote(
            dzr.at[layer, first, h], dzr.at[layer, 2, h], dz_sem, (layer, 2, h),
            (near[1 - first], m),
        )

    def dz_forward(layer, h):
        dz_piece(layer, z_first(layer), h).wait_recv()
        dz_relay(layer, h).start()

    def dz_sent(layer):
        for h in range(2):
            dz_piece(layer, 0, h).wait_send()
            dz_piece(layer, 1, h).wait_send()
            dz_relay(layer, h).wait_send()

    def part(b):
        return m if b < 2 else 1 - m

    def line_copy(layer, b, to, frm):
        return pltpu.make_async_remote_copy(
            src_ref=wpart.at[layer, b, rows_of(to * rc, rc), :],
            dst_ref=zr.at[layer, b, frm],
            send_sem=zr_sem.at[0, layer, b, to],
            recv_sem=zr_sem.at[1, layer, b, frm],
            device_id=(to * 4 + p, m),
            device_id_type=MESH,
        )

    def once(key):
        fresh = key not in kept
        kept[key] = True
        return fresh

    def product(layer, b):
        hr, hc = quarter(layer, 3)
        h = b % 2
        if b >= 2 and once(("y", layer)):
            for who in range(3):
                y_pass_copy(layer, who, 1 - m).wait_recv()
        if once(("dz", layer, h)):
            dz_piece(layer, 1 - z_first(layer), h).wait_recv()
            dz_relay(layer, h).wait_recv()
        own_dz = dz_ref[layer, :, rows_of(hc * half + h * ct, ct)]

        def one(i, _):
            start = part(b) * half + i * ct
            acc = mm(yt[layer, rows_of(hr * cols + start, ct), :], own_dz)
            for who in range(3):
                acc = acc + mm(yr[layer, who, rows_of(start, ct), :], dzr[layer, who, h])
            wpart[layer, b, rows_of(i * ct, ct), :] = acc.astype(BF)
            return 0

        lax.fori_loop(0, half // ct, one, 0)

        def send(i, _):
            line_copy(layer, b, (zi + i) % line, zi).start()
            return 0

        lax.fori_loop(1, line, send, 0)

    def flip_bit(e, d):
        return e + d - 2 * d * ((e // d) % 2)

    def spot(layer, b, e):
        ex, ey = e % 2, (e // 2) % 2
        hr, hc = (ex, ey) if layer == 1 else (ey, ex)
        return wg_hbm.at[
            layer,
            rows_of(hr * cols + part(b) * half + (e // 4) * rc, rc),
            rows_of(hc * half + (b % 2) * ct, ct),
        ]

    def held(base, dims):
        got = [base]
        for d in dims:
            got = got + [flip_bit(e, d) for e in got]
        return got

    def far_copy(layer, b, to, frm):
        return pltpu.make_async_remote_copy(
            src_ref=fin.at[layer, b],
            dst_ref=spot(layer, b, frm),
            send_sem=az_sem.at[0, layer, b, to // 8],
            recv_sem=az_sem.at[1, layer, b, frm // 8],
            device_id=(to, m),
            device_id_type=MESH,
        )

    def hops(layer, b, i, step, arriving):
        own = isinstance(i, int)
        dims = ORDERS[layer][b][0 if own else 1]
        base = (c + 8 * i) % n
        other = flip_bit(c, dims[step])
        slot = 2**step - 1
        copies = []
        for j, e in enumerate(held(base, dims[:step])):
            if arriving:
                e = flip_bit(e, dims[step])
            src = fin.at[layer, b] if own and j == 0 and not arriving else spot(layer, b, e)
            copies.append(
                remote(src, spot(layer, b, e), ag_sem, (layer, b, base // 8, slot + j), (other, m))
            )
        return copies

    def keep(layer, b):
        return pltpu.make_async_copy(
            fin.at[layer, b], spot(layer, b, c), fin_sem.at[layer, b]
        )

    def combine(layer, b):
        def take(i, _):
            frm = (zi + i) % line
            copy = line_copy(layer, b, frm, frm)
            copy.wait_recv()
            copy.wait_send()
            return 0

        lax.fori_loop(1, line, take, 0)
        zr[layer, b, zi] = wpart[layer, b, rows_of(zi * rc, rc), :]
        fin[layer, b] = lax.fori_loop(
            1, line,
            lambda j, t: t + zr[layer, b, j].astype(F32),
            zr[layer, b, 0].astype(F32),
        ).astype(BF)
        keep(layer, b).start()

        def send(i, _):
            far_copy(layer, b, (c + 8 * i) % n, c).start()
            return 0

        lax.fori_loop(1, far, send, 0)
        gather_own(layer, b, 0)

    def gather_own(layer, b, step):
        if step > 0:
            for copy in hops(layer, b, 0, step - 1, True):
                copy.wait_recv()
        for copy in hops(layer, b, 0, step, False):
            copy.start()
        if step > 0:
            for copy in hops(layer, b, 0, step - 1, False):
                copy.wait_send()

    def gather_far(layer, b, step):
        def one(i, _):
            if step == 0:
                frm = (c + 8 * i) % n
                far_copy(layer, b, frm, frm).wait_recv()
            else:
                for copy in hops(layer, b, i, step - 1, True):
                    copy.wait_recv()
            for copy in hops(layer, b, i, step, False):
                copy.start()
            if step > 0:
                for copy in hops(layer, b, i, step - 1, False):
                    copy.wait_send()
            return 0

        lax.fori_loop(1, far, one, 0)

    def gather_finish(layer, b):
        keep(layer, b).wait()

        def ends(i):
            for copy in hops(layer, b, i, 2, True):
                copy.wait_recv()
            for copy in hops(layer, b, i, 2, False):
                copy.wait_send()

        def one(i, _):
            far_copy(layer, b, (c + 8 * i) % n, c).wait_send()
            ends(i)
            return 0

        ends(0)
        lax.fori_loop(1, far, one, 0)

    w_copies = [
        pltpu.make_async_copy(w_hbm.at[layer], w_ref.at[layer], w_sem.at[layer])
        for layer in range(2)
    ]
    og_copy = pltpu.make_async_copy(og_hbm, og_ref, og_sem)
    in_copies = [
        pltpu.make_async_copy(src, dst, in_sem.at[i])
        for i, (src, dst) in enumerate(
            (
                (rows_hbm, rows_ref), (f_hbm, f_ref), (ids_hbm, ids_ref), (ew_hbm, ew_ref),
                (sw_hbm, sw_ref), (valid_hbm, valid_ref), (bias_hbm, bias_ref),
                (gain_hbm, gain_ref), (shift_hbm, shift_ref),
            )
        )
    ]
    small_copies = [
        pltpu.make_async_copy(src, dst, out_sem.at[2 + i])
        for i, (src, dst) in enumerate(
            ((bias_out, bias_res), (gain_out, gain_res), (shift_out, shift_res))
        )
    ]
    out_copy = pltpu.make_async_copy(out_ref, out_hbm, out_sem.at[0])
    ig_copy = pltpu.make_async_copy(h1_ref, ig_hbm, out_sem.at[1])

    def begin():
        for copy in in_copies:
            copy.start()
        barrier = pltpu.get_barrier_semaphore()

        def greet(i, _):
            pl.semaphore_signal(
                barrier, inc=1, device_id=(lax.rem(c + i, n), m), device_id_type=MESH
            )
            return 0

        lax.fori_loop(1, n, greet, 0)
        pl.semaphore_signal(barrier, inc=1, device_id=peer, device_id_type=MESH)
        w_copies[0].start()
        og_copy.start()
        w_copies[1].start()

        in_copies[0].wait()
        lane = lax.broadcasted_iota(jnp.int32, (cap, halo), 1)
        spread = jnp.zeros((cap, halo), F32)
        for d in range(n):
            mine = rows_ref[0, :, d : d + 1].astype(F32)
            spread = jnp.where((lane >= d * cap) & (lane < (d + 1) * cap), mine, spread)
        place_q = lax.broadcasted_iota(jnp.int32, (cap, halo), 0)
        wanted = jnp.sum(jnp.where(lane % cap == place_q, spread, 0.0), axis=0, keepdims=True)
        rows_row[...] = wanted.astype(jnp.int32)

        def choose(i, _):
            r = rows_of(i * 128, 128)
            one_hot = jnp.where(
                rows_row[:, r] == lax.broadcasted_iota(jnp.int32, (nodes, 128), 0), 1.0, 0.0
            )
            sel_t[:, r] = one_hot.astype(BF)
            sel[r, :] = one_hot.T.astype(BF)
            return 0

        lax.fori_loop(0, halo // 128, choose, 0)
        in_copies[1].wait()
        pick(f_ref)
        pl.semaphore_wait(barrier, n)
        halo_start()
        for copy in in_copies[2:]:
            copy.wait()
        mask_ref[...] = jnp.broadcast_to(valid_ref[...].astype(F32), (128, nodes)).T
        rb = 16
        place = lax.broadcasted_iota(jnp.int32, (rb, nodes), 0)
        node = lax.broadcasted_iota(jnp.int32, (rb, nodes), 1)

        def build(i, _):
            slots = place + i * rb
            a = jnp.where(node == slots, 2.0 * sw_ref[...], 0.0)
            for k in range(fan):
                a = a + jnp.where(ids_ref[k : k + 1, :] == slots, ew_ref[k : k + 1, :], 0.0)
            adj_t[rows_of(i * rb, rb), :] = a.astype(BF)
            return 0

        lax.fori_loop(0, lookup // rb, build, 0)

        def turn(i, _):
            r = rows_of(i * 128, 128)
            adj[:, r] = adj_t[r, :].astype(F32).T.astype(BF)
            return 0

        lax.fori_loop(0, lookup // 128, turn, 0)

    def agg_local(layer):
        src = f_ref if layer == 0 else h1_ref
        for h in range(2):
            cs = slice(h * half, (h + 1) * half)
            zacc[:, cs] = mm(adj[:, :nodes], src[:, cs])

    def mp_copy(k, src, dst):
        return remote(src, dst, mp_sem, (k,), peer)

    def y_exchange(layer, h):
        ref = yf.at[layer, m, :, slice(h * half, (h + 1) * half)]
        return mp_copy(layer * 2 + h, ref, ref)

    def agg_halo(layer):
        parts = halo_finish()
        for h in range(2):
            cs = slice(h * half, (h + 1) * half)
            yf[layer, m, :, cs] = (zacc[:, cs] + mm(adj[:, nodes:], parts[h])).astype(BF)
            y_exchange(layer, h).start()

    def z_own(layer):
        w_copies[layer].wait()

        zacc[...] = mm(yf[layer, m], w_ref[layer, rows_of(m * cols, cols), :])
        for h in range(2):
            y_exchange(layer, h).wait_recv()

    def z_other(layer):
        if layer == 1:
            og_copy.wait()
        own_count = jnp.sum(mask_ref[...], axis=0, keepdims=True)
        own_count = jnp.concatenate([own_count] * (ct // 128), axis=1)
        own_inv = 1.0 / jnp.maximum(own_count, 1.0)

        zacc[...] += mm(yf[layer, 1 - m], w_ref[layer, rows_of((1 - m) * cols, cols), :])

        def second(j, _):
            z = zacc[:, col(j)] + bias_ref[layer : layer + 1, col(j)]
            sig = jax.nn.sigmoid(z)
            s = z * sig
            s_ref[layer, :, col(j)] = s
            d_ref[layer, :, col(j)] = (sig * (1.0 + z * (1.0 - sig))).astype(BF)
            valid = mask(ct)
            tot = jnp.sum(s * valid, axis=0, keepdims=True)
            cen = s - tot * own_inv
            st_row[0:1, col(j)] = tot
            st_row[1:2, col(j)] = jnp.sum(cen * cen * valid, axis=0, keepdims=True)
            if layer == 0:
                st_row[2:3, col(j)] = own_count
            else:
                pg = og_ref[:, col(j)].astype(F32) * valid
                st_row[2:3, col(j)] = jnp.sum(pg, axis=0, keepdims=True)
                st_row[3:4, col(j)] = jnp.sum(pg * cen, axis=0, keepdims=True)
            return 0

        lax.fori_loop(0, tiles, second, 0)
        buf = stat0 if layer == 0 else stat1
        for k in range(3 if layer == 0 else 4):
            fold(buf, k, k)

    def stats_out(layer):
        stat_start(layer, stat0 if layer == 0 else stat1)
        for h in range(2):
            y_exchange(layer, h).wait_send()
        y_flip(layer)

    def normalize(layer):
        buf = stat0 if layer == 0 else stat1
        stat_finish(layer, buf)
        count = jnp.maximum(total(stat0, 2), 1.0)
        mu = total(buf, 0) / count

        def spread(s, t):
            nc = stat0[s, 2]
            off = buf[s, 0] / jnp.maximum(nc, 1.0) - mu
            return t + buf[s, 1] + nc * off * off

        var = lax.fori_loop(0, n, spread, jnp.zeros_like(mu)) / count
        inv = lax.rsqrt(var + EPS)
        at = 8 if layer == 0 else 4
        unfold(mu, at)
        unfold(inv, at + 1)
        mu_row, inv_row = st_row[at : at + 1, :], st_row[at + 1 : at + 2, :]
        gain_row = gain_ref[layer : layer + 1, :]
        shift_row = shift_ref[layer : layer + 1, :]
        dst = h1_ref if layer == 0 else out_ref
        for j in range(tiles):
            cs = slice(j * ct, (j + 1) * ct)
            x = (s_ref[layer, :, cs] - mu_row[:, cs]) * inv_row[:, cs]
            dst[:, cs] = (mask(ct) * (gain_row[:, cs] * x + shift_row[:, cs])).astype(BF)
        if layer == 0:
            pick(h1_ref)
            return
        out_copy.start()

        def gains(s, t):
            off = stat1[s, 0] / jnp.maximum(stat0[s, 2], 1.0) - mu
            return t + stat1[s, 3] + off * stat1[s, 2]

        unfold(total(stat1, 2), 6)
        unfold(inv * lax.fori_loop(0, n, gains, jnp.zeros_like(mu)), 7)
        unfold(1.0 / count, 10)
        norm_sums(1)
        pre_grad(1)
        fold(stat2, 2, 11)

    def norm_sums(layer):
        gain_out[layer : layer + 1, :] = st_row[7:8, :]
        shift_out[layer : layer + 1, :] = st_row[6:7, :]

    def pre_grad(layer):
        at = 8 if layer == 0 else 4
        grad_src = og_ref if layer == 1 else g_ref

        def pre(j, _):
            gain = gain_ref[layer : layer + 1, col(j)]
            inv_row = st_row[at + 1 : at + 2, col(j)]
            ic = st_row[10:11, col(j)]
            x = (s_ref[layer, :, col(j)] - st_row[at : at + 1, col(j)]) * inv_row
            valid = mask(ct)
            pg = grad_src[:, col(j)].astype(F32) * valid
            ds = (
                valid
                * (inv_row * gain)
                * (pg - st_row[6:7, col(j)] * ic - x * (st_row[7:8, col(j)] * ic))
            )
            dz = (ds * d_ref[layer, :, col(j)].astype(F32)).astype(BF)
            dz_ref[layer, :, col(j)] = dz
            st_row[11:12, col(j)] = jnp.sum(dz.astype(F32), axis=0, keepdims=True)
            return 0

        lax.fori_loop(0, tiles, pre, 0)

    def dy_copy(layer):
        return mp_copy(4 + layer, dy_send, dy_recv.at[layer])

    def dy_other(layer):
        theirs = w_ref[layer, rows_of((1 - m) * cols, cols), :]
        dy_send[...] = mm_t(dz_ref[layer], theirs).astype(BF)
        dy_copy(layer).start()

    def dy_mine(layer):
        dy_own[...] = mm_t(dz_ref[layer], w_ref[layer, rows_of(m * cols, cols), :])
        dy_copy(layer).wait_recv()
        for j in range(tiles):
            cs = slice(j * ct, (j + 1) * ct)
            dyb[:, cs] = (dy_own[:, cs] + dy_recv[layer, :, cs].astype(F32)).astype(BF)
        back = adj_t[nodes:, :]
        pack_halo(mm(back, dyb[:, :half]), mm(back, dyb[:, half:]))
        halo_start()

    def back_local(layer):
        for h in range(2):
            cs = slice(h * half, (h + 1) * half)
            g_ref[:, cs] = mm(adj_t[:nodes, :], dyb[:, cs])
        dy_copy(layer).wait_send()

    def back_halo(layer):
        parts = halo_finish()
        for h in range(2):
            cs = slice(h * half, (h + 1) * half)
            got = g_ref[:, cs] + mm(sel_t[...], parts[h])
            if layer == 1:
                g_ref[:, cs] = got
                pg = got * mask(half)
                x = (s_ref[0, :, cs] - st_row[8:9, cs]) * st_row[9:10, cs]
                st_row[0:1, cs] = jnp.sum(pg, axis=0, keepdims=True)
                st_row[1:2, cs] = jnp.sum(pg * x, axis=0, keepdims=True)
            else:
                h1_ref[:, cs] = got.astype(BF)
        if layer == 1:
            fold(stat2, 0, 0)
            fold(stat2, 1, 1)
            stat_start(2, stat2)
        else:
            ig_copy.start()

    def back_norm():
        stat_finish(2, stat2)
        unfold(total(stat2, 0), 6)
        unfold(total(stat2, 1), 7)
        unfold(total(stat2, 2), 12)
        norm_sums(0)
        bias_out[1:2, :] = st_row[12:13, :]
        pre_grad(0)
        fold(stat3, 0, 11)
        stat_start(3, stat3)

    table = {
        "A0": lambda: (begin(), agg_local(0), agg_halo(0), z_own(0), z_other(0)),
        "A": lambda: stats_out(0),
        "B0": lambda: normalize(0),
        "B": halo_start,
        "B1": lambda: (agg_local(1), agg_halo(1)),
        "B2": lambda: z_own(1),
        "C": lambda: (z_other(1), stats_out(1)),
        "C2": lambda: normalize(1),
        "C3": lambda: dy_other(1),
        "D": lambda: dy_mine(1),
        "E": lambda: (back_local(1), back_halo(1)),
        "E2": back_norm,
        "E3": lambda: dy_other(0),
        "F": lambda: dy_mine(0),
        "G": lambda: back_local(0),
        "IG": lambda: back_halo(0),
        "ys": lambda l, who, k: y_piece(l, who, k).start(),
        "yf": y_forward,
        "yp": y_pass,
        "ds": lambda l, who, h: dz_piece(l, who, h).start(),
        "df": dz_forward,
        "pr": product,
        "cb": combine,
        "go": gather_own,
        "gf": gather_far,
    }
    for name, *args in SCHEDULE:
        table[name](*args)

    stat_finish(3, stat3)
    unfold(total(stat3, 0), 12)
    bias_out[0:1, :] = st_row[12:13, :]
    for copy in small_copies:
        copy.start()
    out_copy.wait()
    ig_copy.wait()
    for layer in (1, 0):
        y_sent(layer)
        dz_sent(layer)
        for b in range(4):
            gather_finish(layer, b)
    for copy in small_copies:
        copy.wait()


def hand_over(
    rows, slots,
    wg_hbm, out_in, ig_in, bias_in, gain_in, shift_in,
    wg_out, out_out, ig_out, bias_out, gain_out, shift_out,
    narrow, wide, through, in_sem, wide_sem, pass_sem,
):
    blocks = narrow.shape[0]
    per_layer = wg_hbm.shape[1] // rows

    def block(ref, i):
        return ref.at[i // per_layer, pl.ds((i % per_layer) * rows, rows), :]

    def read(i):
        return pltpu.make_async_copy(block(wg_hbm, i), narrow.at[i], in_sem.at[i])

    def write(i):
        return pltpu.make_async_copy(wide.at[i % slots], block(wg_out, i), wide_sem.at[i])

    takes = [
        pltpu.make_async_copy(ref, through.at[i], pass_sem.at[0, i])
        for i, ref in enumerate((out_in, ig_in))
    ]
    gives = [
        pltpu.make_async_copy(through.at[i], ref, pass_sem.at[1, i])
        for i, ref in enumerate((out_out, ig_out))
    ]
    for i in range(blocks):
        read(i).start()
        if i == 1:
            for copy in takes:
                copy.start()
    for i in range(blocks):
        read(i).wait()
        if i >= slots:
            write(i - slots).wait()
        wide[i % slots] = narrow[i].astype(F32)
        write(i).start()
        if i == 2:
            for take, give in zip(takes, gives):
                take.wait()
                give.start()
    bias_out[...] = bias_in[...]
    gain_out[...] = gain_in[...]
    shift_out[...] = shift_in[...]
    for i in range(blocks - slots, blocks):
        write(i).wait()
    for give in gives:
        give.wait()


def per_device(
    features, neighbour_ids, edge_weight, self_weight, send_rows, valid_mask,
    weights, biases, norm_gain, norm_shift, output_grad,
):
    nodes, cols = features.shape
    fan = neighbour_ids.shape[1]
    n, cap = send_rows.shape[1], send_rows.shape[2]
    halo = n * cap
    lookup = nodes + halo
    line = n // 4
    half = cols // 2
    vm = pl.BlockSpec(memory_space=pltpu.VMEM)
    anyspace = pl.BlockSpec(memory_space=pl.ANY)
    dma = pltpu.SemaphoreType.DMA
    small = jax.ShapeDtypeStruct((2, cols), F32)
    wide_block = jax.ShapeDtypeStruct((nodes, cols), BF)
    resident = n <= 16
    place = pltpu.VMEM if resident else jax.ShapeDtypeStruct
    out, ig, wg, bias, gain, shift = pl.pallas_call(
        functools.partial(chain, n, cap, fan),
        out_shape=(
            place((nodes, cols), BF), place((nodes, cols), BF), place((2, 2 * cols, cols), BF),
            *[place((2, cols), F32) for _ in range(3)],
        ),
        in_specs=[anyspace] * 11,
        out_specs=(anyspace,) * 6,
        scratch_shapes=[
            pltpu.VMEM((nodes, cols), BF),
            pltpu.VMEM((1, cap, n), jnp.int32),
            pltpu.VMEM((fan, nodes), jnp.int32),
            pltpu.VMEM((fan, nodes), F32),
            pltpu.VMEM((1, nodes), F32),
            pltpu.VMEM((1, nodes), jnp.int32),
            *[pltpu.VMEM((2, cols), F32) for _ in range(6)],
            pltpu.VMEM((1, halo), jnp.int32),
            dma((9,)),
            pltpu.VMEM((2, 2 * cols, cols), BF),
            pltpu.VMEM((nodes, cols), BF),
            pltpu.VMEM((nodes, lookup), BF),
            pltpu.VMEM((lookup, nodes), BF),
            pltpu.VMEM((halo, nodes), BF),
            pltpu.VMEM((nodes, halo), BF),
            pltpu.VMEM((nodes, 128), F32),
            pltpu.VMEM((nodes, cols), BF),
            pltpu.VMEM((2, 2, nodes, cols), BF),
            pltpu.VMEM((2, nodes, cols), F32),
            pltpu.VMEM((2, nodes, cols), BF),
            pltpu.VMEM((nodes, cols), F32),
            pltpu.VMEM((2, nodes, cols), BF),
            pltpu.VMEM((2 * halo, half), BF),
            pltpu.VMEM((2 * halo, half), BF),
            pltpu.VMEM((16, cols), F32),
            pltpu.VMEM((n, 3, 8, cols // 8), F32),
            pltpu.VMEM((n, 4, 8, cols // 8), F32),
            pltpu.VMEM((n, 3, 8, cols // 8), F32),
            pltpu.VMEM((n, 1, 8, cols // 8), F32),
            pltpu.VMEM((2, 2 * cols, nodes), BF),
            pltpu.VMEM((2, 3, cols, nodes), BF),
            pltpu.VMEM((2, 3, 2, nodes, cols // 4), BF),
            pltpu.VMEM((2, 4, half, cols // 4), BF),
            pltpu.VMEM((2, 4, line, half // line, cols // 4), BF),
            pltpu.VMEM((2, 4, half // line, cols // 4), BF),
            dma((2,)), dma, dma((5,)), dma((2, 6)), dma((2, n)), dma((2, 2, n)),
            dma((2, 2, 3, 4)), dma((2, 2, 3)), dma((2, 2, 3, 2)),
            dma((2, 2, 4, line)), dma((2, 2, 4, n // 8)), dma((2, 2, 4, n // 8, 7)), dma((2, 4)),
        ],
        compiler_params=pltpu.CompilerParams(
            collective_id=0,
            has_side_effects=True,
            vmem_limit_bytes=(52 if resident else 62) * 2**20,
        ),
    )(
        features, jnp.swapaxes(send_rows, 1, 2), neighbour_ids.T, edge_weight.T,
        self_weight.reshape(1, nodes), valid_mask.reshape(1, nodes), biases, norm_gain, norm_shift,
        output_grad, weights,
    )
    if resident:
        out, ig, wg, bias, gain, shift = (
            pltpu.with_memory_space_constraint(v, pltpu.VMEM)
            for v in (out, ig, wg, bias, gain, shift)
        )
    rows, slots = 512, 4
    blocks = 2 * 2 * cols // rows
    wg, out, ig, bias, gain, shift = pl.pallas_call(
        functools.partial(hand_over, rows, slots),
        out_shape=(
            jax.ShapeDtypeStruct((2, 2 * cols, cols), F32), wide_block, wide_block,
            small, small, small,
        ),
        in_specs=[anyspace] * 3 + [vm] * 3,
        out_specs=(anyspace, anyspace, anyspace, vm, vm, vm),
        scratch_shapes=[
            pltpu.VMEM((blocks, rows, cols), BF),
            pltpu.VMEM((slots, rows, cols), F32),
            pltpu.VMEM((2, nodes, cols), BF),
            dma((blocks,)), dma((blocks,)), dma((2, 2)),
        ],
        compiler_params=pltpu.CompilerParams(vmem_limit_bytes=(40 if resident else 62) * 2**20),
    )(wg, out, ig, bias, gain, shift)
    return out, ig, wg, bias, gain, shift


def solution(mesh):
    return jax.shard_map(
        per_device,
        mesh=mesh,
        in_specs=(
            P("cluster", "mp"),
            P("cluster", None),
            P("cluster", None),
            P("cluster"),
            P("cluster", None, None),
            P("cluster"),
            P(None, None, "mp"),
            P(None, "mp"),
            P(None, "mp"),
            P(None, "mp"),
            P("cluster", "mp"),
        ),
        out_specs=(
            P("cluster", "mp"),
            P("cluster", "mp"),
            P(None, None, "mp"),
            P(None, "mp"),
            P(None, "mp"),
            P(None, "mp"),
        ),
        check_vma=False,
    )
```

```python
import functools

import jax
import jax.numpy as jnp
from jax import lax
from jax.experimental import pallas as pl
from jax.experimental.pallas import tpu as pltpu
from jax.sharding import PartitionSpec as P

EPS = 1e-05
MESH = pl.DeviceIdType.MESH
BF = jnp.bfloat16
F32 = jnp.float32

SCHEDULE = (
    ("A0",),
    ("A",), ("ys", 0, 1, 2),
    ("B0",),
    ("B",), ("ys", 0, 1, 3), ("ys", 0, 1, 0), ("ys", 0, 0, 2), ("ys", 0, 0, 0),
    ("B1",), ("ys", 0, 0, 3), ("ys", 0, 0, 1), ("ys", 0, 1, 1),
    ("B2",),
    ("C",), ("ys", 1, 1, 0), ("ys", 1, 0, 2), ("ys", 1, 0, 1), ("ys", 1, 1, 3), ("ys", 1, 1, 2), ("ys", 1, 0, 0),
    ("C2",), ("ds", 1, 1, 1), ("ds", 1, 0, 1),
    ("C3",),
    ("D",), ("ys", 1, 1, 1), ("yf", 1, 2), ("yf", 1, 1), ("df", 1, 1), ("ys", 1, 0, 3), ("yp", 0, 0),
    ("E",), ("yf", 1, 0), ("yf", 1, 3), ("ds", 1, 0, 0), ("yp", 1, 1),
    ("E2",), ("yf", 0, 1), ("ds", 0, 0, 0), ("ds", 1, 1, 0), ("yp", 1, 0), ("yp", 1, 2), ("pr", 1, 1), ("pr", 1, 3),
    ("ds", 0, 1, 0), ("df", 1, 0), ("ds", 0, 0, 1), ("ds", 0, 1, 1), ("cb", 1, 1), ("yf", 0, 3), ("cb", 1, 3),
    ("go", 1, 1, 1), ("pr", 1, 0), ("df", 0, 0), ("yf", 0, 2), ("df", 0, 1), ("go", 1, 3, 1), ("yf", 0, 0),
    ("gf", 1, 3, 0), ("pr", 1, 2), ("go", 1, 1, 2), ("gf", 1, 3, 1), ("cb", 1, 0),
    ("E3",), ("gf", 1, 1, 0), ("yp", 0, 1), ("cb", 1, 2), ("yp", 0, 2), ("pr", 0, 1), ("gf", 1, 0, 0),
    ("go", 1, 0, 1), ("pr", 0, 0), ("go", 1, 0, 2), ("gf", 1, 1, 1), ("cb", 0, 1), ("gf", 1, 0, 1), ("gf", 1, 2, 0),
    ("go", 1, 2, 1), ("go", 1, 3, 2), ("pr", 0, 2), ("gf", 1, 1, 2), ("gf", 1, 0, 2), ("pr", 0, 3), ("gf", 0, 1, 0),
    ("gf", 1, 3, 2), ("gf", 1, 2, 1), ("go", 0, 1, 1), ("gf", 0, 1, 1), ("go", 1, 2, 2), ("cb", 0, 2), ("cb", 0, 3),
    ("cb", 0, 0),
    ("F",), ("gf", 0, 2, 0), ("go", 0, 2, 1), ("go", 0, 0, 1), ("go", 0, 1, 2), ("gf", 0, 1, 2), ("gf", 0, 0, 0),
    ("gf", 0, 3, 0), ("gf", 0, 2, 1), ("gf", 1, 2, 2),
    ("G",), ("go", 0, 0, 2), ("gf", 0, 0, 1),
    ("IG",), ("gf", 0, 3, 1), ("go", 0, 3, 1), ("gf", 0, 2, 2), ("gf", 0, 0, 2), ("go", 0, 3, 2), ("go", 0, 2, 2),
    ("gf", 0, 3, 2),
)
ORDERS = (
    (
        ((1, 2, 4), (4, 1, 2)),
        ((4, 2, 1), (1, 4, 2)),
        ((2, 1, 4), (4, 2, 1)),
        ((4, 2, 1), (4, 1, 2)),
    ),
    (
        ((4, 2, 1), (4, 1, 2)),
        ((4, 2, 1), (4, 2, 1)),
        ((1, 4, 2), (2, 1, 4)),
        ((4, 1, 2), (4, 2, 1)),
    ),
)


def mm(a, b):
    return jnp.dot(a, b, preferred_element_type=F32)


def mm_t(a, b):
    return lax.dot_general(a, b, (((1,), (1,)), ((), ())), preferred_element_type=F32)


def chain(
    n, cap, fan,
    f_hbm, rows_hbm, ids_hbm, ew_hbm, sw_hbm, valid_hbm, bias_hbm, gain_hbm, shift_hbm, og_hbm, w_hbm,
    out_hbm, ig_hbm, wg_hbm, bias_res, gain_res, shift_res,
    f_ref, rows_ref, ids_ref, ew_ref, sw_ref, valid_ref, bias_ref, gain_ref, shift_ref,
    bias_out, gain_out, shift_out, rows_row, in_sem,
    w_ref, og_ref, adj, adj_t, sel, sel_t, mask_ref, h1_ref, yf, s_ref, d_ref, zacc,
    dy_recv, hsend, hrecv, st_row, stat0, stat1, stat2, stat3,
    yt, yr, dzr, wpart, zr, fin,
    w_sem, og_sem, out_sem, mp_sem, h_sem, x_sem,
    y_sem, yp_sem, dz_sem, zr_sem, az_sem, ag_sem, fin_sem,
):
    nodes, cols = f_hbm.shape
    ct = 256
    tiles = cols // ct
    half = cols // 2
    c = lax.axis_index("cluster")
    m = lax.axis_index("mp")
    peer = (c, 1 - m)
    halo = n * cap
    lookup = nodes + halo
    line, far = n // 4, n // 8
    zi, p = c // 4, c % 4
    px, py = p % 2, p // 2
    near = (c + 1 - 2 * px, c + 2 - 4 * py)
    rc = half // line
    dy_own, dyb, g_ref = zacc, og_ref, s_ref.at[1]
    out_ref, dy_send, dz_ref = yf.at[0, 0], yf.at[0, 1], yf.at[1]
    pieces = 4
    prow = half // pieces
    lanes = cols // 8
    kept = {}

    def rows_of(start, size):
        return pl.ds(pl.multiple_of(start, size), size)

    def col(j):
        return rows_of(j * ct, ct)

    def remote(src, dst, sems, idx, to):
        return pltpu.make_async_remote_copy(
            src_ref=src,
            dst_ref=dst,
            send_sem=sems.at[(0, *idx)],
            recv_sem=sems.at[(1, *idx)],
            device_id=to,
            device_id_type=MESH,
        )

    def mask(width):
        return jnp.concatenate([mask_ref[...]] * (width // 128), axis=1)

    def halo_part(d):
        return rows_of(d * 2 * cap, 2 * cap)

    def pack_halo(left, right):
        both = jnp.concatenate(
            [left.reshape(n, cap, half), right.reshape(n, cap, half)], axis=1
        )
        hsend[...] = both.reshape(n * 2 * cap, half).astype(BF)

    def wait_all(ref, size, sem):
        some = ref.at[pl.ds(0, size)]
        pltpu.make_async_copy(some, some, sem).wait()

    def halo_copy(to, frm):
        return pltpu.make_async_remote_copy(
            src_ref=hsend.at[halo_part(to)],
            dst_ref=hrecv.at[halo_part(frm)],
            send_sem=h_sem.at[0],
            recv_sem=h_sem.at[1],
            device_id=(to, m),
            device_id_type=MESH,
        )

    def halo_start():
        def send(i, _):
            halo_copy(lax.rem(c + i, n), c).start()
            return 0

        lax.fori_loop(1, n, send, 0)
        hrecv[halo_part(c)] = hsend[halo_part(c)]

    def halo_finish():
        wait_all(hsend, (n - 1) * 2 * cap, h_sem.at[0])
        wait_all(hrecv, (n - 1) * 2 * cap, h_sem.at[1])
        got = hrecv[...].astype(F32).reshape(n, 2 * cap, half)
        left = got[:, :cap, :].reshape(halo, half).astype(BF)
        right = got[:, cap:, :].reshape(halo, half).astype(BF)
        return left, right

    def pick(src):
        pack_halo(mm(sel[...], src[:, :half]), mm(sel[...], src[:, half:]))

    def stat_copy(e, buf, to, frm):
        return pltpu.make_async_remote_copy(
            src_ref=buf.at[c],
            dst_ref=buf.at[frm],
            send_sem=x_sem.at[0, e % 2],
            recv_sem=x_sem.at[1, e % 2],
            device_id=(to, m),
            device_id_type=MESH,
        )

    def stat_start(e, buf):
        def send(i, _):
            stat_copy(e, buf, lax.rem(c + i, n), c).start()
            return 0

        lax.fori_loop(1, n, send, 0)

    def stat_finish(e, buf):
        for way in range(2):
            wait_all(buf, n - 1, x_sem.at[way, e % 2])

    def fold(buf, k, row):
        for g in range(8):
            buf[c, k, g : g + 1, :] = st_row[row : row + 1, g * lanes : (g + 1) * lanes]

    def unfold(tile, row):
        for g in range(8):
            st_row[row : row + 1, g * lanes : (g + 1) * lanes] = tile[g : g + 1, :]

    def total(buf, k):
        return lax.fori_loop(1, n, lambda s, t: t + buf[s, k], buf[0, k])

    def quarter(layer, who):
        qx = 1 - px if who in (0, 2) else px
        qy = 1 - py if who in (1, 2) else py
        return (qx, qy) if layer == 1 else (qy, qx)

    def y_flip(layer):
        def flip(i, _):
            r = rows_of(i * 128, 128)
            for h in range(2):
                yt[layer, rows_of(h * cols + i * 128, 128), :] = (
                    yf[layer, h, :, r].astype(F32).T.astype(BF)
                )
            return 0

        lax.fori_loop(0, cols // 128, flip, 0)

    def y_piece(layer, who, k):
        hr, _ = quarter(layer, who)
        return remote(
            yt.at[layer, rows_of(hr * cols + m * half + k * prow, prow), :],
            yr.at[layer, who, rows_of(m * half + k * prow, prow), :],
            y_sem, (layer, who, k), (near[who], m),
        )

    def y_first(layer):
        return 1 - layer

    def z_first(layer):
        return layer

    def y_relay(layer, k):
        first = y_first(layer)
        r = rows_of(m * half + k * prow, prow)
        return remote(
            yr.at[layer, first, r, :], yr.at[layer, 2, r, :], y_sem, (layer, 2, k),
            (near[1 - first], m),
        )

    def y_forward(layer, k):
        y_piece(layer, y_first(layer), k).wait_recv()
        y_relay(layer, k).start()

    def y_pass_copy(layer, who, part):
        r = rows_of(part * half, half)
        return remote(
            yr.at[layer, who, r, :], yr.at[layer, who, r, :], yp_sem, (layer, who), peer
        )

    def y_pass(layer, who):
        if who != y_first(layer):
            for k in range(pieces):
                copy = y_relay(layer, k) if who == 2 else y_piece(layer, who, k)
                copy.wait_recv()
        y_pass_copy(layer, who, m).start()

    def y_sent(layer):
        for k in range(pieces):
            y_piece(layer, 0, k).wait_send()
            y_piece(layer, 1, k).wait_send()
            y_relay(layer, k).wait_send()
        for who in range(3):
            y_pass_copy(layer, who, m).wait_send()

    def dz_piece(layer, who, h):
        _, hc = quarter(layer, who)
        return remote(
            dz_ref.at[layer, :, rows_of(hc * half + h * ct, ct)],
            dzr.at[layer, who, h],
            dz_sem, (layer, who, h), (near[who], m),
        )

    def dz_relay(layer, h):
        first = z_first(layer)
        return remote(
            dzr.at[layer, first, h], dzr.at[layer, 2, h], dz_sem, (layer, 2, h),
            (near[1 - first], m),
        )

    def dz_forward(layer, h):
        dz_piece(layer, z_first(layer), h).wait_recv()
        dz_relay(layer, h).start()

    def dz_sent(layer):
        for h in range(2):
            dz_piece(layer, 0, h).wait_send()
            dz_piece(layer, 1, h).wait_send()
            dz_relay(layer, h).wait_send()

    def part(b):
        return m if b < 2 else 1 - m

    def line_copy(layer, b, to, frm):
        return pltpu.make_async_remote_copy(
            src_ref=wpart.at[layer, b, rows_of(to * rc, rc), :],
            dst_ref=zr.at[layer, b, frm],
            send_sem=zr_sem.at[0, layer, b, to],
            recv_sem=zr_sem.at[1, layer, b, frm],
            device_id=(to * 4 + p, m),
            device_id_type=MESH,
        )

    def once(key):
        fresh = key not in kept
        kept[key] = True
        return fresh

    def product(layer, b):
        hr, hc = quarter(layer, 3)
        h = b % 2
        if b >= 2 and once(("y", layer)):
            for who in range(3):
                y_pass_copy(layer, who, 1 - m).wait_recv()
        if once(("dz", layer, h)):
            dz_piece(layer, 1 - z_first(layer), h).wait_recv()
            dz_relay(layer, h).wait_recv()
        own_dz = dz_ref[layer, :, rows_of(hc * half + h * ct, ct)]

        def one(i, _):
            start = part(b) * half + i * ct
            acc = mm(yt[layer, rows_of(hr * cols + start, ct), :], own_dz)
            for who in range(3):
                acc = acc + mm(yr[layer, who, rows_of(start, ct), :], dzr[layer, who, h])
            wpart[layer, b, rows_of(i * ct, ct), :] = acc.astype(BF)
            return 0

        lax.fori_loop(0, half // ct, one, 0)

        def send(i, _):
            line_copy(layer, b, (zi + i) % line, zi).start()
            return 0

        lax.fori_loop(1, line, send, 0)

    def flip_bit(e, d):
        return e + d - 2 * d * ((e // d) % 2)

    def spot(layer, b, e):
        ex, ey = e % 2, (e // 2) % 2
        hr, hc = (ex, ey) if layer == 1 else (ey, ex)
        return wg_hbm.at[
            layer,
            rows_of(hr * cols + part(b) * half + (e // 4) * rc, rc),
            rows_of(hc * half + (b % 2) * ct, ct),
        ]

    def held(base, dims):
        got = [base]
        for d in dims:
            got = got + [flip_bit(e, d) for e in got]
        return got

    def far_copy(layer, b, to, frm):
        return pltpu.make_async_remote_copy(
            src_ref=fin.at[layer, b],
            dst_ref=spot(layer, b, frm),
            send_sem=az_sem.at[0, layer, b, to // 8],
            recv_sem=az_sem.at[1, layer, b, frm // 8],
            device_id=(to, m),
            device_id_type=MESH,
        )

    def hops(layer, b, i, step, arriving):
        own = isinstance(i, int)
        dims = ORDERS[layer][b][0 if own else 1]
        base = (c + 8 * i) % n
        other = flip_bit(c, dims[step])
        slot = 2**step - 1
        copies = []
        for j, e in enumerate(held(base, dims[:step])):
            if arriving:
                e = flip_bit(e, dims[step])
            src = fin.at[layer, b] if own and j == 0 and not arriving else spot(layer, b, e)
            copies.append(
                remote(src, spot(layer, b, e), ag_sem, (layer, b, base // 8, slot + j), (other, m))
            )
        return copies

    def keep(layer, b):
        return pltpu.make_async_copy(
            fin.at[layer, b], spot(layer, b, c), fin_sem.at[layer, b]
        )

    def combine(layer, b):
        def take(i, _):
            frm = (zi + i) % line
            copy = line_copy(layer, b, frm, frm)
            copy.wait_recv()
            copy.wait_send()
            return 0

        lax.fori_loop(1, line, take, 0)
        zr[layer, b, zi] = wpart[layer, b, rows_of(zi * rc, rc), :]
        fin[layer, b] = lax.fori_loop(
            1, line,
            lambda j, t: t + zr[layer, b, j].astype(F32),
            zr[layer, b, 0].astype(F32),
        ).astype(BF)
        keep(layer, b).start()

        def send(i, _):
            far_copy(layer, b, (c + 8 * i) % n, c).start()
            return 0

        lax.fori_loop(1, far, send, 0)
        gather_own(layer, b, 0)

    def gather_own(layer, b, step):
        if step > 0:
            for copy in hops(layer, b, 0, step - 1, True):
                copy.wait_recv()
        for copy in hops(layer, b, 0, step, False):
            copy.start()
        if step > 0:
            for copy in hops(layer, b, 0, step - 1, False):
                copy.wait_send()

    def gather_far(layer, b, step):
        def one(i, _):
            if step == 0:
                frm = (c + 8 * i) % n
                far_copy(layer, b, frm, frm).wait_recv()
            else:
                for copy in hops(layer, b, i, step - 1, True):
                    copy.wait_recv()
            for copy in hops(layer, b, i, step, False):
                copy.start()
            if step > 0:
                for copy in hops(layer, b, i, step - 1, False):
                    copy.wait_send()
            return 0

        lax.fori_loop(1, far, one, 0)

    def gather_finish(layer, b):
        keep(layer, b).wait()

        def ends(i):
            for copy in hops(layer, b, i, 2, True):
                copy.wait_recv()
            for copy in hops(layer, b, i, 2, False):
                copy.wait_send()

        def one(i, _):
            far_copy(layer, b, (c + 8 * i) % n, c).wait_send()
            ends(i)
            return 0

        ends(0)
        lax.fori_loop(1, far, one, 0)

    w_copies = [
        pltpu.make_async_copy(w_hbm.at[layer], w_ref.at[layer], w_sem.at[layer])
        for layer in range(2)
    ]
    og_copy = pltpu.make_async_copy(og_hbm, og_ref, og_sem)
    in_copies = [
        pltpu.make_async_copy(src, dst, in_sem.at[i])
        for i, (src, dst) in enumerate(
            (
                (rows_hbm, rows_ref), (f_hbm, f_ref), (ids_hbm, ids_ref), (ew_hbm, ew_ref),
                (sw_hbm, sw_ref), (valid_hbm, valid_ref), (bias_hbm, bias_ref),
                (gain_hbm, gain_ref), (shift_hbm, shift_ref),
            )
        )
    ]
    small_copies = [
        pltpu.make_async_copy(src, dst, out_sem.at[2 + i])
        for i, (src, dst) in enumerate(
            ((bias_out, bias_res), (gain_out, gain_res), (shift_out, shift_res))
        )
    ]
    out_copy = pltpu.make_async_copy(out_ref, out_hbm, out_sem.at[0])
    ig_copy = pltpu.make_async_copy(h1_ref, ig_hbm, out_sem.at[1])

    def begin():
        for copy in in_copies:
            copy.start()
        barrier = pltpu.get_barrier_semaphore()

        def greet(i, _):
            pl.semaphore_signal(
                barrier, inc=1, device_id=(lax.rem(c + i, n), m), device_id_type=MESH
            )
            return 0

        lax.fori_loop(1, n, greet, 0)
        pl.semaphore_signal(barrier, inc=1, device_id=peer, device_id_type=MESH)
        w_copies[0].start()
        og_copy.start()
        w_copies[1].start()

        in_copies[0].wait()
        lane = lax.broadcasted_iota(jnp.int32, (cap, halo), 1)
        spread = jnp.zeros((cap, halo), F32)
        for d in range(n):
            mine = rows_ref[0, :, d : d + 1].astype(F32)
            spread = jnp.where((lane >= d * cap) & (lane < (d + 1) * cap), mine, spread)
        place_q = lax.broadcasted_iota(jnp.int32, (cap, halo), 0)
        wanted = jnp.sum(jnp.where(lane % cap == place_q, spread, 0.0), axis=0, keepdims=True)
        rows_row[...] = wanted.astype(jnp.int32)

        def choose(i, _):
            r = rows_of(i * 128, 128)
            one_hot = jnp.where(
                rows_row[:, r] == lax.broadcasted_iota(jnp.int32, (nodes, 128), 0), 1.0, 0.0
            )
            sel_t[:, r] = one_hot.astype(BF)
            sel[r, :] = one_hot.T.astype(BF)
            return 0

        lax.fori_loop(0, halo // 128, choose, 0)
        in_copies[1].wait()
        pick(f_ref)
        pl.semaphore_wait(barrier, n)
        halo_start()
        for copy in in_copies[2:]:
            copy.wait()
        mask_ref[...] = jnp.broadcast_to(valid_ref[...].astype(F32), (128, nodes)).T
        rb = 16
        place = lax.broadcasted_iota(jnp.int32, (rb, nodes), 0)
        node = lax.broadcasted_iota(jnp.int32, (rb, nodes), 1)

        def build(i, _):
            slots = place + i * rb
            a = jnp.where(node == slots, 2.0 * sw_ref[...], 0.0)
            for k in range(fan):
                a = a + jnp.where(ids_ref[k : k + 1, :] == slots, ew_ref[k : k + 1, :], 0.0)
            adj_t[rows_of(i * rb, rb), :] = a.astype(BF)
            return 0

        lax.fori_loop(0, lookup // rb, build, 0)

        def turn(i, _):
            r = rows_of(i * 128, 128)
            adj[:, r] = adj_t[r, :].astype(F32).T.astype(BF)
            return 0

        lax.fori_loop(0, lookup // 128, turn, 0)

    def agg_local(layer):
        src = f_ref if layer == 0 else h1_ref
        for h in range(2):
            cs = slice(h * half, (h + 1) * half)
            zacc[:, cs] = mm(adj[:, :nodes], src[:, cs])

    def mp_copy(k, src, dst):
        return remote(src, dst, mp_sem, (k,), peer)

    def y_exchange(layer, h):
        ref = yf.at[layer, m, :, slice(h * half, (h + 1) * half)]
        return mp_copy(layer * 2 + h, ref, ref)

    def agg_halo(layer):
        parts = halo_finish()
        for h in range(2):
            cs = slice(h * half, (h + 1) * half)
            yf[layer, m, :, cs] = (zacc[:, cs] + mm(adj[:, nodes:], parts[h])).astype(BF)
            y_exchange(layer, h).start()

    def z_own(layer):
        w_copies[layer].wait()

        zacc[...] = mm(yf[layer, m], w_ref[layer, rows_of(m * cols, cols), :])
        for h in range(2):
            y_exchange(layer, h).wait_recv()

    def z_other(layer):
        if layer == 1:
            og_copy.wait()
        own_count = jnp.sum(mask_ref[...], axis=0, keepdims=True)
        own_count = jnp.concatenate([own_count] * (ct // 128), axis=1)
        own_inv = 1.0 / jnp.maximum(own_count, 1.0)

        zacc[...] += mm(yf[layer, 1 - m], w_ref[layer, rows_of((1 - m) * cols, cols), :])

        def second(j, _):
            z = zacc[:, col(j)] + bias_ref[layer : layer + 1, col(j)]
            sig = jax.nn.sigmoid(z)
            s = z * sig
            s_ref[layer, :, col(j)] = s
            d_ref[layer, :, col(j)] = (sig * (1.0 + z * (1.0 - sig))).astype(BF)
            valid = mask(ct)
            tot = jnp.sum(s * valid, axis=0, keepdims=True)
            cen = s - tot * own_inv
            st_row[0:1, col(j)] = tot
            st_row[1:2, col(j)] = jnp.sum(cen * cen * valid, axis=0, keepdims=True)
            if layer == 0:
                st_row[2:3, col(j)] = own_count
            else:
                pg = og_ref[:, col(j)].astype(F32) * valid
                st_row[2:3, col(j)] = jnp.sum(pg, axis=0, keepdims=True)
                st_row[3:4, col(j)] = jnp.sum(pg * cen, axis=0, keepdims=True)
            return 0

        lax.fori_loop(0, tiles, second, 0)
        buf = stat0 if layer == 0 else stat1
        for k in range(3 if layer == 0 else 4):
            fold(buf, k, k)

    def stats_out(layer):
        stat_start(layer, stat0 if layer == 0 else stat1)
        for h in range(2):
            y_exchange(layer, h).wait_send()
        y_flip(layer)

    def normalize(layer):
        buf = stat0 if layer == 0 else stat1
        stat_finish(layer, buf)
        count = jnp.maximum(total(stat0, 2), 1.0)
        mu = total(buf, 0) / count

        def spread(s, t):
            nc = stat0[s, 2]
            off = buf[s, 0] / jnp.maximum(nc, 1.0) - mu
            return t + buf[s, 1] + nc * off * off

        var = lax.fori_loop(0, n, spread, jnp.zeros_like(mu)) / count
        inv = lax.rsqrt(var + EPS)
        at = 8 if layer == 0 else 4
        unfold(mu, at)
        unfold(inv, at + 1)
        mu_row, inv_row = st_row[at : at + 1, :], st_row[at + 1 : at + 2, :]
        gain_row = gain_ref[layer : layer + 1, :]
        shift_row = shift_ref[layer : layer + 1, :]
        dst = h1_ref if layer == 0 else out_ref
        for j in range(tiles):
            cs = slice(j * ct, (j + 1) * ct)
            x = (s_ref[layer, :, cs] - mu_row[:, cs]) * inv_row[:, cs]
            dst[:, cs] = (mask(ct) * (gain_row[:, cs] * x + shift_row[:, cs])).astype(BF)
        if layer == 0:
            pick(h1_ref)
            return
        out_copy.start()

        def gains(s, t):
            off = stat1[s, 0] / jnp.maximum(stat0[s, 2], 1.0) - mu
            return t + stat1[s, 3] + off * stat1[s, 2]

        unfold(total(stat1, 2), 6)
        unfold(inv * lax.fori_loop(0, n, gains, jnp.zeros_like(mu)), 7)
        unfold(1.0 / count, 10)
        norm_sums(1)
        pre_grad(1)
        fold(stat2, 2, 11)

    def norm_sums(layer):
        gain_out[layer : layer + 1, :] = st_row[7:8, :]
        shift_out[layer : layer + 1, :] = st_row[6:7, :]

    def pre_grad(layer):
        at = 8 if layer == 0 else 4
        grad_src = og_ref if layer == 1 else g_ref

        def pre(j, _):
            gain = gain_ref[layer : layer + 1, col(j)]
            inv_row = st_row[at + 1 : at + 2, col(j)]
            ic = st_row[10:11, col(j)]
            x = (s_ref[layer, :, col(j)] - st_row[at : at + 1, col(j)]) * inv_row
            valid = mask(ct)
            pg = grad_src[:, col(j)].astype(F32) * valid
            ds = (
                valid
                * (inv_row * gain)
                * (pg - st_row[6:7, col(j)] * ic - x * (st_row[7:8, col(j)] * ic))
            )
            dz = (ds * d_ref[layer, :, col(j)].astype(F32)).astype(BF)
            dz_ref[layer, :, col(j)] = dz
            st_row[11:12, col(j)] = jnp.sum(dz.astype(F32), axis=0, keepdims=True)
            return 0

        lax.fori_loop(0, tiles, pre, 0)

    def dy_copy(layer):
        return mp_copy(4 + layer, dy_send, dy_recv.at[layer])

    def dy_other(layer):
        theirs = w_ref[layer, rows_of((1 - m) * cols, cols), :]
        dy_send[...] = mm_t(dz_ref[layer], theirs).astype(BF)
        dy_copy(layer).start()

    def dy_mine(layer):
        dy_own[...] = mm_t(dz_ref[layer], w_ref[layer, rows_of(m * cols, cols), :])
        dy_copy(layer).wait_recv()
        for j in range(tiles):
            cs = slice(j * ct, (j + 1) * ct)
            dyb[:, cs] = (dy_own[:, cs] + dy_recv[layer, :, cs].astype(F32)).astype(BF)
        back = adj_t[nodes:, :]
        pack_halo(mm(back, dyb[:, :half]), mm(back, dyb[:, half:]))
        halo_start()

    def back_local(layer):
        for h in range(2):
            cs = slice(h * half, (h + 1) * half)
            g_ref[:, cs] = mm(adj_t[:nodes, :], dyb[:, cs])
        dy_copy(layer).wait_send()

    def back_halo(layer):
        parts = halo_finish()
        for h in range(2):
            cs = slice(h * half, (h + 1) * half)
            got = g_ref[:, cs] + mm(sel_t[...], parts[h])
            if layer == 1:
                g_ref[:, cs] = got
                pg = got * mask(half)
                x = (s_ref[0, :, cs] - st_row[8:9, cs]) * st_row[9:10, cs]
                st_row[0:1, cs] = jnp.sum(pg, axis=0, keepdims=True)
                st_row[1:2, cs] = jnp.sum(pg * x, axis=0, keepdims=True)
            else:
                h1_ref[:, cs] = got.astype(BF)
        if layer == 1:
            fold(stat2, 0, 0)
            fold(stat2, 1, 1)
            stat_start(2, stat2)
        else:
            ig_copy.start()

    def back_norm():
        stat_finish(2, stat2)
        unfold(total(stat2, 0), 6)
        unfold(total(stat2, 1), 7)
        unfold(total(stat2, 2), 12)
        norm_sums(0)
        bias_out[1:2, :] = st_row[12:13, :]
        pre_grad(0)
        fold(stat3, 0, 11)
        stat_start(3, stat3)

    table = {
        "A0": lambda: (begin(), agg_local(0), agg_halo(0), z_own(0), z_other(0)),
        "A": lambda: stats_out(0),
        "B0": lambda: normalize(0),
        "B": halo_start,
        "B1": lambda: (agg_local(1), agg_halo(1)),
        "B2": lambda: z_own(1),
        "C": lambda: (z_other(1), stats_out(1)),
        "C2": lambda: normalize(1),
        "C3": lambda: dy_other(1),
        "D": lambda: dy_mine(1),
        "E": lambda: (back_local(1), back_halo(1)),
        "E2": back_norm,
        "E3": lambda: dy_other(0),
        "F": lambda: dy_mine(0),
        "G": lambda: back_local(0),
        "IG": lambda: back_halo(0),
        "ys": lambda l, who, k: y_piece(l, who, k).start(),
        "yf": y_forward,
        "yp": y_pass,
        "ds": lambda l, who, h: dz_piece(l, who, h).start(),
        "df": dz_forward,
        "pr": product,
        "cb": combine,
        "go": gather_own,
        "gf": gather_far,
    }
    for name, *args in SCHEDULE:
        table[name](*args)

    stat_finish(3, stat3)
    unfold(total(stat3, 0), 12)
    bias_out[0:1, :] = st_row[12:13, :]
    for copy in small_copies:
        copy.start()
    out_copy.wait()
    ig_copy.wait()
    for layer in (1, 0):
        y_sent(layer)
        dz_sent(layer)
        for b in range(4):
            gather_finish(layer, b)
    for copy in small_copies:
        copy.wait()


def hand_over(
    rows, slots,
    wg_hbm, out_in, ig_in, bias_in, gain_in, shift_in,
    wg_out, out_out, ig_out, bias_out, gain_out, shift_out,
    wide, through, in_sem, wide_sem, pass_sem, *narrow,
):
    blocks = in_sem.shape[0]
    per_layer = wg_hbm.shape[1] // rows

    def block(ref, i):
        return ref.at[i // per_layer, pl.ds((i % per_layer) * rows, rows), :]

    resident = not narrow

    def read(i):
        return pltpu.make_async_copy(block(wg_hbm, i), narrow[0].at[i], in_sem.at[i])

    def write(i):
        return pltpu.make_async_copy(wide.at[i % slots], block(wg_out, i), wide_sem.at[i])

    takes = [
        pltpu.make_async_copy(ref, through.at[i], pass_sem.at[0, i])
        for i, ref in enumerate((out_in, ig_in))
    ]
    gives = [
        pltpu.make_async_copy(through.at[i], ref, pass_sem.at[1, i])
        for i, ref in enumerate((out_out, ig_out))
    ]
    for i in range(blocks):
        if not resident:
            read(i).start()
        if i == 1:
            for copy in takes:
                copy.start()
    for i in range(blocks):
        if not resident:
            read(i).wait()
        if i >= slots:
            write(i - slots).wait()
        wide[i % slots] = (block(wg_hbm, i) if resident else narrow[0].at[i])[...].astype(F32)
        write(i).start()
        if i == 2:
            for take, give in zip(takes, gives):
                take.wait()
                give.start()
    bias_out[...] = bias_in[...]
    gain_out[...] = gain_in[...]
    shift_out[...] = shift_in[...]
    for i in range(blocks - slots, blocks):
        write(i).wait()
    for give in gives:
        give.wait()


def per_device(
    features, neighbour_ids, edge_weight, self_weight, send_rows, valid_mask,
    weights, biases, norm_gain, norm_shift, output_grad,
):
    nodes, cols = features.shape
    fan = neighbour_ids.shape[1]
    n, cap = send_rows.shape[1], send_rows.shape[2]
    halo = n * cap
    lookup = nodes + halo
    line = n // 4
    half = cols // 2
    vm = pl.BlockSpec(memory_space=pltpu.VMEM)
    anyspace = pl.BlockSpec(memory_space=pl.ANY)
    dma = pltpu.SemaphoreType.DMA
    small = jax.ShapeDtypeStruct((2, cols), F32)
    wide_block = jax.ShapeDtypeStruct((nodes, cols), BF)
    resident = n <= 16
    place = pltpu.VMEM if resident else jax.ShapeDtypeStruct
    out, ig, wg, bias, gain, shift = pl.pallas_call(
        functools.partial(chain, n, cap, fan),
        out_shape=(
            place((nodes, cols), BF), place((nodes, cols), BF), place((2, 2 * cols, cols), BF),
            *[place((2, cols), F32) for _ in range(3)],
        ),
        in_specs=[anyspace] * 11,
        out_specs=(anyspace,) * 6,
        scratch_shapes=[
            pltpu.VMEM((nodes, cols), BF),
            pltpu.VMEM((1, cap, n), jnp.int32),
            pltpu.VMEM((fan, nodes), jnp.int32),
            pltpu.VMEM((fan, nodes), F32),
            pltpu.VMEM((1, nodes), F32),
            pltpu.VMEM((1, nodes), jnp.int32),
            *[pltpu.VMEM((2, cols), F32) for _ in range(6)],
            pltpu.VMEM((1, halo), jnp.int32),
            dma((9,)),
            pltpu.VMEM((2, 2 * cols, cols), BF),
            pltpu.VMEM((nodes, cols), BF),
            pltpu.VMEM((nodes, lookup), BF),
            pltpu.VMEM((lookup, nodes), BF),
            pltpu.VMEM((halo, nodes), BF),
            pltpu.VMEM((nodes, halo), BF),
            pltpu.VMEM((nodes, 128), F32),
            pltpu.VMEM((nodes, cols), BF),
            pltpu.VMEM((2, 2, nodes, cols), BF),
            pltpu.VMEM((2, nodes, cols), F32),
            pltpu.VMEM((2, nodes, cols), BF),
            pltpu.VMEM((nodes, cols), F32),
            pltpu.VMEM((2, nodes, cols), BF),
            pltpu.VMEM((2 * halo, half), BF),
            pltpu.VMEM((2 * halo, half), BF),
            pltpu.VMEM((16, cols), F32),
            pltpu.VMEM((n, 3, 8, cols // 8), F32),
            pltpu.VMEM((n, 4, 8, cols // 8), F32),
            pltpu.VMEM((n, 3, 8, cols // 8), F32),
            pltpu.VMEM((n, 1, 8, cols // 8), F32),
            pltpu.VMEM((2, 2 * cols, nodes), BF),
            pltpu.VMEM((2, 3, cols, nodes), BF),
            pltpu.VMEM((2, 3, 2, nodes, cols // 4), BF),
            pltpu.VMEM((2, 4, half, cols // 4), BF),
            pltpu.VMEM((2, 4, line, half // line, cols // 4), BF),
            pltpu.VMEM((2, 4, half // line, cols // 4), BF),
            dma((2,)), dma, dma((5,)), dma((2, 6)), dma((2,)), dma((2, 2)),
            dma((2, 2, 3, 4)), dma((2, 2, 3)), dma((2, 2, 3, 2)),
            dma((2, 2, 4, line)), dma((2, 2, 4, n // 8)), dma((2, 2, 4, n // 8, 7)), dma((2, 4)),
        ],
        compiler_params=pltpu.CompilerParams(
            collective_id=0,
            has_side_effects=True,
            vmem_limit_bytes=(52 if resident else 62) * 2**20,
        ),
    )(
        features, jnp.swapaxes(send_rows, 1, 2), neighbour_ids.T, edge_weight.T,
        self_weight.reshape(1, nodes), valid_mask.reshape(1, nodes), biases, norm_gain, norm_shift,
        output_grad, weights,
    )
    if resident:
        out, ig, wg, bias, gain, shift = (
            pltpu.with_memory_space_constraint(v, pltpu.VMEM)
            for v in (out, ig, wg, bias, gain, shift)
        )
    rows, slots = 512, 4
    blocks = 2 * 2 * cols // rows
    wg, out, ig, bias, gain, shift = pl.pallas_call(
        functools.partial(hand_over, rows, slots),
        out_shape=(
            jax.ShapeDtypeStruct((2, 2 * cols, cols), F32), wide_block, wide_block,
            small, small, small,
        ),
        in_specs=[vm if resident else anyspace] + [anyspace] * 2 + [vm] * 3,
        out_specs=(anyspace, anyspace, anyspace, vm, vm, vm),
        scratch_shapes=[
            pltpu.VMEM((slots, rows, cols), F32),
            pltpu.VMEM((2, nodes, cols), BF),
            dma((blocks,)), dma((blocks,)), dma((2, 2)),
            *([] if resident else [pltpu.VMEM((blocks, rows, cols), BF)]),
        ],
        compiler_params=pltpu.CompilerParams(vmem_limit_bytes=(40 if resident else 62) * 2**20),
    )(wg, out, ig, bias, gain, shift)
    return out, ig, wg, bias, gain, shift


def solution(mesh):
    return jax.shard_map(
        per_device,
        mesh=mesh,
        in_specs=(
            P("cluster", "mp"),
            P("cluster", None),
            P("cluster", None),
            P("cluster"),
            P("cluster", None, None),
            P("cluster"),
            P(None, None, "mp"),
            P(None, "mp"),
            P(None, "mp"),
            P(None, "mp"),
            P("cluster", "mp"),
        ),
        out_specs=(
            P("cluster", "mp"),
            P("cluster", "mp"),
            P(None, None, "mp"),
            P(None, "mp"),
            P(None, "mp"),
            P(None, "mp"),
        ),
        check_vma=False,
    )
```

```python
import functools

import jax
import jax.numpy as jnp
from jax import lax
from jax.experimental import pallas as pl
from jax.experimental.pallas import tpu as pltpu
from jax.sharding import PartitionSpec as P

EPS = 1e-05
MESH = pl.DeviceIdType.MESH
BF = jnp.bfloat16
F32 = jnp.float32

SCHEDULE = (
    ("A0",),
    ("A",), ("ys", 0, 1, 2),
    ("B0",),
    ("B",), ("ys", 0, 1, 3), ("ys", 0, 1, 0), ("ys", 0, 0, 2), ("ys", 0, 0, 0),
    ("B1",), ("ys", 0, 0, 3), ("ys", 0, 0, 1), ("ys", 0, 1, 1),
    ("B2",),
    ("C",), ("ys", 1, 1, 0), ("ys", 1, 0, 2), ("ys", 1, 0, 1), ("ys", 1, 1, 3), ("ys", 1, 1, 2), ("ys", 1, 0, 0),
    ("C2",), ("ds", 1, 1, 1), ("ds", 1, 0, 1),
    ("C3",),
    ("D",), ("ys", 1, 1, 1), ("yf", 1, 2), ("yf", 1, 1), ("df", 1, 1), ("ys", 1, 0, 3), ("yp", 0, 0),
    ("E",), ("yf", 1, 0), ("yf", 1, 3), ("ds", 1, 0, 0), ("yp", 1, 1),
    ("E2",), ("yf", 0, 1), ("ds", 0, 0, 0), ("ds", 1, 1, 0), ("yp", 1, 0), ("yp", 1, 2), ("pr", 1, 1), ("pr", 1, 3),
    ("ds", 0, 1, 0), ("df", 1, 0), ("ds", 0, 0, 1), ("ds", 0, 1, 1), ("cb", 1, 1), ("yf", 0, 3), ("cb", 1, 3),
    ("go", 1, 1, 1), ("pr", 1, 0), ("df", 0, 0), ("yf", 0, 2), ("df", 0, 1), ("go", 1, 3, 1), ("yf", 0, 0),
    ("gf", 1, 3, 0), ("pr", 1, 2), ("go", 1, 1, 2), ("gf", 1, 3, 1), ("cb", 1, 0),
    ("E3",), ("gf", 1, 1, 0), ("yp", 0, 1), ("cb", 1, 2), ("yp", 0, 2), ("pr", 0, 1), ("gf", 1, 0, 0),
    ("go", 1, 0, 1), ("pr", 0, 0), ("go", 1, 0, 2), ("gf", 1, 1, 1), ("cb", 0, 1), ("gf", 1, 0, 1), ("gf", 1, 2, 0),
    ("go", 1, 2, 1), ("go", 1, 3, 2), ("pr", 0, 2), ("gf", 1, 1, 2), ("gf", 1, 0, 2), ("pr", 0, 3), ("gf", 0, 1, 0),
    ("gf", 1, 3, 2), ("gf", 1, 2, 1), ("go", 0, 1, 1), ("gf", 0, 1, 1), ("go", 1, 2, 2), ("cb", 0, 2), ("cb", 0, 3),
    ("cb", 0, 0),
    ("F",), ("gf", 0, 2, 0), ("go", 0, 2, 1), ("go", 0, 0, 1), ("go", 0, 1, 2), ("gf", 0, 1, 2), ("gf", 0, 0, 0),
    ("gf", 0, 3, 0), ("gf", 0, 2, 1), ("gf", 1, 2, 2),
    ("G",), ("go", 0, 0, 2), ("gf", 0, 0, 1),
    ("IG",), ("gf", 0, 3, 1), ("go", 0, 3, 1), ("gf", 0, 2, 2), ("gf", 0, 0, 2), ("go", 0, 3, 2), ("go", 0, 2, 2),
    ("gf", 0, 3, 2),
)
ORDERS = (
    (
        ((1, 2, 4), (4, 1, 2)),
        ((4, 2, 1), (1, 4, 2)),
        ((2, 1, 4), (4, 2, 1)),
        ((4, 2, 1), (4, 1, 2)),
    ),
    (
        ((4, 2, 1), (4, 1, 2)),
        ((4, 2, 1), (4, 2, 1)),
        ((1, 4, 2), (2, 1, 4)),
        ((4, 1, 2), (4, 2, 1)),
    ),
)


def mm(a, b):
    return jnp.dot(a, b, preferred_element_type=F32)


def mm_t(a, b):
    return lax.dot_general(a, b, (((1,), (1,)), ((), ())), preferred_element_type=F32)


def chain(
    n, cap, fan, exact,
    f_hbm, rows_hbm, ids_hbm, ew_hbm, sw_hbm, valid_hbm, bias_hbm, gain_hbm, shift_hbm, og_hbm, w_hbm,
    out_hbm, ig_hbm, wg_hbm, bias_res, gain_res, shift_res,
    f_ref, rows_ref, ids_ref, ew_ref, sw_ref, valid_ref, bias_ref, gain_ref, shift_ref,
    bias_out, gain_out, shift_out, rows_row, in_sem,
    w_ref, og_ref, adj, adj_lo, adj_t, adj_tlo, a_block, sel, sel_t, mask_ref, h1_ref, yf, s_ref, d_ref, zacc,
    dy_recv, hsend, hrecv, st_row, stat0, stat1, stat2, stat3,
    yt, yr, dzr, wpart, zr, fin,
    w_sem, og_sem, out_sem, mp_sem, h_sem, x_sem,
    y_sem, yp_sem, dz_sem, zr_sem, az_sem, ag_sem, fin_sem,
):
    nodes, cols = f_hbm.shape
    ct = 256
    tiles = cols // ct
    half = cols // 2
    c = lax.axis_index("cluster")
    m = lax.axis_index("mp")
    peer = (c, 1 - m)
    halo = n * cap
    lookup = nodes + halo
    line, far = n // 4, n // 8
    zi, p = c // 4, c % 4
    px, py = p % 2, p // 2
    near = (c + 1 - 2 * px, c + 2 - 4 * py)
    rc = half // line
    dy_own, dyb, g_ref = zacc, og_ref, s_ref.at[1]
    out_ref, dy_send, dz_ref = yf.at[0, 0], yf.at[0, 1], yf.at[1]
    pieces = 4
    prow = half // pieces
    lanes = cols // 8
    kept = {}

    def rows_of(start, size):
        return pl.ds(pl.multiple_of(start, size), size)

    def col(j):
        return rows_of(j * ct, ct)

    def remote(src, dst, sems, idx, to):
        return pltpu.make_async_remote_copy(
            src_ref=src,
            dst_ref=dst,
            send_sem=sems.at[(0, *idx)],
            recv_sem=sems.at[(1, *idx)],
            device_id=to,
            device_id_type=MESH,
        )

    def mask(width):
        return jnp.concatenate([mask_ref[...]] * (width // 128), axis=1)

    def halo_part(d):
        return rows_of(d * 2 * cap, 2 * cap)

    def pack_halo(left, right):
        both = jnp.concatenate(
            [left.reshape(n, cap, half), right.reshape(n, cap, half)], axis=1
        )
        hsend[...] = both.reshape(n * 2 * cap, half).astype(BF)

    def wait_all(ref, size, sem):
        some = ref.at[pl.ds(0, size)]
        pltpu.make_async_copy(some, some, sem).wait()

    def halo_copy(to, frm):
        return pltpu.make_async_remote_copy(
            src_ref=hsend.at[halo_part(to)],
            dst_ref=hrecv.at[halo_part(frm)],
            send_sem=h_sem.at[0],
            recv_sem=h_sem.at[1],
            device_id=(to, m),
            device_id_type=MESH,
        )

    def halo_start():
        def send(i, _):
            halo_copy(lax.rem(c + i, n), c).start()
            return 0

        lax.fori_loop(1, n, send, 0)
        hrecv[halo_part(c)] = hsend[halo_part(c)]

    def halo_finish():
        wait_all(hsend, (n - 1) * 2 * cap, h_sem.at[0])
        wait_all(hrecv, (n - 1) * 2 * cap, h_sem.at[1])
        got = hrecv[...].astype(F32).reshape(n, 2 * cap, half)
        left = got[:, :cap, :].reshape(halo, half).astype(BF)
        right = got[:, cap:, :].reshape(halo, half).astype(BF)
        return left, right

    def pick(src):
        pack_halo(mm(sel[...], src[:, :half]), mm(sel[...], src[:, half:]))

    def stat_copy(e, buf, to, frm):
        return pltpu.make_async_remote_copy(
            src_ref=buf.at[c],
            dst_ref=buf.at[frm],
            send_sem=x_sem.at[0, e % 2],
            recv_sem=x_sem.at[1, e % 2],
            device_id=(to, m),
            device_id_type=MESH,
        )

    def stat_start(e, buf):
        def send(i, _):
            stat_copy(e, buf, lax.rem(c + i, n), c).start()
            return 0

        lax.fori_loop(1, n, send, 0)

    def stat_finish(e, buf):
        for way in range(2):
            wait_all(buf, n - 1, x_sem.at[way, e % 2])

    def fold(buf, k, row):
        for g in range(8):
            buf[c, k, g : g + 1, :] = st_row[row : row + 1, g * lanes : (g + 1) * lanes]

    def unfold(tile, row):
        for g in range(8):
            st_row[row : row + 1, g * lanes : (g + 1) * lanes] = tile[g : g + 1, :]

    def total(buf, k):
        return lax.fori_loop(1, n, lambda s, t: t + buf[s, k], buf[0, k])

    def quarter(layer, who):
        qx = 1 - px if who in (0, 2) else px
        qy = 1 - py if who in (1, 2) else py
        return (qx, qy) if layer == 1 else (qy, qx)

    def y_flip(layer):
        def flip(i, _):
            r = rows_of(i * 128, 128)
            for h in range(2):
                yt[layer, rows_of(h * cols + i * 128, 128), :] = (
                    yf[layer, h, :, r].astype(F32).T.astype(BF)
                )
            return 0

        lax.fori_loop(0, cols // 128, flip, 0)

    def y_piece(layer, who, k):
        hr, _ = quarter(layer, who)
        return remote(
            yt.at[layer, rows_of(hr * cols + m * half + k * prow, prow), :],
            yr.at[layer, who, rows_of(m * half + k * prow, prow), :],
            y_sem, (layer, who, k), (near[who], m),
        )

    def y_first(layer):
        return 1 - layer

    def z_first(layer):
        return layer

    def y_relay(layer, k):
        first = y_first(layer)
        r = rows_of(m * half + k * prow, prow)
        return remote(
            yr.at[layer, first, r, :], yr.at[layer, 2, r, :], y_sem, (layer, 2, k),
            (near[1 - first], m),
        )

    def y_forward(layer, k):
        y_piece(layer, y_first(layer), k).wait_recv()
        y_relay(layer, k).start()

    def y_pass_copy(layer, who, part):
        r = rows_of(part * half, half)
        return remote(
            yr.at[layer, who, r, :], yr.at[layer, who, r, :], yp_sem, (layer, who), peer
        )

    def y_pass(layer, who):
        if who != y_first(layer):
            for k in range(pieces):
                copy = y_relay(layer, k) if who == 2 else y_piece(layer, who, k)
                copy.wait_recv()
        y_pass_copy(layer, who, m).start()

    def y_sent(layer):
        for k in range(pieces):
            y_piece(layer, 0, k).wait_send()
            y_piece(layer, 1, k).wait_send()
            y_relay(layer, k).wait_send()
        for who in range(3):
            y_pass_copy(layer, who, m).wait_send()

    def dz_piece(layer, who, h):
        _, hc = quarter(layer, who)
        return remote(
            dz_ref.at[layer, :, rows_of(hc * half + h * ct, ct)],
            dzr.at[layer, who, h],
            dz_sem, (layer, who, h), (near[who], m),
        )

    def dz_relay(layer, h):
        first = z_first(layer)
        return remote(
            dzr.at[layer, first, h], dzr.at[layer, 2, h], dz_sem, (layer, 2, h),
            (near[1 - first], m),
        )

    def dz_forward(layer, h):
        dz_piece(layer, z_first(layer), h).wait_recv()
        dz_relay(layer, h).start()

    def dz_sent(layer):
        for h in range(2):
            dz_piece(layer, 0, h).wait_send()
            dz_piece(layer, 1, h).wait_send()
            dz_relay(layer, h).wait_send()

    def part(b):
        return m if b < 2 else 1 - m

    def line_copy(layer, b, to, frm):
        return pltpu.make_async_remote_copy(
            src_ref=wpart.at[layer, b, rows_of(to * rc, rc), :],
            dst_ref=zr.at[layer, b, frm],
            send_sem=zr_sem.at[0, layer, b, to],
            recv_sem=zr_sem.at[1, layer, b, frm],
            device_id=(to * 4 + p, m),
            device_id_type=MESH,
        )

    def once(key):
        fresh = key not in kept
        kept[key] = True
        return fresh

    def product(layer, b):
        hr, hc = quarter(layer, 3)
        h = b % 2
        if b >= 2 and once(("y", layer)):
            for who in range(3):
                y_pass_copy(layer, who, 1 - m).wait_recv()
        if once(("dz", layer, h)):
            dz_piece(layer, 1 - z_first(layer), h).wait_recv()
            dz_relay(layer, h).wait_recv()
        own_dz = dz_ref[layer, :, rows_of(hc * half + h * ct, ct)]

        def one(i, _):
            start = part(b) * half + i * ct
            acc = mm(yt[layer, rows_of(hr * cols + start, ct), :], own_dz)
            for who in range(3):
                acc = acc + mm(yr[layer, who, rows_of(start, ct), :], dzr[layer, who, h])
            wpart[layer, b, rows_of(i * ct, ct), :] = acc.astype(BF)
            return 0

        lax.fori_loop(0, half // ct, one, 0)

        def send(i, _):
            line_copy(layer, b, (zi + i) % line, zi).start()
            return 0

        lax.fori_loop(1, line, send, 0)

    def flip_bit(e, d):
        return e + d - 2 * d * ((e // d) % 2)

    def spot(layer, b, e):
        ex, ey = e % 2, (e // 2) % 2
        hr, hc = (ex, ey) if layer == 1 else (ey, ex)
        return wg_hbm.at[
            layer,
            rows_of(hr * cols + part(b) * half + (e // 4) * rc, rc),
            rows_of(hc * half + (b % 2) * ct, ct),
        ]

    def held(base, dims):
        got = [base]
        for d in dims:
            got = got + [flip_bit(e, d) for e in got]
        return got

    def far_copy(layer, b, to, frm):
        return pltpu.make_async_remote_copy(
            src_ref=fin.at[layer, b],
            dst_ref=spot(layer, b, frm),
            send_sem=az_sem.at[0, layer, b, to // 8],
            recv_sem=az_sem.at[1, layer, b, frm // 8],
            device_id=(to, m),
            device_id_type=MESH,
        )

    def hops(layer, b, i, step, arriving):
        own = isinstance(i, int)
        dims = ORDERS[layer][b][0 if own else 1]
        base = (c + 8 * i) % n
        other = flip_bit(c, dims[step])
        slot = 2**step - 1
        copies = []
        for j, e in enumerate(held(base, dims[:step])):
            if arriving:
                e = flip_bit(e, dims[step])
            src = fin.at[layer, b] if own and j == 0 and not arriving else spot(layer, b, e)
            copies.append(
                remote(src, spot(layer, b, e), ag_sem, (layer, b, base // 8, slot + j), (other, m))
            )
        return copies

    def keep(layer, b):
        return pltpu.make_async_copy(
            fin.at[layer, b], spot(layer, b, c), fin_sem.at[layer, b]
        )

    def combine(layer, b):
        def take(i, _):
            frm = (zi + i) % line
            copy = line_copy(layer, b, frm, frm)
            copy.wait_recv()
            copy.wait_send()
            return 0

        lax.fori_loop(1, line, take, 0)
        zr[layer, b, zi] = wpart[layer, b, rows_of(zi * rc, rc), :]
        fin[layer, b] = lax.fori_loop(
            1, line,
            lambda j, t: t + zr[layer, b, j].astype(F32),
            zr[layer, b, 0].astype(F32),
        ).astype(BF)
        keep(layer, b).start()

        def send(i, _):
            far_copy(layer, b, (c + 8 * i) % n, c).start()
            return 0

        lax.fori_loop(1, far, send, 0)
        gather_own(layer, b, 0)

    def gather_own(layer, b, step):
        if step > 0:
            for copy in hops(layer, b, 0, step - 1, True):
                copy.wait_recv()
        for copy in hops(layer, b, 0, step, False):
            copy.start()
        if step > 0:
            for copy in hops(layer, b, 0, step - 1, False):
                copy.wait_send()

    def gather_far(layer, b, step):
        def one(i, _):
            if step == 0:
                frm = (c + 8 * i) % n
                far_copy(layer, b, frm, frm).wait_recv()
            else:
                for copy in hops(layer, b, i, step - 1, True):
                    copy.wait_recv()
            for copy in hops(layer, b, i, step, False):
                copy.start()
            if step > 0:
                for copy in hops(layer, b, i, step - 1, False):
                    copy.wait_send()
            return 0

        lax.fori_loop(1, far, one, 0)

    def gather_finish(layer, b):
        keep(layer, b).wait()

        def ends(i):
            for copy in hops(layer, b, i, 2, True):
                copy.wait_recv()
            for copy in hops(layer, b, i, 2, False):
                copy.wait_send()

        def one(i, _):
            far_copy(layer, b, (c + 8 * i) % n, c).wait_send()
            ends(i)
            return 0

        ends(0)
        lax.fori_loop(1, far, one, 0)

    w_copies = [
        pltpu.make_async_copy(w_hbm.at[layer], w_ref.at[layer], w_sem.at[layer])
        for layer in range(2)
    ]
    og_copy = pltpu.make_async_copy(og_hbm, og_ref, og_sem)
    in_copies = [
        pltpu.make_async_copy(src, dst, in_sem.at[i])
        for i, (src, dst) in enumerate(
            (
                (rows_hbm, rows_ref), (f_hbm, f_ref), (ids_hbm, ids_ref), (ew_hbm, ew_ref),
                (sw_hbm, sw_ref), (valid_hbm, valid_ref), (bias_hbm, bias_ref),
                (gain_hbm, gain_ref), (shift_hbm, shift_ref),
            )
        )
    ]
    small_copies = [
        pltpu.make_async_copy(src, dst, out_sem.at[2 + i])
        for i, (src, dst) in enumerate(
            ((bias_out, bias_res), (gain_out, gain_res), (shift_out, shift_res))
        )
    ]
    out_copy = pltpu.make_async_copy(out_ref, out_hbm, out_sem.at[0])
    ig_copy = pltpu.make_async_copy(h1_ref, ig_hbm, out_sem.at[1])

    def begin():
        for copy in in_copies:
            copy.start()
        barrier = pltpu.get_barrier_semaphore()

        def greet(i, _):
            pl.semaphore_signal(
                barrier, inc=1, device_id=(lax.rem(c + i, n), m), device_id_type=MESH
            )
            return 0

        lax.fori_loop(1, n, greet, 0)
        pl.semaphore_signal(barrier, inc=1, device_id=peer, device_id_type=MESH)
        w_copies[0].start()
        og_copy.start()
        w_copies[1].start()

        in_copies[0].wait()
        lane = lax.broadcasted_iota(jnp.int32, (cap, halo), 1)
        spread = jnp.zeros((cap, halo), F32)
        for d in range(n):
            mine = rows_ref[0, :, d : d + 1].astype(F32)
            spread = jnp.where((lane >= d * cap) & (lane < (d + 1) * cap), mine, spread)
        place_q = lax.broadcasted_iota(jnp.int32, (cap, halo), 0)
        wanted = jnp.sum(jnp.where(lane % cap == place_q, spread, 0.0), axis=0, keepdims=True)
        rows_row[...] = wanted.astype(jnp.int32)

        def choose(i, _):
            r = rows_of(i * 128, 128)
            one_hot = jnp.where(
                rows_row[:, r] == lax.broadcasted_iota(jnp.int32, (nodes, 128), 0), 1.0, 0.0
            )
            sel_t[:, r] = one_hot.astype(BF)
            sel[r, :] = one_hot.T.astype(BF)
            return 0

        lax.fori_loop(0, halo // 128, choose, 0)
        in_copies[1].wait()
        pick(f_ref)
        pl.semaphore_wait(barrier, n)
        halo_start()
        for copy in in_copies[2:]:
            copy.wait()
        mask_ref[...] = jnp.broadcast_to(valid_ref[...].astype(F32), (128, nodes)).T
        rb = 16
        place = lax.broadcasted_iota(jnp.int32, (rb, nodes), 0)
        node = lax.broadcasted_iota(jnp.int32, (rb, nodes), 1)

        def build(i, _):
            def rows(j, _):
                slots = place + (i * 128 + j * rb)
                a = jnp.where(node == slots, 2.0 * sw_ref[...], 0.0)
                for k in range(fan):
                    a = a + jnp.where(ids_ref[k : k + 1, :] == slots, ew_ref[k : k + 1, :], 0.0)
                a_block[rows_of(j * rb, rb), :] = a
                return 0

            lax.fori_loop(0, 128 // rb, rows, 0)
            r = rows_of(i * 128, 128)
            a = a_block[...]
            high = a.astype(BF)
            adj_t[r, :] = high
            if exact:
                adj_tlo[r, :] = (a - high.astype(F32)).astype(BF)
            a = a.T
            high = a.astype(BF)
            adj[:, r] = high
            if exact:
                adj_lo[:, r] = (a - high.astype(F32)).astype(BF)
            return 0

        lax.fori_loop(0, lookup // 128, build, 0)

    def ahead(what, x):
        got = mm(adj[:, what], x)
        return got + mm(adj_lo[:, what], x) if exact else got

    def back(what, x):
        got = mm(adj_t[what, :], x)
        return got + mm(adj_tlo[what, :], x) if exact else got

    inner, outer = slice(0, nodes), slice(nodes, lookup)

    def agg_local(layer):
        src = f_ref if layer == 0 else h1_ref
        for h in range(2):
            cs = slice(h * half, (h + 1) * half)
            zacc[:, cs] = ahead(inner, src[:, cs])

    def mp_copy(k, src, dst):
        return remote(src, dst, mp_sem, (k,), peer)

    def y_exchange(layer, h):
        ref = yf.at[layer, m, :, slice(h * half, (h + 1) * half)]
        return mp_copy(layer * 2 + h, ref, ref)

    def agg_halo(layer):
        parts = halo_finish()
        for h in range(2):
            cs = slice(h * half, (h + 1) * half)
            yf[layer, m, :, cs] = (zacc[:, cs] + ahead(outer, parts[h])).astype(BF)
            y_exchange(layer, h).start()

    def z_own(layer):
        w_copies[layer].wait()

        zacc[...] = mm(yf[layer, m], w_ref[layer, rows_of(m * cols, cols), :])
        for h in range(2):
            y_exchange(layer, h).wait_recv()

    def z_other(layer):
        if layer == 1:
            og_copy.wait()
        own_count = jnp.sum(mask_ref[...], axis=0, keepdims=True)
        own_count = jnp.concatenate([own_count] * (ct // 128), axis=1)
        own_inv = 1.0 / jnp.maximum(own_count, 1.0)

        zacc[...] += mm(yf[layer, 1 - m], w_ref[layer, rows_of((1 - m) * cols, cols), :])

        def second(j, _):
            z = zacc[:, col(j)] + bias_ref[layer : layer + 1, col(j)]
            sig = jax.nn.sigmoid(z)
            s = z * sig
            s_ref[layer, :, col(j)] = s
            d_ref[layer, :, col(j)] = (sig * (1.0 + z * (1.0 - sig))).astype(d_ref.dtype)
            valid = mask(ct)
            tot = jnp.sum(s * valid, axis=0, keepdims=True)
            cen = s - tot * own_inv
            st_row[0:1, col(j)] = tot
            st_row[1:2, col(j)] = jnp.sum(cen * cen * valid, axis=0, keepdims=True)
            if layer == 0:
                st_row[2:3, col(j)] = own_count
            else:
                pg = og_ref[:, col(j)].astype(F32) * valid
                st_row[2:3, col(j)] = jnp.sum(pg, axis=0, keepdims=True)
                st_row[3:4, col(j)] = jnp.sum(pg * cen, axis=0, keepdims=True)
            return 0

        lax.fori_loop(0, tiles, second, 0)
        buf = stat0 if layer == 0 else stat1
        for k in range(3 if layer == 0 else 4):
            fold(buf, k, k)

    def stats_out(layer):
        stat_start(layer, stat0 if layer == 0 else stat1)
        for h in range(2):
            y_exchange(layer, h).wait_send()
        y_flip(layer)

    def normalize(layer):
        buf = stat0 if layer == 0 else stat1
        stat_finish(layer, buf)
        count = jnp.maximum(total(stat0, 2), 1.0)
        mu = total(buf, 0) / count

        def spread(s, t):
            nc = stat0[s, 2]
            off = buf[s, 0] / jnp.maximum(nc, 1.0) - mu
            return t + buf[s, 1] + nc * off * off

        var = lax.fori_loop(0, n, spread, jnp.zeros_like(mu)) / count
        inv = lax.rsqrt(var + EPS)
        at = 8 if layer == 0 else 4
        unfold(mu, at)
        unfold(inv, at + 1)
        mu_row, inv_row = st_row[at : at + 1, :], st_row[at + 1 : at + 2, :]
        gain_row = gain_ref[layer : layer + 1, :]
        shift_row = shift_ref[layer : layer + 1, :]
        dst = h1_ref if layer == 0 else out_ref
        for j in range(tiles):
            cs = slice(j * ct, (j + 1) * ct)
            x = (s_ref[layer, :, cs] - mu_row[:, cs]) * inv_row[:, cs]
            dst[:, cs] = (mask(ct) * (gain_row[:, cs] * x + shift_row[:, cs])).astype(BF)
        if layer == 0:
            pick(h1_ref)
            return
        out_copy.start()

        def gains(s, t):
            off = stat1[s, 0] / jnp.maximum(stat0[s, 2], 1.0) - mu
            return t + stat1[s, 3] + off * stat1[s, 2]

        unfold(total(stat1, 2), 6)
        unfold(inv * lax.fori_loop(0, n, gains, jnp.zeros_like(mu)), 7)
        unfold(1.0 / count, 10)
        norm_sums(1)
        pre_grad(1)
        fold(stat2, 2, 11)

    def norm_sums(layer):
        gain_out[layer : layer + 1, :] = st_row[7:8, :]
        shift_out[layer : layer + 1, :] = st_row[6:7, :]

    def pre_grad(layer):
        at = 8 if layer == 0 else 4
        grad_src = og_ref if layer == 1 else g_ref

        def pre(j, _):
            gain = gain_ref[layer : layer + 1, col(j)]
            inv_row = st_row[at + 1 : at + 2, col(j)]
            ic = st_row[10:11, col(j)]
            x = (s_ref[layer, :, col(j)] - st_row[at : at + 1, col(j)]) * inv_row
            valid = mask(ct)
            pg = grad_src[:, col(j)].astype(F32) * valid
            ds = (
                valid
                * (inv_row * gain)
                * (pg - st_row[6:7, col(j)] * ic - x * (st_row[7:8, col(j)] * ic))
            )
            dz = (ds * d_ref[layer, :, col(j)].astype(F32)).astype(BF)
            dz_ref[layer, :, col(j)] = dz
            st_row[11:12, col(j)] = jnp.sum(dz.astype(F32), axis=0, keepdims=True)
            return 0

        lax.fori_loop(0, tiles, pre, 0)

    def dy_copy(layer):
        return mp_copy(4 + layer, dy_send, dy_recv.at[layer])

    def dy_other(layer):
        theirs = w_ref[layer, rows_of((1 - m) * cols, cols), :]
        dy_send[...] = mm_t(dz_ref[layer], theirs).astype(BF)
        dy_copy(layer).start()

    def dy_mine(layer):
        dy_own[...] = mm_t(dz_ref[layer], w_ref[layer, rows_of(m * cols, cols), :])
        dy_copy(layer).wait_recv()
        for j in range(tiles):
            cs = slice(j * ct, (j + 1) * ct)
            dyb[:, cs] = (dy_own[:, cs] + dy_recv[layer, :, cs].astype(F32)).astype(BF)
        pack_halo(back(outer, dyb[:, :half]), back(outer, dyb[:, half:]))
        halo_start()

    def back_local(layer):
        for h in range(2):
            cs = slice(h * half, (h + 1) * half)
            g_ref[:, cs] = back(inner, dyb[:, cs])
        dy_copy(layer).wait_send()

    def back_halo(layer):
        parts = halo_finish()
        for h in range(2):
            cs = slice(h * half, (h + 1) * half)
            got = g_ref[:, cs] + mm(sel_t[...], parts[h])
            if layer == 1:
                g_ref[:, cs] = got
                pg = got * mask(half)
                x = (s_ref[0, :, cs] - st_row[8:9, cs]) * st_row[9:10, cs]
                st_row[0:1, cs] = jnp.sum(pg, axis=0, keepdims=True)
                st_row[1:2, cs] = jnp.sum(pg * x, axis=0, keepdims=True)
            else:
                h1_ref[:, cs] = got.astype(BF)
        if layer == 1:
            fold(stat2, 0, 0)
            fold(stat2, 1, 1)
            stat_start(2, stat2)
        else:
            ig_copy.start()

    def back_norm():
        stat_finish(2, stat2)
        unfold(total(stat2, 0), 6)
        unfold(total(stat2, 1), 7)
        unfold(total(stat2, 2), 12)
        norm_sums(0)
        bias_out[1:2, :] = st_row[12:13, :]
        pre_grad(0)
        fold(stat3, 0, 11)
        stat_start(3, stat3)

    table = {
        "A0": lambda: (begin(), agg_local(0), agg_halo(0), z_own(0), z_other(0)),
        "A": lambda: stats_out(0),
        "B0": lambda: normalize(0),
        "B": halo_start,
        "B1": lambda: (agg_local(1), agg_halo(1)),
        "B2": lambda: z_own(1),
        "C": lambda: (z_other(1), stats_out(1)),
        "C2": lambda: normalize(1),
        "C3": lambda: dy_other(1),
        "D": lambda: dy_mine(1),
        "E": lambda: (back_local(1), back_halo(1)),
        "E2": back_norm,
        "E3": lambda: dy_other(0),
        "F": lambda: dy_mine(0),
        "G": lambda: back_local(0),
        "IG": lambda: back_halo(0),
        "ys": lambda l, who, k: y_piece(l, who, k).start(),
        "yf": y_forward,
        "yp": y_pass,
        "ds": lambda l, who, h: dz_piece(l, who, h).start(),
        "df": dz_forward,
        "pr": product,
        "cb": combine,
        "go": gather_own,
        "gf": gather_far,
    }
    for name, *args in SCHEDULE:
        table[name](*args)

    stat_finish(3, stat3)
    unfold(total(stat3, 0), 12)
    bias_out[0:1, :] = st_row[12:13, :]
    for copy in small_copies:
        copy.start()
    out_copy.wait()
    ig_copy.wait()
    for layer in (1, 0):
        y_sent(layer)
        dz_sent(layer)
        for b in range(4):
            gather_finish(layer, b)
    for copy in small_copies:
        copy.wait()


def hand_over(
    rows, slots,
    wg_hbm, out_in, ig_in, bias_in, gain_in, shift_in,
    wg_out, out_out, ig_out, bias_out, gain_out, shift_out,
    wide, through, in_sem, wide_sem, pass_sem, *narrow,
):
    blocks = in_sem.shape[0]
    per_layer = wg_hbm.shape[1] // rows

    def block(ref, i):
        return ref.at[i // per_layer, pl.ds((i % per_layer) * rows, rows), :]

    resident = not narrow

    def read(i):
        return pltpu.make_async_copy(block(wg_hbm, i), narrow[0].at[i], in_sem.at[i])

    def write(i):
        return pltpu.make_async_copy(wide.at[i % slots], block(wg_out, i), wide_sem.at[i])

    takes = [
        pltpu.make_async_copy(ref, through.at[i], pass_sem.at[0, i])
        for i, ref in enumerate((out_in, ig_in))
    ]
    gives = [
        pltpu.make_async_copy(through.at[i], ref, pass_sem.at[1, i])
        for i, ref in enumerate((out_out, ig_out))
    ]
    for i in range(blocks):
        if not resident:
            read(i).start()
        if i == 1:
            for copy in takes:
                copy.start()
    for i in range(blocks):
        if not resident:
            read(i).wait()
        if i >= slots:
            write(i - slots).wait()
        wide[i % slots] = (block(wg_hbm, i) if resident else narrow[0].at[i])[...].astype(F32)
        write(i).start()
        if i == 2:
            for take, give in zip(takes, gives):
                take.wait()
                give.start()
    bias_out[...] = bias_in[...]
    gain_out[...] = gain_in[...]
    shift_out[...] = shift_in[...]
    for i in range(blocks - slots, blocks):
        write(i).wait()
    for give in gives:
        give.wait()


def per_device(
    features, neighbour_ids, edge_weight, self_weight, send_rows, valid_mask,
    weights, biases, norm_gain, norm_shift, output_grad,
):
    nodes, cols = features.shape
    fan = neighbour_ids.shape[1]
    n, cap = send_rows.shape[1], send_rows.shape[2]
    halo = n * cap
    lookup = nodes + halo
    line = n // 4
    half = cols // 2
    vm = pl.BlockSpec(memory_space=pltpu.VMEM)
    anyspace = pl.BlockSpec(memory_space=pl.ANY)
    dma = pltpu.SemaphoreType.DMA
    small = jax.ShapeDtypeStruct((2, cols), F32)
    wide_block = jax.ShapeDtypeStruct((nodes, cols), BF)
    resident = n <= 16
    place = pltpu.VMEM if resident else jax.ShapeDtypeStruct
    out, ig, wg, bias, gain, shift = pl.pallas_call(
        functools.partial(chain, n, cap, fan, resident),
        out_shape=(
            place((nodes, cols), BF), place((nodes, cols), BF), place((2, 2 * cols, cols), BF),
            *[place((2, cols), F32) for _ in range(3)],
        ),
        in_specs=[anyspace] * 11,
        out_specs=(anyspace,) * 6,
        scratch_shapes=[
            pltpu.VMEM((nodes, cols), BF),
            pltpu.VMEM((1, cap, n), jnp.int32),
            pltpu.VMEM((fan, nodes), jnp.int32),
            pltpu.VMEM((fan, nodes), F32),
            pltpu.VMEM((1, nodes), F32),
            pltpu.VMEM((1, nodes), jnp.int32),
            *[pltpu.VMEM((2, cols), F32) for _ in range(6)],
            pltpu.VMEM((1, halo), jnp.int32),
            dma((9,)),
            pltpu.VMEM((2, 2 * cols, cols), BF),
            pltpu.VMEM((nodes, cols), BF),
            pltpu.VMEM((nodes, lookup), BF),
            pltpu.VMEM((nodes if resident else 16, lookup), BF),
            pltpu.VMEM((lookup, nodes), BF),
            pltpu.VMEM((lookup if resident else 16, nodes), BF),
            pltpu.VMEM((128, nodes), F32),
            pltpu.VMEM((halo, nodes), BF),
            pltpu.VMEM((nodes, halo), BF),
            pltpu.VMEM((nodes, 128), F32),
            pltpu.VMEM((nodes, cols), BF),
            pltpu.VMEM((2, 2, nodes, cols), BF),
            pltpu.VMEM((2, nodes, cols), F32),
            pltpu.VMEM((2, nodes, cols), F32 if resident else BF),
            pltpu.VMEM((nodes, cols), F32),
            pltpu.VMEM((2, nodes, cols), BF),
            pltpu.VMEM((2 * halo, half), BF),
            pltpu.VMEM((2 * halo, half), BF),
            pltpu.VMEM((16, cols), F32),
            pltpu.VMEM((n, 3, 8, cols // 8), F32),
            pltpu.VMEM((n, 4, 8, cols // 8), F32),
            pltpu.VMEM((n, 3, 8, cols // 8), F32),
            pltpu.VMEM((n, 1, 8, cols // 8), F32),
            pltpu.VMEM((2, 2 * cols, nodes), BF),
            pltpu.VMEM((2, 3, cols, nodes), BF),
            pltpu.VMEM((2, 3, 2, nodes, cols // 4), BF),
            pltpu.VMEM((2, 4, half, cols // 4), BF),
            pltpu.VMEM((2, 4, line, half // line, cols // 4), BF),
            pltpu.VMEM((2, 4, half // line, cols // 4), BF),
            dma((2,)), dma, dma((5,)), dma((2, 6)), dma((2,)), dma((2, 2)),
            dma((2, 2, 3, 4)), dma((2, 2, 3)), dma((2, 2, 3, 2)),
            dma((2, 2, 4, line)), dma((2, 2, 4, n // 8)), dma((2, 2, 4, n // 8, 7)), dma((2, 4)),
        ],
        compiler_params=pltpu.CompilerParams(
            collective_id=0,
            has_side_effects=True,
            vmem_limit_bytes=(53 if resident else 62) * 2**20,
        ),
    )(
        features, jnp.swapaxes(send_rows, 1, 2), neighbour_ids.T, edge_weight.T,
        self_weight.reshape(1, nodes), valid_mask.reshape(1, nodes), biases, norm_gain, norm_shift,
        output_grad, weights,
    )
    if resident:
        out, ig, wg, bias, gain, shift = (
            pltpu.with_memory_space_constraint(v, pltpu.VMEM)
            for v in (out, ig, wg, bias, gain, shift)
        )
    rows, slots = 512, 4
    blocks = 2 * 2 * cols // rows
    wg, out, ig, bias, gain, shift = pl.pallas_call(
        functools.partial(hand_over, rows, slots),
        out_shape=(
            jax.ShapeDtypeStruct((2, 2 * cols, cols), F32), wide_block, wide_block,
            small, small, small,
        ),
        in_specs=[vm if resident else anyspace] + [anyspace] * 2 + [vm] * 3,
        out_specs=(anyspace, anyspace, anyspace, vm, vm, vm),
        scratch_shapes=[
            pltpu.VMEM((slots, rows, cols), F32),
            pltpu.VMEM((2, nodes, cols), BF),
            dma((blocks,)), dma((blocks,)), dma((2, 2)),
            *([] if resident else [pltpu.VMEM((blocks, rows, cols), BF)]),
        ],
        compiler_params=pltpu.CompilerParams(vmem_limit_bytes=(40 if resident else 62) * 2**20),
    )(wg, out, ig, bias, gain, shift)
    return out, ig, wg, bias, gain, shift


def solution(mesh):
    return jax.shard_map(
        per_device,
        mesh=mesh,
        in_specs=(
            P("cluster", "mp"),
            P("cluster", None),
            P("cluster", None),
            P("cluster"),
            P("cluster", None, None),
            P("cluster"),
            P(None, None, "mp"),
            P(None, "mp"),
            P(None, "mp"),
            P(None, "mp"),
            P("cluster", "mp"),
        ),
        out_specs=(
            P("cluster", "mp"),
            P("cluster", "mp"),
            P(None, None, "mp"),
            P(None, "mp"),
            P(None, "mp"),
            P(None, "mp"),
        ),
        check_vma=False,
    )
```

```python
import functools

import jax
import jax.numpy as jnp
from jax import lax
from jax.experimental import pallas as pl
from jax.experimental.pallas import tpu as pltpu
from jax.sharding import PartitionSpec as P

EPS = 1e-05
MESH = pl.DeviceIdType.MESH
BF = jnp.bfloat16
F32 = jnp.float32

SCHEDULE = (
    ("A0",),
    ("A",), ("ys", 0, 1, 2),
    ("B0",),
    ("B",), ("ys", 0, 1, 3), ("ys", 0, 1, 0), ("ys", 0, 0, 2), ("ys", 0, 0, 0),
    ("B1",), ("ys", 0, 0, 3), ("ys", 0, 0, 1), ("ys", 0, 1, 1),
    ("B2",),
    ("C",), ("ys", 1, 1, 0), ("ys", 1, 0, 2), ("ys", 1, 0, 1), ("ys", 1, 1, 3), ("ys", 1, 1, 2), ("ys", 1, 0, 0),
    ("C2",), ("ds", 1, 1, 1), ("ds", 1, 0, 1),
    ("C3",),
    ("D",), ("ys", 1, 1, 1), ("yf", 1, 2), ("yf", 1, 1), ("df", 1, 1), ("ys", 1, 0, 3), ("yp", 0, 0),
    ("E",), ("yf", 1, 0), ("yf", 1, 3), ("ds", 1, 0, 0), ("yp", 1, 1),
    ("E2",), ("yf", 0, 1), ("ds", 0, 0, 0), ("ds", 1, 1, 0), ("yp", 1, 0), ("yp", 1, 2), ("pr", 1, 1), ("pr", 1, 3),
    ("ds", 0, 1, 0), ("df", 1, 0), ("ds", 0, 0, 1), ("ds", 0, 1, 1), ("cb", 1, 1), ("yf", 0, 3), ("cb", 1, 3),
    ("go", 1, 1, 1), ("pr", 1, 0), ("df", 0, 0), ("yf", 0, 2), ("df", 0, 1), ("go", 1, 3, 1), ("yf", 0, 0),
    ("gf", 1, 3, 0), ("pr", 1, 2), ("go", 1, 1, 2), ("gf", 1, 3, 1), ("cb", 1, 0),
    ("E3",), ("gf", 1, 1, 0), ("yp", 0, 1), ("cb", 1, 2), ("yp", 0, 2), ("pr", 0, 1), ("gf", 1, 0, 0),
    ("go", 1, 0, 1), ("pr", 0, 0), ("go", 1, 0, 2), ("gf", 1, 1, 1), ("cb", 0, 1), ("gf", 1, 0, 1), ("gf", 1, 2, 0),
    ("go", 1, 2, 1), ("go", 1, 3, 2), ("pr", 0, 2), ("gf", 1, 1, 2), ("gf", 1, 0, 2), ("pr", 0, 3), ("gf", 0, 1, 0),
    ("gf", 1, 3, 2), ("gf", 1, 2, 1), ("go", 0, 1, 1), ("gf", 0, 1, 1), ("go", 1, 2, 2), ("cb", 0, 2), ("cb", 0, 3),
    ("cb", 0, 0),
    ("F",), ("gf", 0, 2, 0), ("go", 0, 2, 1), ("go", 0, 0, 1), ("go", 0, 1, 2), ("gf", 0, 1, 2), ("gf", 0, 0, 0),
    ("gf", 0, 3, 0), ("gf", 0, 2, 1), ("gf", 1, 2, 2),
    ("G",), ("go", 0, 0, 2), ("gf", 0, 0, 1),
    ("IG",), ("gf", 0, 3, 1), ("go", 0, 3, 1), ("gf", 0, 2, 2), ("gf", 0, 0, 2), ("go", 0, 3, 2), ("go", 0, 2, 2),
    ("gf", 0, 3, 2),
)
ORDERS = (
    (
        ((1, 2, 4), (4, 1, 2)),
        ((4, 2, 1), (1, 4, 2)),
        ((2, 1, 4), (4, 2, 1)),
        ((4, 2, 1), (4, 1, 2)),
    ),
    (
        ((4, 2, 1), (4, 1, 2)),
        ((4, 2, 1), (4, 2, 1)),
        ((1, 4, 2), (2, 1, 4)),
        ((4, 1, 2), (4, 2, 1)),
    ),
)


def mm(a, b):
    return jnp.dot(a, b, preferred_element_type=F32)


def mm_t(a, b):
    return lax.dot_general(a, b, (((1,), (1,)), ((), ())), preferred_element_type=F32)


def chain(
    n, cap, fan, exact,
    f_hbm, rows_hbm, ids_hbm, ew_hbm, sw_hbm, valid_hbm, bias_hbm, gain_hbm, shift_hbm, og_hbm, w_hbm,
    out_hbm, ig_hbm, wg_hbm, bias_res, gain_res, shift_res,
    f_ref, rows_ref, ids_ref, ew_ref, sw_ref, valid_ref, bias_ref, gain_ref, shift_ref,
    bias_out, gain_out, shift_out, rows_row, in_sem,
    w_ref, og_ref, adj, adj_lo, adj_t, adj_tlo, a_block, sel, sel_t, mask_ref, h1_ref, yf, s_ref, d_ref, zacc,
    dy_recv, hsend, hrecv, st_row, stat0, stat1, stat2, stat3,
    yt, yr, dzr, wpart, zr, fin,
    w_sem, og_sem, out_sem, mp_sem, h_sem, x_sem,
    y_sem, yp_sem, dz_sem, zr_sem, az_sem, ag_sem, fin_sem,
):
    nodes, cols = f_hbm.shape
    ct = 256
    tiles = cols // ct
    half = cols // 2
    c = lax.axis_index("cluster")
    m = lax.axis_index("mp")
    peer = (c, 1 - m)
    halo = n * cap
    lookup = nodes + halo
    line, far = n // 4, n // 8
    zi, p = c // 4, c % 4
    px, py = p % 2, p // 2
    near = (c + 1 - 2 * px, c + 2 - 4 * py)
    rc = half // line
    dy_own, dyb, g_ref = zacc, og_ref, s_ref.at[1]
    out_ref, dy_send, dz_ref = yf.at[0, 0], yf.at[0, 1], yf.at[1]
    pieces = 4
    prow = half // pieces
    lanes = cols // 8
    kept = {}

    def rows_of(start, size):
        return pl.ds(pl.multiple_of(start, size), size)

    def col(j):
        return rows_of(j * ct, ct)

    def remote(src, dst, sems, idx, to):
        return pltpu.make_async_remote_copy(
            src_ref=src,
            dst_ref=dst,
            send_sem=sems.at[(0, *idx)],
            recv_sem=sems.at[(1, *idx)],
            device_id=to,
            device_id_type=MESH,
        )

    def mask(width):
        return jnp.concatenate([mask_ref[...]] * (width // 128), axis=1)

    def halo_part(d):
        return rows_of(d * 2 * cap, 2 * cap)

    def pack_halo(left, right):
        both = jnp.concatenate(
            [left.reshape(n, cap, half), right.reshape(n, cap, half)], axis=1
        )
        hsend[...] = both.reshape(n * 2 * cap, half).astype(BF)

    def wait_all(ref, size, sem):
        some = ref.at[pl.ds(0, size)]
        pltpu.make_async_copy(some, some, sem).wait()

    def halo_copy(to, frm):
        return pltpu.make_async_remote_copy(
            src_ref=hsend.at[halo_part(to)],
            dst_ref=hrecv.at[halo_part(frm)],
            send_sem=h_sem.at[0],
            recv_sem=h_sem.at[1],
            device_id=(to, m),
            device_id_type=MESH,
        )

    def halo_start():
        def send(i, _):
            halo_copy(lax.rem(c + i, n), c).start()
            return 0

        lax.fori_loop(1, n, send, 0)
        hrecv[halo_part(c)] = hsend[halo_part(c)]

    def halo_finish():
        wait_all(hsend, (n - 1) * 2 * cap, h_sem.at[0])
        wait_all(hrecv, (n - 1) * 2 * cap, h_sem.at[1])
        got = hrecv[...].astype(F32).reshape(n, 2 * cap, half)
        left = got[:, :cap, :].reshape(halo, half).astype(BF)
        right = got[:, cap:, :].reshape(halo, half).astype(BF)
        return left, right

    def pick(src):
        pack_halo(mm(sel[...], src[:, :half]), mm(sel[...], src[:, half:]))

    def stat_copy(e, buf, to, frm):
        return pltpu.make_async_remote_copy(
            src_ref=buf.at[c],
            dst_ref=buf.at[frm],
            send_sem=x_sem.at[0, e % 2],
            recv_sem=x_sem.at[1, e % 2],
            device_id=(to, m),
            device_id_type=MESH,
        )

    def stat_start(e, buf):
        def send(i, _):
            stat_copy(e, buf, lax.rem(c + i, n), c).start()
            return 0

        lax.fori_loop(1, n, send, 0)

    def stat_finish(e, buf):
        for way in range(2):
            wait_all(buf, n - 1, x_sem.at[way, e % 2])

    def fold(buf, k, row):
        for g in range(8):
            buf[c, k, g : g + 1, :] = st_row[row : row + 1, g * lanes : (g + 1) * lanes]

    def unfold(tile, row):
        for g in range(8):
            st_row[row : row + 1, g * lanes : (g + 1) * lanes] = tile[g : g + 1, :]

    def total(buf, k):
        return lax.fori_loop(1, n, lambda s, t: t + buf[s, k], buf[0, k])

    def quarter(layer, who):
        qx = 1 - px if who in (0, 2) else px
        qy = 1 - py if who in (1, 2) else py
        return (qx, qy) if layer == 1 else (qy, qx)

    def y_flip(layer):
        def flip(i, _):
            r = rows_of(i * 128, 128)
            for h in range(2):
                yt[layer, rows_of(h * cols + i * 128, 128), :] = (
                    yf[layer, h, :, r].astype(F32).T.astype(BF)
                )
            return 0

        lax.fori_loop(0, cols // 128, flip, 0)

    def y_piece(layer, who, k):
        hr, _ = quarter(layer, who)
        return remote(
            yt.at[layer, rows_of(hr * cols + m * half + k * prow, prow), :],
            yr.at[layer, who, rows_of(m * half + k * prow, prow), :],
            y_sem, (layer, who, k), (near[who], m),
        )

    def y_first(layer):
        return 1 - layer

    def z_first(layer):
        return layer

    def y_relay(layer, k):
        first = y_first(layer)
        r = rows_of(m * half + k * prow, prow)
        return remote(
            yr.at[layer, first, r, :], yr.at[layer, 2, r, :], y_sem, (layer, 2, k),
            (near[1 - first], m),
        )

    def y_forward(layer, k):
        y_piece(layer, y_first(layer), k).wait_recv()
        y_relay(layer, k).start()

    def y_pass_copy(layer, who, part):
        r = rows_of(part * half, half)
        return remote(
            yr.at[layer, who, r, :], yr.at[layer, who, r, :], yp_sem, (layer, who), peer
        )

    def y_pass(layer, who):
        if who != y_first(layer):
            for k in range(pieces):
                copy = y_relay(layer, k) if who == 2 else y_piece(layer, who, k)
                copy.wait_recv()
        y_pass_copy(layer, who, m).start()

    def y_sent(layer):
        for k in range(pieces):
            y_piece(layer, 0, k).wait_send()
            y_piece(layer, 1, k).wait_send()
            y_relay(layer, k).wait_send()
        for who in range(3):
            y_pass_copy(layer, who, m).wait_send()

    def dz_piece(layer, who, h):
        _, hc = quarter(layer, who)
        return remote(
            dz_ref.at[layer, :, rows_of(hc * half + h * ct, ct)],
            dzr.at[layer, who, h],
            dz_sem, (layer, who, h), (near[who], m),
        )

    def dz_relay(layer, h):
        first = z_first(layer)
        return remote(
            dzr.at[layer, first, h], dzr.at[layer, 2, h], dz_sem, (layer, 2, h),
            (near[1 - first], m),
        )

    def dz_forward(layer, h):
        dz_piece(layer, z_first(layer), h).wait_recv()
        dz_relay(layer, h).start()

    def dz_sent(layer):
        for h in range(2):
            dz_piece(layer, 0, h).wait_send()
            dz_piece(layer, 1, h).wait_send()
            dz_relay(layer, h).wait_send()

    def part(b):
        return m if b < 2 else 1 - m

    def line_copy(layer, b, to, frm):
        return pltpu.make_async_remote_copy(
            src_ref=wpart.at[layer, b, rows_of(to * rc, rc), :],
            dst_ref=zr.at[layer, b, frm],
            send_sem=zr_sem.at[0, layer, b, to],
            recv_sem=zr_sem.at[1, layer, b, frm],
            device_id=(to * 4 + p, m),
            device_id_type=MESH,
        )

    def once(key):
        fresh = key not in kept
        kept[key] = True
        return fresh

    def product(layer, b):
        hr, hc = quarter(layer, 3)
        h = b % 2
        if b >= 2 and once(("y", layer)):
            for who in range(3):
                y_pass_copy(layer, who, 1 - m).wait_recv()
        if once(("dz", layer, h)):
            dz_piece(layer, 1 - z_first(layer), h).wait_recv()
            dz_relay(layer, h).wait_recv()
        own_dz = dz_ref[layer, :, rows_of(hc * half + h * ct, ct)]

        def one(i, _):
            start = part(b) * half + i * ct
            acc = mm(yt[layer, rows_of(hr * cols + start, ct), :], own_dz)
            for who in range(3):
                acc = acc + mm(yr[layer, who, rows_of(start, ct), :], dzr[layer, who, h])
            wpart[layer, b, rows_of(i * ct, ct), :] = acc.astype(BF)
            return 0

        lax.fori_loop(0, half // ct, one, 0)

        def send(i, _):
            line_copy(layer, b, (zi + i) % line, zi).start()
            return 0

        lax.fori_loop(1, line, send, 0)

    def flip_bit(e, d):
        return e + d - 2 * d * ((e // d) % 2)

    def spot(layer, b, e):
        ex, ey = e % 2, (e // 2) % 2
        hr, hc = (ex, ey) if layer == 1 else (ey, ex)
        return wg_hbm.at[
            layer,
            rows_of(hr * cols + part(b) * half + (e // 4) * rc, rc),
            rows_of(hc * half + (b % 2) * ct, ct),
        ]

    def held(base, dims):
        got = [base]
        for d in dims:
            got = got + [flip_bit(e, d) for e in got]
        return got

    def far_copy(layer, b, to, frm):
        return pltpu.make_async_remote_copy(
            src_ref=fin.at[layer, b],
            dst_ref=spot(layer, b, frm),
            send_sem=az_sem.at[0, layer, b, to // 8],
            recv_sem=az_sem.at[1, layer, b, frm // 8],
            device_id=(to, m),
            device_id_type=MESH,
        )

    def hops(layer, b, i, step, arriving):
        own = isinstance(i, int)
        dims = ORDERS[layer][b][0 if own else 1]
        base = (c + 8 * i) % n
        other = flip_bit(c, dims[step])
        slot = 2**step - 1
        copies = []
        for j, e in enumerate(held(base, dims[:step])):
            if arriving:
                e = flip_bit(e, dims[step])
            src = fin.at[layer, b] if own and j == 0 and not arriving else spot(layer, b, e)
            copies.append(
                remote(src, spot(layer, b, e), ag_sem, (layer, b, base // 8, slot + j), (other, m))
            )
        return copies

    def keep(layer, b):
        return pltpu.make_async_copy(
            fin.at[layer, b], spot(layer, b, c), fin_sem.at[layer, b]
        )

    def combine(layer, b):
        def take(i, _):
            frm = (zi + i) % line
            copy = line_copy(layer, b, frm, frm)
            copy.wait_recv()
            copy.wait_send()
            return 0

        lax.fori_loop(1, line, take, 0)
        zr[layer, b, zi] = wpart[layer, b, rows_of(zi * rc, rc), :]
        fin[layer, b] = lax.fori_loop(
            1, line,
            lambda j, t: t + zr[layer, b, j].astype(F32),
            zr[layer, b, 0].astype(F32),
        ).astype(BF)
        keep(layer, b).start()

        def send(i, _):
            far_copy(layer, b, (c + 8 * i) % n, c).start()
            return 0

        lax.fori_loop(1, far, send, 0)
        gather_own(layer, b, 0)

    def gather_own(layer, b, step):
        if step > 0:
            for copy in hops(layer, b, 0, step - 1, True):
                copy.wait_recv()
        for copy in hops(layer, b, 0, step, False):
            copy.start()
        if step > 0:
            for copy in hops(layer, b, 0, step - 1, False):
                copy.wait_send()

    def gather_far(layer, b, step):
        def one(i, _):
            if step == 0:
                frm = (c + 8 * i) % n
                far_copy(layer, b, frm, frm).wait_recv()
            else:
                for copy in hops(layer, b, i, step - 1, True):
                    copy.wait_recv()
            for copy in hops(layer, b, i, step, False):
                copy.start()
            if step > 0:
                for copy in hops(layer, b, i, step - 1, False):
                    copy.wait_send()
            return 0

        lax.fori_loop(1, far, one, 0)

    def gather_finish(layer, b):
        keep(layer, b).wait()

        def ends(i):
            for copy in hops(layer, b, i, 2, True):
                copy.wait_recv()
            for copy in hops(layer, b, i, 2, False):
                copy.wait_send()

        def one(i, _):
            far_copy(layer, b, (c + 8 * i) % n, c).wait_send()
            ends(i)
            return 0

        ends(0)
        lax.fori_loop(1, far, one, 0)

    w_copies = [
        pltpu.make_async_copy(w_hbm.at[layer], w_ref.at[layer], w_sem.at[layer])
        for layer in range(2)
    ]
    og_copy = pltpu.make_async_copy(og_hbm, og_ref, og_sem)
    in_copies = [
        pltpu.make_async_copy(src, dst, in_sem.at[i])
        for i, (src, dst) in enumerate(
            (
                (rows_hbm, rows_ref), (f_hbm, f_ref), (ids_hbm, ids_ref), (ew_hbm, ew_ref),
                (sw_hbm, sw_ref), (valid_hbm, valid_ref), (bias_hbm, bias_ref),
                (gain_hbm, gain_ref), (shift_hbm, shift_ref),
            )
        )
    ]
    small_copies = [
        pltpu.make_async_copy(src, dst, out_sem.at[2 + i])
        for i, (src, dst) in enumerate(
            ((bias_out, bias_res), (gain_out, gain_res), (shift_out, shift_res))
        )
    ]
    out_copy = pltpu.make_async_copy(out_ref, out_hbm, out_sem.at[0])
    ig_copy = pltpu.make_async_copy(h1_ref, ig_hbm, out_sem.at[1])

    def begin():
        barrier = pltpu.get_barrier_semaphore()

        def greet(i, _):
            pl.semaphore_signal(
                barrier, inc=1, device_id=(lax.rem(c + i, n), m), device_id_type=MESH
            )
            return 0

        lax.fori_loop(1, n, greet, 0)
        pl.semaphore_signal(barrier, inc=1, device_id=peer, device_id_type=MESH)
        for copy in in_copies:
            copy.start()

        in_copies[0].wait()
        lane = lax.broadcasted_iota(jnp.int32, (cap, halo), 1)
        spread = jnp.zeros((cap, halo), F32)
        for d in range(n):
            mine = rows_ref[0, :, d : d + 1].astype(F32)
            spread = jnp.where((lane >= d * cap) & (lane < (d + 1) * cap), mine, spread)
        place_q = lax.broadcasted_iota(jnp.int32, (cap, halo), 0)
        wanted = jnp.sum(jnp.where(lane % cap == place_q, spread, 0.0), axis=0, keepdims=True)
        rows_row[...] = wanted.astype(jnp.int32)

        def choose(i, _):
            r = rows_of(i * 128, 128)
            one_hot = jnp.where(
                rows_row[:, r] == lax.broadcasted_iota(jnp.int32, (nodes, 128), 0), 1.0, 0.0
            )
            sel_t[:, r] = one_hot.astype(BF)
            sel[r, :] = one_hot.T.astype(BF)
            return 0

        lax.fori_loop(0, halo // 128, choose, 0)
        in_copies[1].wait()
        pick(f_ref)
        pl.semaphore_wait(barrier, n)
        halo_start()
        w_copies[0].start()
        og_copy.start()
        w_copies[1].start()
        for copy in in_copies[2:]:
            copy.wait()
        mask_ref[...] = jnp.broadcast_to(valid_ref[...].astype(F32), (128, nodes)).T
        rb = 16
        place = lax.broadcasted_iota(jnp.int32, (rb, nodes), 0)
        node = lax.broadcasted_iota(jnp.int32, (rb, nodes), 1)

        def build(i, _):
            def rows(j, _):
                slots = place + (i * 128 + j * rb)
                a = jnp.where(node == slots, 2.0 * sw_ref[...], 0.0)
                for k in range(fan):
                    a = a + jnp.where(ids_ref[k : k + 1, :] == slots, ew_ref[k : k + 1, :], 0.0)
                a_block[rows_of(j * rb, rb), :] = a
                return 0

            lax.fori_loop(0, 128 // rb, rows, 0)
            r = rows_of(i * 128, 128)
            a = a_block[...]
            high = a.astype(BF)
            adj_t[r, :] = high
            if exact:
                adj_tlo[r, :] = (a - high.astype(F32)).astype(BF)
            a = a.T
            high = a.astype(BF)
            adj[:, r] = high
            if exact:
                adj_lo[:, r] = (a - high.astype(F32)).astype(BF)
            return 0

        lax.fori_loop(0, lookup // 128, build, 0)

    def ahead(what, x):
        got = mm(adj[:, what], x)
        return got + mm(adj_lo[:, what], x) if exact else got

    def back(what, x):
        got = mm(adj_t[what, :], x)
        return got + mm(adj_tlo[what, :], x) if exact else got

    inner, outer = slice(0, nodes), slice(nodes, lookup)

    def agg_local(layer):
        src = f_ref if layer == 0 else h1_ref
        for h in range(2):
            cs = slice(h * half, (h + 1) * half)
            zacc[:, cs] = ahead(inner, src[:, cs])

    def mp_copy(k, src, dst):
        return remote(src, dst, mp_sem, (k,), peer)

    def y_exchange(layer, h):
        ref = yf.at[layer, m, :, slice(h * half, (h + 1) * half)]
        return mp_copy(layer * 2 + h, ref, ref)

    def agg_halo(layer):
        parts = halo_finish()
        for h in range(2):
            cs = slice(h * half, (h + 1) * half)
            yf[layer, m, :, cs] = (zacc[:, cs] + ahead(outer, parts[h])).astype(BF)
            y_exchange(layer, h).start()

    def z_own(layer):
        w_copies[layer].wait()

        zacc[...] = mm(yf[layer, m], w_ref[layer, rows_of(m * cols, cols), :])
        for h in range(2):
            y_exchange(layer, h).wait_recv()

    def z_other(layer):
        if layer == 1:
            og_copy.wait()
        own_count = jnp.sum(mask_ref[...], axis=0, keepdims=True)
        own_count = jnp.concatenate([own_count] * (ct // 128), axis=1)
        own_inv = 1.0 / jnp.maximum(own_count, 1.0)

        zacc[...] += mm(yf[layer, 1 - m], w_ref[layer, rows_of((1 - m) * cols, cols), :])

        def second(j, _):
            z = zacc[:, col(j)] + bias_ref[layer : layer + 1, col(j)]
            sig = jax.nn.sigmoid(z)
            s = z * sig
            s_ref[layer, :, col(j)] = s
            d_ref[layer, :, col(j)] = (sig * (1.0 + z * (1.0 - sig))).astype(d_ref.dtype)
            valid = mask(ct)
            tot = jnp.sum(s * valid, axis=0, keepdims=True)
            cen = s - tot * own_inv
            st_row[0:1, col(j)] = tot
            st_row[1:2, col(j)] = jnp.sum(cen * cen * valid, axis=0, keepdims=True)
            if layer == 0:
                st_row[2:3, col(j)] = own_count
            else:
                pg = og_ref[:, col(j)].astype(F32) * valid
                st_row[2:3, col(j)] = jnp.sum(pg, axis=0, keepdims=True)
                st_row[3:4, col(j)] = jnp.sum(pg * cen, axis=0, keepdims=True)
            return 0

        lax.fori_loop(0, tiles, second, 0)
        buf = stat0 if layer == 0 else stat1
        for k in range(3 if layer == 0 else 4):
            fold(buf, k, k)

    def stats_out(layer):
        stat_start(layer, stat0 if layer == 0 else stat1)
        for h in range(2):
            y_exchange(layer, h).wait_send()
        y_flip(layer)

    def normalize(layer):
        buf = stat0 if layer == 0 else stat1
        stat_finish(layer, buf)
        count = jnp.maximum(total(stat0, 2), 1.0)
        mu = total(buf, 0) / count

        def spread(s, t):
            nc = stat0[s, 2]
            off = buf[s, 0] / jnp.maximum(nc, 1.0) - mu
            return t + buf[s, 1] + nc * off * off

        var = lax.fori_loop(0, n, spread, jnp.zeros_like(mu)) / count
        inv = lax.rsqrt(var + EPS)
        at = 8 if layer == 0 else 4
        unfold(mu, at)
        unfold(inv, at + 1)
        mu_row, inv_row = st_row[at : at + 1, :], st_row[at + 1 : at + 2, :]
        gain_row = gain_ref[layer : layer + 1, :]
        shift_row = shift_ref[layer : layer + 1, :]
        dst = h1_ref if layer == 0 else out_ref
        for j in range(tiles):
            cs = slice(j * ct, (j + 1) * ct)
            x = (s_ref[layer, :, cs] - mu_row[:, cs]) * inv_row[:, cs]
            dst[:, cs] = (mask(ct) * (gain_row[:, cs] * x + shift_row[:, cs])).astype(BF)
        if layer == 0:
            pick(h1_ref)
            return
        out_copy.start()

        def gains(s, t):
            off = stat1[s, 0] / jnp.maximum(stat0[s, 2], 1.0) - mu
            return t + stat1[s, 3] + off * stat1[s, 2]

        unfold(total(stat1, 2), 6)
        unfold(inv * lax.fori_loop(0, n, gains, jnp.zeros_like(mu)), 7)
        unfold(1.0 / count, 10)
        norm_sums(1)
        pre_grad(1)
        fold(stat2, 2, 11)

    def norm_sums(layer):
        gain_out[layer : layer + 1, :] = st_row[7:8, :]
        shift_out[layer : layer + 1, :] = st_row[6:7, :]

    def pre_grad(layer):
        at = 8 if layer == 0 else 4
        grad_src = og_ref if layer == 1 else g_ref

        def pre(j, _):
            gain = gain_ref[layer : layer + 1, col(j)]
            inv_row = st_row[at + 1 : at + 2, col(j)]
            ic = st_row[10:11, col(j)]
            x = (s_ref[layer, :, col(j)] - st_row[at : at + 1, col(j)]) * inv_row
            valid = mask(ct)
            pg = grad_src[:, col(j)].astype(F32) * valid
            ds = (
                valid
                * (inv_row * gain)
                * (pg - st_row[6:7, col(j)] * ic - x * (st_row[7:8, col(j)] * ic))
            )
            dz = (ds * d_ref[layer, :, col(j)].astype(F32)).astype(BF)
            dz_ref[layer, :, col(j)] = dz
            st_row[11:12, col(j)] = jnp.sum(dz.astype(F32), axis=0, keepdims=True)
            return 0

        lax.fori_loop(0, tiles, pre, 0)

    def dy_copy(layer):
        return mp_copy(4 + layer, dy_send, dy_recv.at[layer])

    def dy_other(layer):
        theirs = w_ref[layer, rows_of((1 - m) * cols, cols), :]
        dy_send[...] = mm_t(dz_ref[layer], theirs).astype(BF)
        dy_copy(layer).start()

    def dy_mine(layer):
        dy_own[...] = mm_t(dz_ref[layer], w_ref[layer, rows_of(m * cols, cols), :])
        dy_copy(layer).wait_recv()
        for j in range(tiles):
            cs = slice(j * ct, (j + 1) * ct)
            dyb[:, cs] = (dy_own[:, cs] + dy_recv[layer, :, cs].astype(F32)).astype(BF)
        pack_halo(back(outer, dyb[:, :half]), back(outer, dyb[:, half:]))
        halo_start()

    def back_local(layer):
        for h in range(2):
            cs = slice(h * half, (h + 1) * half)
            g_ref[:, cs] = back(inner, dyb[:, cs])
        dy_copy(layer).wait_send()

    def back_halo(layer):
        parts = halo_finish()
        for h in range(2):
            cs = slice(h * half, (h + 1) * half)
            got = g_ref[:, cs] + mm(sel_t[...], parts[h])
            if layer == 1:
                g_ref[:, cs] = got
                pg = got * mask(half)
                x = (s_ref[0, :, cs] - st_row[8:9, cs]) * st_row[9:10, cs]
                st_row[0:1, cs] = jnp.sum(pg, axis=0, keepdims=True)
                st_row[1:2, cs] = jnp.sum(pg * x, axis=0, keepdims=True)
            else:
                h1_ref[:, cs] = got.astype(BF)
        if layer == 1:
            fold(stat2, 0, 0)
            fold(stat2, 1, 1)
            stat_start(2, stat2)
        else:
            ig_copy.start()

    def back_norm():
        stat_finish(2, stat2)
        unfold(total(stat2, 0), 6)
        unfold(total(stat2, 1), 7)
        unfold(total(stat2, 2), 12)
        norm_sums(0)
        bias_out[1:2, :] = st_row[12:13, :]
        pre_grad(0)
        fold(stat3, 0, 11)
        stat_start(3, stat3)

    table = {
        "A0": lambda: (begin(), agg_local(0), agg_halo(0), z_own(0), z_other(0)),
        "A": lambda: stats_out(0),
        "B0": lambda: normalize(0),
        "B": halo_start,
        "B1": lambda: (agg_local(1), agg_halo(1)),
        "B2": lambda: z_own(1),
        "C": lambda: (z_other(1), stats_out(1)),
        "C2": lambda: normalize(1),
        "C3": lambda: dy_other(1),
        "D": lambda: dy_mine(1),
        "E": lambda: (back_local(1), back_halo(1)),
        "E2": back_norm,
        "E3": lambda: dy_other(0),
        "F": lambda: dy_mine(0),
        "G": lambda: back_local(0),
        "IG": lambda: back_halo(0),
        "ys": lambda l, who, k: y_piece(l, who, k).start(),
        "yf": y_forward,
        "yp": y_pass,
        "ds": lambda l, who, h: dz_piece(l, who, h).start(),
        "df": dz_forward,
        "pr": product,
        "cb": combine,
        "go": gather_own,
        "gf": gather_far,
    }
    for name, *args in SCHEDULE:
        table[name](*args)

    stat_finish(3, stat3)
    unfold(total(stat3, 0), 12)
    bias_out[0:1, :] = st_row[12:13, :]
    for copy in small_copies:
        copy.start()
    out_copy.wait()
    ig_copy.wait()
    for layer in (1, 0):
        y_sent(layer)
        dz_sent(layer)
        for b in range(4):
            gather_finish(layer, b)
    for copy in small_copies:
        copy.wait()


def hand_over(
    rows, slots,
    wg_hbm, out_in, ig_in, bias_in, gain_in, shift_in,
    wg_out, out_out, ig_out, bias_out, gain_out, shift_out,
    wide, through, in_sem, wide_sem, pass_sem, *narrow,
):
    blocks = in_sem.shape[0]
    per_layer = wg_hbm.shape[1] // rows

    def block(ref, i):
        return ref.at[i // per_layer, pl.ds((i % per_layer) * rows, rows), :]

    resident = not narrow

    def read(i):
        return pltpu.make_async_copy(block(wg_hbm, i), narrow[0].at[i], in_sem.at[i])

    def write(i):
        return pltpu.make_async_copy(wide.at[i % slots], block(wg_out, i), wide_sem.at[i])

    takes = [
        pltpu.make_async_copy(ref, through.at[i], pass_sem.at[0, i])
        for i, ref in enumerate((out_in, ig_in))
    ]
    gives = [
        pltpu.make_async_copy(through.at[i], ref, pass_sem.at[1, i])
        for i, ref in enumerate((out_out, ig_out))
    ]
    for i in range(blocks):
        if not resident:
            read(i).start()
        if i == 1:
            for copy in takes:
                copy.start()
    for i in range(blocks):
        if not resident:
            read(i).wait()
        if i >= slots:
            write(i - slots).wait()
        wide[i % slots] = (block(wg_hbm, i) if resident else narrow[0].at[i])[...].astype(F32)
        write(i).start()
        if i == 2:
            for take, give in zip(takes, gives):
                take.wait()
                give.start()
    bias_out[...] = bias_in[...]
    gain_out[...] = gain_in[...]
    shift_out[...] = shift_in[...]
    for i in range(blocks - slots, blocks):
        write(i).wait()
    for give in gives:
        give.wait()


def per_device(
    features, neighbour_ids, edge_weight, self_weight, send_rows, valid_mask,
    weights, biases, norm_gain, norm_shift, output_grad,
):
    nodes, cols = features.shape
    fan = neighbour_ids.shape[1]
    n, cap = send_rows.shape[1], send_rows.shape[2]
    halo = n * cap
    lookup = nodes + halo
    line = n // 4
    half = cols // 2
    vm = pl.BlockSpec(memory_space=pltpu.VMEM)
    anyspace = pl.BlockSpec(memory_space=pl.ANY)
    dma = pltpu.SemaphoreType.DMA
    small = jax.ShapeDtypeStruct((2, cols), F32)
    wide_block = jax.ShapeDtypeStruct((nodes, cols), BF)
    resident = n <= 16
    place = pltpu.VMEM if resident else jax.ShapeDtypeStruct
    out, ig, wg, bias, gain, shift = pl.pallas_call(
        functools.partial(chain, n, cap, fan, resident),
        out_shape=(
            place((nodes, cols), BF), place((nodes, cols), BF), place((2, 2 * cols, cols), BF),
            *[place((2, cols), F32) for _ in range(3)],
        ),
        in_specs=[anyspace] * 11,
        out_specs=(anyspace,) * 6,
        scratch_shapes=[
            pltpu.VMEM((nodes, cols), BF),
            pltpu.VMEM((1, cap, n), jnp.int32),
            pltpu.VMEM((fan, nodes), jnp.int32),
            pltpu.VMEM((fan, nodes), F32),
            pltpu.VMEM((1, nodes), F32),
            pltpu.VMEM((1, nodes), jnp.int32),
            *[pltpu.VMEM((2, cols), F32) for _ in range(6)],
            pltpu.VMEM((1, halo), jnp.int32),
            dma((9,)),
            pltpu.VMEM((2, 2 * cols, cols), BF),
            pltpu.VMEM((nodes, cols), BF),
            pltpu.VMEM((nodes, lookup), BF),
            pltpu.VMEM((nodes if resident else 16, lookup), BF),
            pltpu.VMEM((lookup, nodes), BF),
            pltpu.VMEM((lookup if resident else 16, nodes), BF),
            pltpu.VMEM((128, nodes), F32),
            pltpu.VMEM((halo, nodes), BF),
            pltpu.VMEM((nodes, halo), BF),
            pltpu.VMEM((nodes, 128), F32),
            pltpu.VMEM((nodes, cols), BF),
            pltpu.VMEM((2, 2, nodes, cols), BF),
            pltpu.VMEM((2, nodes, cols), F32),
            pltpu.VMEM((2, nodes, cols), F32 if resident else BF),
            pltpu.VMEM((nodes, cols), F32),
            pltpu.VMEM((2, nodes, cols), BF),
            pltpu.VMEM((2 * halo, half), BF),
            pltpu.VMEM((2 * halo, half), BF),
            pltpu.VMEM((16, cols), F32),
            pltpu.VMEM((n, 3, 8, cols // 8), F32),
            pltpu.VMEM((n, 4, 8, cols // 8), F32),
            pltpu.VMEM((n, 3, 8, cols // 8), F32),
            pltpu.VMEM((n, 1, 8, cols // 8), F32),
            pltpu.VMEM((2, 2 * cols, nodes), BF),
            pltpu.VMEM((2, 3, cols, nodes), BF),
            pltpu.VMEM((2, 3, 2, nodes, cols // 4), BF),
            pltpu.VMEM((2, 4, half, cols // 4), BF),
            pltpu.VMEM((2, 4, line, half // line, cols // 4), BF),
            pltpu.VMEM((2, 4, half // line, cols // 4), BF),
            dma((2,)), dma, dma((5,)), dma((2, 6)), dma((2,)), dma((2, 2)),
            dma((2, 2, 3, 4)), dma((2, 2, 3)), dma((2, 2, 3, 2)),
            dma((2, 2, 4, line)), dma((2, 2, 4, n // 8)), dma((2, 2, 4, n // 8, 7)), dma((2, 4)),
        ],
        compiler_params=pltpu.CompilerParams(
            collective_id=0,
            has_side_effects=True,
            vmem_limit_bytes=(53 if resident else 62) * 2**20,
        ),
    )(
        features, jnp.swapaxes(send_rows, 1, 2), neighbour_ids.T, edge_weight.T,
        self_weight.reshape(1, nodes), valid_mask.reshape(1, nodes), biases, norm_gain, norm_shift,
        output_grad, weights,
    )
    if resident:
        out, ig, wg, bias, gain, shift = (
            pltpu.with_memory_space_constraint(v, pltpu.VMEM)
            for v in (out, ig, wg, bias, gain, shift)
        )
    rows, slots = 512, 4
    blocks = 2 * 2 * cols // rows
    wg, out, ig, bias, gain, shift = pl.pallas_call(
        functools.partial(hand_over, rows, slots),
        out_shape=(
            jax.ShapeDtypeStruct((2, 2 * cols, cols), F32), wide_block, wide_block,
            small, small, small,
        ),
        in_specs=[vm if resident else anyspace] + [anyspace] * 2 + [vm] * 3,
        out_specs=(anyspace, anyspace, anyspace, vm, vm, vm),
        scratch_shapes=[
            pltpu.VMEM((slots, rows, cols), F32),
            pltpu.VMEM((2, nodes, cols), BF),
            dma((blocks,)), dma((blocks,)), dma((2, 2)),
            *([] if resident else [pltpu.VMEM((blocks, rows, cols), BF)]),
        ],
        compiler_params=pltpu.CompilerParams(vmem_limit_bytes=(40 if resident else 62) * 2**20),
    )(wg, out, ig, bias, gain, shift)
    return out, ig, wg, bias, gain, shift


def solution(mesh):
    return jax.shard_map(
        per_device,
        mesh=mesh,
        in_specs=(
            P("cluster", "mp"),
            P("cluster", None),
            P("cluster", None),
            P("cluster"),
            P("cluster", None, None),
            P("cluster"),
            P(None, None, "mp"),
            P(None, "mp"),
            P(None, "mp"),
            P(None, "mp"),
            P("cluster", "mp"),
        ),
        out_specs=(
            P("cluster", "mp"),
            P("cluster", "mp"),
            P(None, None, "mp"),
            P(None, "mp"),
            P(None, "mp"),
            P(None, "mp"),
        ),
        check_vma=False,
    )
```

```python
import functools

import jax
import jax.numpy as jnp
from jax import lax
from jax.experimental import pallas as pl
from jax.experimental.pallas import tpu as pltpu
from jax.sharding import PartitionSpec as P

EPS = 1e-05
MESH = pl.DeviceIdType.MESH
BF = jnp.bfloat16
F32 = jnp.float32

SCHEDULE = (
    ("A0",),
    ("A",), ("ys", 0, 1, 2),
    ("B0",),
    ("B",), ("ys", 0, 1, 3), ("ys", 0, 1, 0), ("ys", 0, 0, 2), ("ys", 0, 0, 0),
    ("B1",), ("ys", 0, 0, 3), ("ys", 0, 0, 1), ("ys", 0, 1, 1),
    ("B2",),
    ("C",), ("ys", 1, 1, 0), ("ys", 1, 0, 2), ("ys", 1, 0, 1), ("ys", 1, 1, 3), ("ys", 1, 1, 2), ("ys", 1, 0, 0),
    ("C2",), ("ds", 1, 1, 1), ("ds", 1, 0, 1),
    ("C3",),
    ("D",), ("ys", 1, 1, 1), ("yf", 1, 2), ("yf", 1, 1), ("df", 1, 1), ("ys", 1, 0, 3), ("yp", 0, 0),
    ("E",), ("yf", 1, 0), ("yf", 1, 3), ("ds", 1, 0, 0), ("yp", 1, 1),
    ("E2",), ("yf", 0, 1), ("ds", 0, 0, 0), ("ds", 1, 1, 0), ("yp", 1, 0), ("yp", 1, 2), ("pr", 1, 1), ("pr", 1, 3),
    ("ds", 0, 1, 0), ("df", 1, 0), ("ds", 0, 0, 1), ("ds", 0, 1, 1), ("cb", 1, 1), ("yf", 0, 3), ("cb", 1, 3),
    ("go", 1, 1, 1), ("pr", 1, 0), ("df", 0, 0), ("yf", 0, 2), ("df", 0, 1), ("go", 1, 3, 1), ("yf", 0, 0),
    ("gf", 1, 3, 0), ("pr", 1, 2), ("go", 1, 1, 2), ("gf", 1, 3, 1), ("cb", 1, 0),
    ("E3",), ("gf", 1, 1, 0), ("yp", 0, 1), ("cb", 1, 2), ("yp", 0, 2), ("pr", 0, 1), ("gf", 1, 0, 0),
    ("go", 1, 0, 1), ("pr", 0, 0), ("go", 1, 0, 2), ("gf", 1, 1, 1), ("cb", 0, 1), ("gf", 1, 0, 1), ("gf", 1, 2, 0),
    ("go", 1, 2, 1), ("go", 1, 3, 2), ("pr", 0, 2), ("gf", 1, 1, 2), ("gf", 1, 0, 2), ("pr", 0, 3), ("gf", 0, 1, 0),
    ("gf", 1, 3, 2), ("gf", 1, 2, 1), ("go", 0, 1, 1), ("gf", 0, 1, 1), ("go", 1, 2, 2), ("cb", 0, 2), ("cb", 0, 3),
    ("cb", 0, 0),
    ("F",), ("gf", 0, 2, 0), ("go", 0, 2, 1), ("go", 0, 0, 1), ("go", 0, 1, 2), ("gf", 0, 1, 2), ("gf", 0, 0, 0),
    ("gf", 0, 3, 0), ("gf", 0, 2, 1), ("gf", 1, 2, 2),
    ("G",), ("go", 0, 0, 2), ("gf", 0, 0, 1),
    ("IG",), ("gf", 0, 3, 1), ("go", 0, 3, 1), ("gf", 0, 2, 2), ("gf", 0, 0, 2), ("go", 0, 3, 2), ("go", 0, 2, 2),
    ("gf", 0, 3, 2),
)
ORDERS = (
    (
        ((1, 2, 4), (4, 1, 2)),
        ((4, 2, 1), (1, 4, 2)),
        ((2, 1, 4), (4, 2, 1)),
        ((4, 2, 1), (4, 1, 2)),
    ),
    (
        ((4, 2, 1), (4, 1, 2)),
        ((4, 2, 1), (4, 2, 1)),
        ((1, 4, 2), (2, 1, 4)),
        ((4, 1, 2), (4, 2, 1)),
    ),
)


def mm(a, b):
    return jnp.dot(a, b, preferred_element_type=F32)


def mm_t(a, b):
    return lax.dot_general(a, b, (((1,), (1,)), ((), ())), preferred_element_type=F32)


def chain(
    n, cap, fan, exact,
    f_hbm, rows_hbm, ids_hbm, ew_hbm, sw_hbm, valid_hbm, bias_hbm, gain_hbm, shift_hbm, og_hbm, w_hbm,
    out_hbm, ig_hbm, wg_hbm, bias_res, gain_res, shift_res,
    f_ref, rows_ref, ids_ref, ew_ref, sw_ref, valid_ref, bias_ref, gain_ref, shift_ref,
    bias_out, gain_out, shift_out, rows_row, in_sem,
    w_ref, og_ref, adj, adj_lo, adj_t, adj_tlo, a_block, sel, sel_t, mask_ref, h1_ref, yf, s_ref, d_ref, zacc,
    dy_recv, hsend, hrecv, st_row, stat0, stat1, stat2, stat3,
    yt, yr, dzr, wpart, zr, fin,
    w_sem, og_sem, out_sem, mp_sem, h_sem, x_sem,
    y_sem, yp_sem, dz_sem, zr_sem, az_sem, ag_sem, fin_sem,
):
    nodes, cols = f_hbm.shape
    ct = 256
    tiles = cols // ct
    half = cols // 2
    c = lax.axis_index("cluster")
    m = lax.axis_index("mp")
    peer = (c, 1 - m)
    halo = n * cap
    lookup = nodes + halo
    line, far = n // 4, n // 8
    zi, p = c // 4, c % 4
    px, py = p % 2, p // 2
    near = (c + 1 - 2 * px, c + 2 - 4 * py)
    rc = half // line
    dy_own, dyb, g_ref = zacc, og_ref, s_ref.at[1]
    out_ref, dy_send, dz_ref = yf.at[0, 0], yf.at[0, 1], yf.at[1]
    pieces = 4
    prow = half // pieces
    lanes = cols // 8
    kept = {}

    def rows_of(start, size):
        return pl.ds(pl.multiple_of(start, size), size)

    def col(j):
        return rows_of(j * ct, ct)

    def remote(src, dst, sems, idx, to):
        return pltpu.make_async_remote_copy(
            src_ref=src,
            dst_ref=dst,
            send_sem=sems.at[(0, *idx)],
            recv_sem=sems.at[(1, *idx)],
            device_id=to,
            device_id_type=MESH,
        )

    def mask(width):
        return jnp.concatenate([mask_ref[...]] * (width // 128), axis=1)

    def halo_part(d):
        return rows_of(d * 2 * cap, 2 * cap)

    def pack_halo(left, right):
        both = jnp.concatenate(
            [left.reshape(n, cap, half), right.reshape(n, cap, half)], axis=1
        )
        hsend[...] = both.reshape(n * 2 * cap, half).astype(BF)

    def wait_all(ref, size, sem):
        some = ref.at[pl.ds(0, size)]
        pltpu.make_async_copy(some, some, sem).wait()

    def halo_copy(to, frm):
        return pltpu.make_async_remote_copy(
            src_ref=hsend.at[halo_part(to)],
            dst_ref=hrecv.at[halo_part(frm)],
            send_sem=h_sem.at[0],
            recv_sem=h_sem.at[1],
            device_id=(to, m),
            device_id_type=MESH,
        )

    def halo_start():
        for i in range(1, n):
            halo_copy(lax.rem(c + i, n), c).start()
        hrecv[halo_part(c)] = hsend[halo_part(c)]

    def halo_finish():
        wait_all(hsend, (n - 1) * 2 * cap, h_sem.at[0])
        wait_all(hrecv, (n - 1) * 2 * cap, h_sem.at[1])
        got = hrecv[...].astype(F32).reshape(n, 2 * cap, half)
        left = got[:, :cap, :].reshape(halo, half).astype(BF)
        right = got[:, cap:, :].reshape(halo, half).astype(BF)
        return left, right

    def pick(src):
        pack_halo(mm(sel[...], src[:, :half]), mm(sel[...], src[:, half:]))

    def stat_copy(e, buf, to, frm):
        return pltpu.make_async_remote_copy(
            src_ref=buf.at[c],
            dst_ref=buf.at[frm],
            send_sem=x_sem.at[0, e % 2],
            recv_sem=x_sem.at[1, e % 2],
            device_id=(to, m),
            device_id_type=MESH,
        )

    def stat_start(e, buf):
        def send(i, _):
            stat_copy(e, buf, lax.rem(c + i, n), c).start()
            return 0

        lax.fori_loop(1, n, send, 0)

    def stat_finish(e, buf):
        for way in range(2):
            wait_all(buf, n - 1, x_sem.at[way, e % 2])

    def fold(buf, k, row):
        for g in range(8):
            buf[c, k, g : g + 1, :] = st_row[row : row + 1, g * lanes : (g + 1) * lanes]

    def unfold(tile, row):
        for g in range(8):
            st_row[row : row + 1, g * lanes : (g + 1) * lanes] = tile[g : g + 1, :]

    def total(buf, k):
        return lax.fori_loop(1, n, lambda s, t: t + buf[s, k], buf[0, k])

    def quarter(layer, who):
        qx = 1 - px if who in (0, 2) else px
        qy = 1 - py if who in (1, 2) else py
        return (qx, qy) if layer == 1 else (qy, qx)

    def y_flip(layer):
        def flip(i, _):
            r = rows_of(i * 128, 128)
            for h in range(2):
                yt[layer, rows_of(h * cols + i * 128, 128), :] = (
                    yf[layer, h, :, r].astype(F32).T.astype(BF)
                )
            return 0

        lax.fori_loop(0, cols // 128, flip, 0)

    def y_piece(layer, who, k):
        hr, _ = quarter(layer, who)
        return remote(
            yt.at[layer, rows_of(hr * cols + m * half + k * prow, prow), :],
            yr.at[layer, who, rows_of(m * half + k * prow, prow), :],
            y_sem, (layer, who, k), (near[who], m),
        )

    def y_first(layer):
        return 1 - layer

    def z_first(layer):
        return layer

    def y_relay(layer, k):
        first = y_first(layer)
        r = rows_of(m * half + k * prow, prow)
        return remote(
            yr.at[layer, first, r, :], yr.at[layer, 2, r, :], y_sem, (layer, 2, k),
            (near[1 - first], m),
        )

    def y_forward(layer, k):
        y_piece(layer, y_first(layer), k).wait_recv()
        y_relay(layer, k).start()

    def y_pass_copy(layer, who, part):
        r = rows_of(part * half, half)
        return remote(
            yr.at[layer, who, r, :], yr.at[layer, who, r, :], yp_sem, (layer, who), peer
        )

    def y_pass(layer, who):
        if who != y_first(layer):
            for k in range(pieces):
                copy = y_relay(layer, k) if who == 2 else y_piece(layer, who, k)
                copy.wait_recv()
        y_pass_copy(layer, who, m).start()

    def y_sent(layer):
        for k in range(pieces):
            y_piece(layer, 0, k).wait_send()
            y_piece(layer, 1, k).wait_send()
            y_relay(layer, k).wait_send()
        for who in range(3):
            y_pass_copy(layer, who, m).wait_send()

    def dz_piece(layer, who, h):
        _, hc = quarter(layer, who)
        return remote(
            dz_ref.at[layer, :, rows_of(hc * half + h * ct, ct)],
            dzr.at[layer, who, h],
            dz_sem, (layer, who, h), (near[who], m),
        )

    def dz_relay(layer, h):
        first = z_first(layer)
        return remote(
            dzr.at[layer, first, h], dzr.at[layer, 2, h], dz_sem, (layer, 2, h),
            (near[1 - first], m),
        )

    def dz_forward(layer, h):
        dz_piece(layer, z_first(layer), h).wait_recv()
        dz_relay(layer, h).start()

    def dz_sent(layer):
        for h in range(2):
            dz_piece(layer, 0, h).wait_send()
            dz_piece(layer, 1, h).wait_send()
            dz_relay(layer, h).wait_send()

    def part(b):
        return m if b < 2 else 1 - m

    def line_copy(layer, b, to, frm):
        return pltpu.make_async_remote_copy(
            src_ref=wpart.at[layer, b, rows_of(to * rc, rc), :],
            dst_ref=zr.at[layer, b, frm],
            send_sem=zr_sem.at[0, layer, b, to],
            recv_sem=zr_sem.at[1, layer, b, frm],
            device_id=(to * 4 + p, m),
            device_id_type=MESH,
        )

    def once(key):
        fresh = key not in kept
        kept[key] = True
        return fresh

    def product(layer, b):
        hr, hc = quarter(layer, 3)
        h = b % 2
        if b >= 2 and once(("y", layer)):
            for who in range(3):
                y_pass_copy(layer, who, 1 - m).wait_recv()
        if once(("dz", layer, h)):
            dz_piece(layer, 1 - z_first(layer), h).wait_recv()
            dz_relay(layer, h).wait_recv()
        own_dz = dz_ref[layer, :, rows_of(hc * half + h * ct, ct)]

        def one(i, _):
            start = part(b) * half + i * ct
            acc = mm(yt[layer, rows_of(hr * cols + start, ct), :], own_dz)
            for who in range(3):
                acc = acc + mm(yr[layer, who, rows_of(start, ct), :], dzr[layer, who, h])
            wpart[layer, b, rows_of(i * ct, ct), :] = acc.astype(BF)
            return 0

        lax.fori_loop(0, half // ct, one, 0)

        def send(i, _):
            line_copy(layer, b, (zi + i) % line, zi).start()
            return 0

        lax.fori_loop(1, line, send, 0)

    def flip_bit(e, d):
        return e + d - 2 * d * ((e // d) % 2)

    def spot(layer, b, e):
        ex, ey = e % 2, (e // 2) % 2
        hr, hc = (ex, ey) if layer == 1 else (ey, ex)
        return wg_hbm.at[
            layer,
            rows_of(hr * cols + part(b) * half + (e // 4) * rc, rc),
            rows_of(hc * half + (b % 2) * ct, ct),
        ]

    def held(base, dims):
        got = [base]
        for d in dims:
            got = got + [flip_bit(e, d) for e in got]
        return got

    def far_copy(layer, b, to, frm):
        return pltpu.make_async_remote_copy(
            src_ref=fin.at[layer, b],
            dst_ref=spot(layer, b, frm),
            send_sem=az_sem.at[0, layer, b, to // 8],
            recv_sem=az_sem.at[1, layer, b, frm // 8],
            device_id=(to, m),
            device_id_type=MESH,
        )

    def hops(layer, b, i, step, arriving):
        own = isinstance(i, int)
        dims = ORDERS[layer][b][0 if own else 1]
        base = (c + 8 * i) % n
        other = flip_bit(c, dims[step])
        slot = 2**step - 1
        copies = []
        for j, e in enumerate(held(base, dims[:step])):
            if arriving:
                e = flip_bit(e, dims[step])
            src = fin.at[layer, b] if own and j == 0 and not arriving else spot(layer, b, e)
            copies.append(
                remote(src, spot(layer, b, e), ag_sem, (layer, b, base // 8, slot + j), (other, m))
            )
        return copies

    def keep(layer, b):
        return pltpu.make_async_copy(
            fin.at[layer, b], spot(layer, b, c), fin_sem.at[layer, b]
        )

    def combine(layer, b):
        def take(i, _):
            frm = (zi + i) % line
            copy = line_copy(layer, b, frm, frm)
            copy.wait_recv()
            copy.wait_send()
            return 0

        lax.fori_loop(1, line, take, 0)
        zr[layer, b, zi] = wpart[layer, b, rows_of(zi * rc, rc), :]
        fin[layer, b] = lax.fori_loop(
            1, line,
            lambda j, t: t + zr[layer, b, j].astype(F32),
            zr[layer, b, 0].astype(F32),
        ).astype(BF)
        keep(layer, b).start()

        def send(i, _):
            far_copy(layer, b, (c + 8 * i) % n, c).start()
            return 0

        lax.fori_loop(1, far, send, 0)
        gather_own(layer, b, 0)

    def gather_own(layer, b, step):
        if step > 0:
            for copy in hops(layer, b, 0, step - 1, True):
                copy.wait_recv()
        for copy in hops(layer, b, 0, step, False):
            copy.start()
        if step > 0:
            for copy in hops(layer, b, 0, step - 1, False):
                copy.wait_send()

    def gather_far(layer, b, step):
        def one(i, _):
            if step == 0:
                frm = (c + 8 * i) % n
                far_copy(layer, b, frm, frm).wait_recv()
            else:
                for copy in hops(layer, b, i, step - 1, True):
                    copy.wait_recv()
            for copy in hops(layer, b, i, step, False):
                copy.start()
            if step > 0:
                for copy in hops(layer, b, i, step - 1, False):
                    copy.wait_send()
            return 0

        lax.fori_loop(1, far, one, 0)

    def gather_finish(layer, b):
        keep(layer, b).wait()

        def ends(i):
            for copy in hops(layer, b, i, 2, True):
                copy.wait_recv()
            for copy in hops(layer, b, i, 2, False):
                copy.wait_send()

        def one(i, _):
            far_copy(layer, b, (c + 8 * i) % n, c).wait_send()
            ends(i)
            return 0

        ends(0)
        lax.fori_loop(1, far, one, 0)

    w_copies = [
        pltpu.make_async_copy(w_hbm.at[layer], w_ref.at[layer], w_sem.at[layer])
        for layer in range(2)
    ]
    og_copy = pltpu.make_async_copy(og_hbm, og_ref, og_sem)
    in_copies = [
        pltpu.make_async_copy(src, dst, in_sem.at[i])
        for i, (src, dst) in enumerate(
            (
                (rows_hbm, rows_ref), (f_hbm, f_ref), (ids_hbm, ids_ref), (ew_hbm, ew_ref),
                (sw_hbm, sw_ref), (valid_hbm, valid_ref), (bias_hbm, bias_ref),
                (gain_hbm, gain_ref), (shift_hbm, shift_ref),
            )
        )
    ]
    small_copies = [
        pltpu.make_async_copy(src, dst, out_sem.at[2 + i])
        for i, (src, dst) in enumerate(
            ((bias_out, bias_res), (gain_out, gain_res), (shift_out, shift_res))
        )
    ]
    out_copy = pltpu.make_async_copy(out_ref, out_hbm, out_sem.at[0])
    ig_copy = pltpu.make_async_copy(h1_ref, ig_hbm, out_sem.at[1])

    def begin():
        barrier = pltpu.get_barrier_semaphore()

        def greet(i, _):
            pl.semaphore_signal(
                barrier, inc=1, device_id=(lax.rem(c + i, n), m), device_id_type=MESH
            )
            return 0

        lax.fori_loop(1, n, greet, 0)
        pl.semaphore_signal(barrier, inc=1, device_id=peer, device_id_type=MESH)
        for copy in in_copies:
            copy.start()

        in_copies[0].wait()
        lane = lax.broadcasted_iota(jnp.int32, (cap, halo), 1)
        spread = jnp.zeros((cap, halo), F32)
        for d in range(n):
            mine = rows_ref[0, :, d : d + 1].astype(F32)
            spread = jnp.where((lane >= d * cap) & (lane < (d + 1) * cap), mine, spread)
        place_q = lax.broadcasted_iota(jnp.int32, (cap, halo), 0)
        wanted = jnp.sum(jnp.where(lane % cap == place_q, spread, 0.0), axis=0, keepdims=True)
        rows_row[...] = wanted.astype(jnp.int32)

        def choose(i, _):
            r = rows_of(i * 128, 128)
            one_hot = jnp.where(
                rows_row[:, r] == lax.broadcasted_iota(jnp.int32, (nodes, 128), 0), 1.0, 0.0
            )
            sel_t[:, r] = one_hot.astype(BF)
            sel[r, :] = one_hot.T.astype(BF)
            return 0

        lax.fori_loop(0, halo // 128, choose, 0)
        in_copies[1].wait()
        pick(f_ref)
        pl.semaphore_wait(barrier, n)
        halo_start()
        w_copies[0].start()
        og_copy.start()
        w_copies[1].start()
        for copy in in_copies[2:]:
            copy.wait()
        mask_ref[...] = jnp.broadcast_to(valid_ref[...].astype(F32), (128, nodes)).T
        rb = 16
        place = lax.broadcasted_iota(jnp.int32, (rb, nodes), 0)
        node = lax.broadcasted_iota(jnp.int32, (rb, nodes), 1)

        def build(i, _):
            def rows(j, _):
                slots = place + (i * 128 + j * rb)
                a = jnp.where(node == slots, 2.0 * sw_ref[...], 0.0)
                for k in range(fan):
                    a = a + jnp.where(ids_ref[k : k + 1, :] == slots, ew_ref[k : k + 1, :], 0.0)
                a_block[rows_of(j * rb, rb), :] = a
                return 0

            lax.fori_loop(0, 128 // rb, rows, 0)
            r = rows_of(i * 128, 128)
            a = a_block[...]
            high = a.astype(BF)
            adj_t[r, :] = high
            if exact:
                adj_tlo[r, :] = (a - high.astype(F32)).astype(BF)
            a = a.T
            high = a.astype(BF)
            adj[:, r] = high
            if exact:
                adj_lo[:, r] = (a - high.astype(F32)).astype(BF)
            return 0

        lax.fori_loop(0, lookup // 128, build, 0)

    def ahead(what, x):
        got = mm(adj[:, what], x)
        return got + mm(adj_lo[:, what], x) if exact else got

    def back(what, x):
        got = mm(adj_t[what, :], x)
        return got + mm(adj_tlo[what, :], x) if exact else got

    inner, outer = slice(0, nodes), slice(nodes, lookup)

    def agg_local(layer):
        src = f_ref if layer == 0 else h1_ref
        for h in range(2):
            cs = slice(h * half, (h + 1) * half)
            zacc[:, cs] = ahead(inner, src[:, cs])

    def mp_copy(k, src, dst):
        return remote(src, dst, mp_sem, (k,), peer)

    def y_exchange(layer, h):
        ref = yf.at[layer, m, :, slice(h * half, (h + 1) * half)]
        return mp_copy(layer * 2 + h, ref, ref)

    def agg_halo(layer):
        parts = halo_finish()
        for h in range(2):
            cs = slice(h * half, (h + 1) * half)
            yf[layer, m, :, cs] = (zacc[:, cs] + ahead(outer, parts[h])).astype(BF)
            y_exchange(layer, h).start()

    def z_own(layer):
        w_copies[layer].wait()

        zacc[...] = mm(yf[layer, m], w_ref[layer, rows_of(m * cols, cols), :])
        for h in range(2):
            y_exchange(layer, h).wait_recv()

    def z_other(layer):
        if layer == 1:
            og_copy.wait()
        own_count = jnp.sum(mask_ref[...], axis=0, keepdims=True)
        own_count = jnp.concatenate([own_count] * (ct // 128), axis=1)
        own_inv = 1.0 / jnp.maximum(own_count, 1.0)

        zacc[...] += mm(yf[layer, 1 - m], w_ref[layer, rows_of((1 - m) * cols, cols), :])

        def second(j, _):
            z = zacc[:, col(j)] + bias_ref[layer : layer + 1, col(j)]
            sig = jax.nn.sigmoid(z)
            s = z * sig
            s_ref[layer, :, col(j)] = s
            d_ref[layer, :, col(j)] = (sig * (1.0 + z * (1.0 - sig))).astype(d_ref.dtype)
            valid = mask(ct)
            tot = jnp.sum(s * valid, axis=0, keepdims=True)
            cen = s - tot * own_inv
            st_row[0:1, col(j)] = tot
            st_row[1:2, col(j)] = jnp.sum(cen * cen * valid, axis=0, keepdims=True)
            if layer == 0:
                st_row[2:3, col(j)] = own_count
            else:
                pg = og_ref[:, col(j)].astype(F32) * valid
                st_row[2:3, col(j)] = jnp.sum(pg, axis=0, keepdims=True)
                st_row[3:4, col(j)] = jnp.sum(pg * cen, axis=0, keepdims=True)
            return 0

        lax.fori_loop(0, tiles, second, 0)
        buf = stat0 if layer == 0 else stat1
        for k in range(3 if layer == 0 else 4):
            fold(buf, k, k)

    def stats_out(layer):
        stat_start(layer, stat0 if layer == 0 else stat1)
        for h in range(2):
            y_exchange(layer, h).wait_send()
        y_flip(layer)

    def normalize(layer):
        buf = stat0 if layer == 0 else stat1
        stat_finish(layer, buf)
        count = jnp.maximum(total(stat0, 2), 1.0)
        mu = total(buf, 0) / count

        def spread(s, t):
            nc = stat0[s, 2]
            off = buf[s, 0] / jnp.maximum(nc, 1.0) - mu
            return t + buf[s, 1] + nc * off * off

        var = lax.fori_loop(0, n, spread, jnp.zeros_like(mu)) / count
        inv = lax.rsqrt(var + EPS)
        at = 8 if layer == 0 else 4
        unfold(mu, at)
        unfold(inv, at + 1)
        mu_row, inv_row = st_row[at : at + 1, :], st_row[at + 1 : at + 2, :]
        gain_row = gain_ref[layer : layer + 1, :]
        shift_row = shift_ref[layer : layer + 1, :]
        dst = h1_ref if layer == 0 else out_ref
        for j in range(tiles):
            cs = slice(j * ct, (j + 1) * ct)
            x = (s_ref[layer, :, cs] - mu_row[:, cs]) * inv_row[:, cs]
            dst[:, cs] = (mask(ct) * (gain_row[:, cs] * x + shift_row[:, cs])).astype(BF)
        if layer == 0:
            pick(h1_ref)
            return
        out_copy.start()

        def gains(s, t):
            off = stat1[s, 0] / jnp.maximum(stat0[s, 2], 1.0) - mu
            return t + stat1[s, 3] + off * stat1[s, 2]

        unfold(total(stat1, 2), 6)
        unfold(inv * lax.fori_loop(0, n, gains, jnp.zeros_like(mu)), 7)
        unfold(1.0 / count, 10)
        norm_sums(1)
        pre_grad(1)
        fold(stat2, 2, 11)

    def norm_sums(layer):
        gain_out[layer : layer + 1, :] = st_row[7:8, :]
        shift_out[layer : layer + 1, :] = st_row[6:7, :]

    def pre_grad(layer):
        at = 8 if layer == 0 else 4
        grad_src = og_ref if layer == 1 else g_ref

        def pre(j, _):
            gain = gain_ref[layer : layer + 1, col(j)]
            inv_row = st_row[at + 1 : at + 2, col(j)]
            ic = st_row[10:11, col(j)]
            x = (s_ref[layer, :, col(j)] - st_row[at : at + 1, col(j)]) * inv_row
            valid = mask(ct)
            pg = grad_src[:, col(j)].astype(F32) * valid
            ds = (
                valid
                * (inv_row * gain)
                * (pg - st_row[6:7, col(j)] * ic - x * (st_row[7:8, col(j)] * ic))
            )
            dz = (ds * d_ref[layer, :, col(j)].astype(F32)).astype(BF)
            dz_ref[layer, :, col(j)] = dz
            st_row[11:12, col(j)] = jnp.sum(dz.astype(F32), axis=0, keepdims=True)
            return 0

        lax.fori_loop(0, tiles, pre, 0)

    def dy_copy(layer):
        return mp_copy(4 + layer, dy_send, dy_recv.at[layer])

    def dy_other(layer):
        theirs = w_ref[layer, rows_of((1 - m) * cols, cols), :]
        dy_send[...] = mm_t(dz_ref[layer], theirs).astype(BF)
        dy_copy(layer).start()

    def dy_mine(layer):
        dy_own[...] = mm_t(dz_ref[layer], w_ref[layer, rows_of(m * cols, cols), :])
        dy_copy(layer).wait_recv()
        for j in range(tiles):
            cs = slice(j * ct, (j + 1) * ct)
            dyb[:, cs] = (dy_own[:, cs] + dy_recv[layer, :, cs].astype(F32)).astype(BF)
        pack_halo(back(outer, dyb[:, :half]), back(outer, dyb[:, half:]))
        halo_start()

    def back_local(layer):
        for h in range(2):
            cs = slice(h * half, (h + 1) * half)
            g_ref[:, cs] = back(inner, dyb[:, cs])
        dy_copy(layer).wait_send()

    def back_halo(layer):
        parts = halo_finish()
        for h in range(2):
            cs = slice(h * half, (h + 1) * half)
            got = g_ref[:, cs] + mm(sel_t[...], parts[h])
            if layer == 1:
                g_ref[:, cs] = got
                pg = got * mask(half)
                x = (s_ref[0, :, cs] - st_row[8:9, cs]) * st_row[9:10, cs]
                st_row[0:1, cs] = jnp.sum(pg, axis=0, keepdims=True)
                st_row[1:2, cs] = jnp.sum(pg * x, axis=0, keepdims=True)
            else:
                h1_ref[:, cs] = got.astype(BF)
        if layer == 1:
            fold(stat2, 0, 0)
            fold(stat2, 1, 1)
            stat_start(2, stat2)
        else:
            ig_copy.start()

    def back_norm():
        stat_finish(2, stat2)
        unfold(total(stat2, 0), 6)
        unfold(total(stat2, 1), 7)
        unfold(total(stat2, 2), 12)
        norm_sums(0)
        bias_out[1:2, :] = st_row[12:13, :]
        pre_grad(0)
        fold(stat3, 0, 11)
        stat_start(3, stat3)

    table = {
        "A0": lambda: (begin(), agg_local(0), agg_halo(0), z_own(0), z_other(0)),
        "A": lambda: stats_out(0),
        "B0": lambda: normalize(0),
        "B": halo_start,
        "B1": lambda: (agg_local(1), agg_halo(1)),
        "B2": lambda: z_own(1),
        "C": lambda: (z_other(1), stats_out(1)),
        "C2": lambda: normalize(1),
        "C3": lambda: dy_other(1),
        "D": lambda: dy_mine(1),
        "E": lambda: (back_local(1), back_halo(1)),
        "E2": back_norm,
        "E3": lambda: dy_other(0),
        "F": lambda: dy_mine(0),
        "G": lambda: back_local(0),
        "IG": lambda: back_halo(0),
        "ys": lambda l, who, k: y_piece(l, who, k).start(),
        "yf": y_forward,
        "yp": y_pass,
        "ds": lambda l, who, h: dz_piece(l, who, h).start(),
        "df": dz_forward,
        "pr": product,
        "cb": combine,
        "go": gather_own,
        "gf": gather_far,
    }
    for name, *args in SCHEDULE:
        table[name](*args)

    stat_finish(3, stat3)
    unfold(total(stat3, 0), 12)
    bias_out[0:1, :] = st_row[12:13, :]
    for copy in small_copies:
        copy.start()
    out_copy.wait()
    ig_copy.wait()
    for layer in (1, 0):
        y_sent(layer)
        dz_sent(layer)
        for b in range(4):
            gather_finish(layer, b)
    for copy in small_copies:
        copy.wait()


def hand_over(
    rows, slots,
    wg_hbm, out_in, ig_in, bias_in, gain_in, shift_in,
    wg_out, out_out, ig_out, bias_out, gain_out, shift_out,
    wide, through, in_sem, wide_sem, pass_sem, *narrow,
):
    blocks = in_sem.shape[0]
    per_layer = wg_hbm.shape[1] // rows

    def block(ref, i):
        return ref.at[i // per_layer, pl.ds((i % per_layer) * rows, rows), :]

    resident = not narrow

    def read(i):
        return pltpu.make_async_copy(block(wg_hbm, i), narrow[0].at[i], in_sem.at[i])

    def write(i):
        return pltpu.make_async_copy(wide.at[i % slots], block(wg_out, i), wide_sem.at[i])

    takes = [
        pltpu.make_async_copy(ref, through.at[i], pass_sem.at[0, i])
        for i, ref in enumerate((out_in, ig_in))
    ]
    gives = [
        pltpu.make_async_copy(through.at[i], ref, pass_sem.at[1, i])
        for i, ref in enumerate((out_out, ig_out))
    ]
    for i in range(blocks):
        if not resident:
            read(i).start()
        if i == 1:
            for copy in takes:
                copy.start()
    for i in range(blocks):
        if not resident:
            read(i).wait()
        if i >= slots:
            write(i - slots).wait()
        wide[i % slots] = (block(wg_hbm, i) if resident else narrow[0].at[i])[...].astype(F32)
        write(i).start()
        if i == 2:
            for take, give in zip(takes, gives):
                take.wait()
                give.start()
    bias_out[...] = bias_in[...]
    gain_out[...] = gain_in[...]
    shift_out[...] = shift_in[...]
    for i in range(blocks - slots, blocks):
        write(i).wait()
    for give in gives:
        give.wait()


def per_device(
    features, neighbour_ids, edge_weight, self_weight, send_rows, valid_mask,
    weights, biases, norm_gain, norm_shift, output_grad,
):
    nodes, cols = features.shape
    fan = neighbour_ids.shape[1]
    n, cap = send_rows.shape[1], send_rows.shape[2]
    halo = n * cap
    lookup = nodes + halo
    line = n // 4
    half = cols // 2
    vm = pl.BlockSpec(memory_space=pltpu.VMEM)
    anyspace = pl.BlockSpec(memory_space=pl.ANY)
    dma = pltpu.SemaphoreType.DMA
    small = jax.ShapeDtypeStruct((2, cols), F32)
    wide_block = jax.ShapeDtypeStruct((nodes, cols), BF)
    resident = n <= 16
    place = pltpu.VMEM if resident else jax.ShapeDtypeStruct
    out, ig, wg, bias, gain, shift = pl.pallas_call(
        functools.partial(chain, n, cap, fan, resident),
        out_shape=(
            place((nodes, cols), BF), place((nodes, cols), BF), place((2, 2 * cols, cols), BF),
            *[place((2, cols), F32) for _ in range(3)],
        ),
        in_specs=[anyspace] * 11,
        out_specs=(anyspace,) * 6,
        scratch_shapes=[
            pltpu.VMEM((nodes, cols), BF),
            pltpu.VMEM((1, cap, n), jnp.int32),
            pltpu.VMEM((fan, nodes), jnp.int32),
            pltpu.VMEM((fan, nodes), F32),
            pltpu.VMEM((1, nodes), F32),
            pltpu.VMEM((1, nodes), jnp.int32),
            *[pltpu.VMEM((2, cols), F32) for _ in range(6)],
            pltpu.VMEM((1, halo), jnp.int32),
            dma((9,)),
            pltpu.VMEM((2, 2 * cols, cols), BF),
            pltpu.VMEM((nodes, cols), BF),
            pltpu.VMEM((nodes, lookup), BF),
            pltpu.VMEM((nodes if resident else 16, lookup), BF),
            pltpu.VMEM((lookup, nodes), BF),
            pltpu.VMEM((lookup if resident else 16, nodes), BF),
            pltpu.VMEM((128, nodes), F32),
            pltpu.VMEM((halo, nodes), BF),
            pltpu.VMEM((nodes, halo), BF),
            pltpu.VMEM((nodes, 128), F32),
            pltpu.VMEM((nodes, cols), BF),
            pltpu.VMEM((2, 2, nodes, cols), BF),
            pltpu.VMEM((2, nodes, cols), F32),
            pltpu.VMEM((2, nodes, cols), F32 if resident else BF),
            pltpu.VMEM((nodes, cols), F32),
            pltpu.VMEM((2, nodes, cols), BF),
            pltpu.VMEM((2 * halo, half), BF),
            pltpu.VMEM((2 * halo, half), BF),
            pltpu.VMEM((16, cols), F32),
            pltpu.VMEM((n, 3, 8, cols // 8), F32),
            pltpu.VMEM((n, 4, 8, cols // 8), F32),
            pltpu.VMEM((n, 3, 8, cols // 8), F32),
            pltpu.VMEM((n, 1, 8, cols // 8), F32),
            pltpu.VMEM((2, 2 * cols, nodes), BF),
            pltpu.VMEM((2, 3, cols, nodes), BF),
            pltpu.VMEM((2, 3, 2, nodes, cols // 4), BF),
            pltpu.VMEM((2, 4, half, cols // 4), BF),
            pltpu.VMEM((2, 4, line, half // line, cols // 4), BF),
            pltpu.VMEM((2, 4, half // line, cols // 4), BF),
            dma((2,)), dma, dma((5,)), dma((2, 6)), dma((2,)), dma((2, 2)),
            dma((2, 2, 3, 4)), dma((2, 2, 3)), dma((2, 2, 3, 2)),
            dma((2, 2, 4, line)), dma((2, 2, 4, n // 8)), dma((2, 2, 4, n // 8, 7)), dma((2, 4)),
        ],
        compiler_params=pltpu.CompilerParams(
            collective_id=0,
            has_side_effects=True,
            vmem_limit_bytes=(53 if resident else 62) * 2**20,
        ),
    )(
        features, jnp.swapaxes(send_rows, 1, 2), neighbour_ids.T, edge_weight.T,
        self_weight.reshape(1, nodes), valid_mask.reshape(1, nodes), biases, norm_gain, norm_shift,
        output_grad, weights,
    )
    if resident:
        out, ig, wg, bias, gain, shift = (
            pltpu.with_memory_space_constraint(v, pltpu.VMEM)
            for v in (out, ig, wg, bias, gain, shift)
        )
    rows, slots = 512, 4
    blocks = 2 * 2 * cols // rows
    wg, out, ig, bias, gain, shift = pl.pallas_call(
        functools.partial(hand_over, rows, slots),
        out_shape=(
            jax.ShapeDtypeStruct((2, 2 * cols, cols), F32), wide_block, wide_block,
            small, small, small,
        ),
        in_specs=[vm if resident else anyspace] + [anyspace] * 2 + [vm] * 3,
        out_specs=(anyspace, anyspace, anyspace, vm, vm, vm),
        scratch_shapes=[
            pltpu.VMEM((slots, rows, cols), F32),
            pltpu.VMEM((2, nodes, cols), BF),
            dma((blocks,)), dma((blocks,)), dma((2, 2)),
            *([] if resident else [pltpu.VMEM((blocks, rows, cols), BF)]),
        ],
        compiler_params=pltpu.CompilerParams(vmem_limit_bytes=(40 if resident else 62) * 2**20),
    )(wg, out, ig, bias, gain, shift)
    return out, ig, wg, bias, gain, shift


def solution(mesh):
    return jax.shard_map(
        per_device,
        mesh=mesh,
        in_specs=(
            P("cluster", "mp"),
            P("cluster", None),
            P("cluster", None),
            P("cluster"),
            P("cluster", None, None),
            P("cluster"),
            P(None, None, "mp"),
            P(None, "mp"),
            P(None, "mp"),
            P(None, "mp"),
            P("cluster", "mp"),
        ),
        out_specs=(
            P("cluster", "mp"),
            P("cluster", "mp"),
            P(None, None, "mp"),
            P(None, "mp"),
            P(None, "mp"),
            P(None, "mp"),
        ),
        check_vma=False,
    )
```
